32 devices in a mesh: segment: 4 (over x, core), ctx: 8 (over z, y).
Axes of the slice: x: 2, y: 2, z: 4, core: 2. Of those that a mesh axis runs over, the one named last changes fastest.
Arguments:
- query_stream: bfloat16 [4, 4096, 512], P('segment', 'ctx'), may hold values from -6 to 6
- key_stream: bfloat16 [4, 4096, 512], P('segment', 'ctx'), may hold values from -6 to 6
- value_stream: bfloat16 [4, 4096, 512], P('segment', 'ctx'), may hold values from -6 to 6
- filter_taps: bfloat16 [4, 4096, 512], P('segment', 'ctx'), may hold values from -1 to 1
- skip_weight: float32 [4, 512], P('segment'), may hold values from -3 to 3
Outputs:
- handed_on: bfloat16 [4, 4096, 512], P('segment', 'ctx')
The draws below stay inside these ranges and needn't reach their ends.
All inputs are finite; a program needn't handle non-finite values.
Results may differ from the reference program's by a relative error of at most 0.001.
Values may be sent and summed in bfloat16 or wider, within the bound.
No kernel may reach another device: no remote copies, remote signals or barrier semaphores. Data moves between devices by JAX's collectives and lax.ppermute only.
A program may use at most 128 MiB of HBM per device.

```python
import math
import jax
import jax.numpy as jnp
from jax import lax

C = 512
SEQ = 4096
SEGMENTS = 4


def draw_filter_taps(key, part):
    key = jax.random.fold_in(key, 7)
    rate_key, noise_key = jax.random.split(key)
    lograte = jax.random.uniform(rate_key, (SEGMENTS, 1, C), minval=0.0, maxval=1.0)
    low = -jnp.log(jnp.float32(SEQ))
    high = jnp.float32(-math.log(32.0))
    lograte = low + (high - low) * lograte
    noise = jnp.clip(jax.random.normal(noise_key, (SEGMENTS, SEQ, C)), -4.0, 4.0)
    rate = jnp.exp(lograte)
    position = jnp.arange(SEQ).astype(jnp.float32)[None, :, None]
    taps = noise * jnp.sqrt(2.0 * rate) * jnp.exp(-rate * position)
    return taps.astype(jnp.bfloat16)


def block_levels(own_key, dims, cuts, smallest, largest):
    def one(dim, shards_of):
        steps = jax.random.uniform(jax.random.fold_in(jax.random.fold_in(own_key, 6), dim), (shards_of,), jnp.float32, smallest / len(cuts), largest / len(cuts))
        return jnp.repeat(jnp.exp(steps), dims[dim] // shards_of).reshape((-1,) + (1,) * (len(dims) - dim - 1))

    level = one(*cuts[0])
    for cut in cuts[1:]:
        level = level * one(*cut)
    return level


def gaussian(rng, dims, width, bound, shards=(), dtype=jnp.bfloat16):
    gain = block_levels(rng, dims, shards, -0.22, 0.18) if shards else 1.0
    array = jax.random.normal(rng, dims, jnp.float32) * width * gain
    return jnp.minimum(jnp.maximum(array, -bound), bound).astype(dtype)


def setup_inputs(seed: int = 0) -> dict:
    streams_of = jax.random.split(jax.random.key(seed), 6)
    return {
        "query_stream": gaussian(streams_of[0], (SEGMENTS, SEQ, C), 1.0, 6.0, ((0, 4), (1, 8))),
        "key_stream": gaussian(streams_of[1], (SEGMENTS, SEQ, C), 1.0, 6.0, ((0, 4), (1, 8))),
        "value_stream": gaussian(streams_of[2], (SEGMENTS, SEQ, C), 1.0, 6.0, ((0, 4), (1, 8))),
        "filter_taps": draw_filter_taps(jax.random.fold_in(streams_of[5], 71), 0),
        "skip_weight": gaussian(streams_of[4], (SEGMENTS, C), 1.0, 3.0, ((0, 4),), jnp.float32),
    }


def causal_convolution(product, taps):
    length = product.shape[0]
    spectrum = jnp.fft.rfft(product, n=2 * length, axis=0) * jnp.fft.rfft(taps, n=2 * length, axis=0)
    return jnp.fft.irfft(spectrum, n=2 * length, axis=0)[:length]


def one_section(pieces):
    query, keys, values, taps, weight = pieces
    product = keys.astype(jnp.float32) * values.astype(jnp.float32)
    convolved = causal_convolution(product, taps.astype(jnp.float32)).astype(jnp.float32)
    gated = query.astype(jnp.float32) * (convolved + weight[None, :] * product)
    return gated.astype(jnp.bfloat16)


def reference(query_stream, key_stream, value_stream, filter_taps, skip_weight):
    gated = lax.map(one_section, (query_stream, key_stream, value_stream, filter_taps, skip_weight))
    return jnp.roll(gated, 1, axis=0)
```

```python
import functools
import math

import jax
import jax.numpy as jnp
import numpy as np
from jax import lax
from jax.experimental import pallas as pl
from jax.experimental.pallas import tpu as pltpu
from jax.sharding import PartitionSpec as P

HIGHEST = lax.Precision.HIGHEST
LANES = 128
HALF = 64
INNER = 64
STEP = 8
F32 = jnp.float32
BF16 = jnp.bfloat16


def from_behind(value, axis, steps):
    count = lax.axis_size(axis)
    pairs = [(source, (source + steps) % count) for source in range(count)]
    return lax.ppermute(value, axis, pairs)


def angles(modulus, left, right):
    phase = left[:, None] * right[None, :] % modulus
    theta = phase.astype(jnp.float32) * (2.0 * math.pi / modulus)
    return (jnp.cos(theta), jnp.sin(theta))


def frequency_order(width):
    rows = jnp.arange(2 * width, dtype=jnp.int32)
    halves = rows // 2
    return jnp.where(rows % 2 == 0, halves, jnp.where(halves == 0, width, 2 * width - halves))


def across(table, data):
    return jnp.einsum("rd,dsc->rsc", table, data, precision=HIGHEST)


def along(table, data):
    return jnp.einsum("kb,rbc->rkc", table, data, precision=HIGHEST)


def rotate(real_part, imag_part, cosine, sine):
    return (real_part * cosine + imag_part * sine, imag_part * cosine - real_part * sine)


def general_on_device(query_stream, key_stream, value_stream, filter_taps, skip_weight):
    parts = lax.axis_size("ctx")
    device = lax.axis_index("ctx")
    length = query_stream.shape[1]
    channels = query_stream.shape[2]
    share = length // parts
    total = 2 * parts * length
    product = key_stream[0].astype(jnp.float32) * value_stream[0].astype(jnp.float32)
    taps = filter_taps[0].astype(jnp.float32)
    block_prod, block_taps = (
        lax.all_to_all(
            product.reshape(1, length, channels), "ctx", split_axis=1, concat_axis=0, tiled=True
        ),
        lax.all_to_all(
            taps.reshape(1, length, channels), "ctx", split_axis=1, concat_axis=0, tiled=True
        ),
    )
    order = frequency_order(parts)
    cos_cross, sin_cross = angles(2 * parts, order, jnp.arange(parts, dtype=jnp.int32))
    positions = device * share + jnp.arange(share, dtype=jnp.int32)
    cos_twist, sin_twist = angles(total, order, positions)
    cos_twist = cos_twist[:, :, None]
    sin_twist = sin_twist[:, :, None]
    span = jnp.arange(length, dtype=jnp.int32)
    cos_along, sin_along = angles(length, span, span)
    local_rows = lax.dynamic_slice(order, (2 * device,), (2,))
    cos_back, sin_back = angles(total, local_rows, span)
    cos_back = cos_back[:, :, None]
    sin_back = sin_back[:, :, None]

    def forward_along(real_part, imag_part):
        return (
            along(cos_along, real_part) + along(sin_along, imag_part),
            along(cos_along, imag_part) - along(sin_along, real_part),
        )

    prod_real, prod_imag = rotate(
        across(cos_cross, block_prod), -across(sin_cross, block_prod), cos_twist, sin_twist
    )
    taps_real, taps_imag = rotate(
        across(cos_cross, block_taps), -across(sin_cross, block_taps), cos_twist, sin_twist
    )
    first_real, first_imag = forward_along(
        lax.all_to_all(prod_real, "ctx", split_axis=0, concat_axis=1, tiled=True),
        lax.all_to_all(prod_imag, "ctx", split_axis=0, concat_axis=1, tiled=True),
    )
    second_real, second_imag = forward_along(
        lax.all_to_all(taps_real, "ctx", split_axis=0, concat_axis=1, tiled=True),
        lax.all_to_all(taps_imag, "ctx", split_axis=0, concat_axis=1, tiled=True),
    )
    result_real = first_real * second_real - first_imag * second_imag
    result_imag = first_real * second_imag + first_imag * second_real
    back_real = along(cos_along, result_real) - along(sin_along, result_imag)
    back_imag = along(cos_along, result_imag) + along(sin_along, result_real)
    spec_real, spec_imag = rotate(back_real, back_imag, cos_back, -sin_back)
    rows_real, rows_imag = (
        lax.all_to_all(spec_real, "ctx", split_axis=1, concat_axis=0, tiled=True),
        lax.all_to_all(spec_imag, "ctx", split_axis=1, concat_axis=0, tiled=True),
    )
    cos_final, sin_final = angles(2 * parts, jnp.arange(parts, dtype=jnp.int32), order)
    by_block = jnp.einsum("dr,rsc->dsc", cos_final, rows_real, precision=HIGHEST) - jnp.einsum(
        "dr,rsc->dsc", sin_final, rows_imag, precision=HIGHEST
    )
    by_block = by_block * (1.0 / total)
    convolved = lax.all_to_all(by_block, "ctx", split_axis=0, concat_axis=1, tiled=True)[0]
    gated = query_stream[0].astype(jnp.float32) * (convolved + skip_weight[0][None, :] * product)
    gated = gated.astype(jnp.bfloat16)[None]
    return from_behind(gated, "segment", 1)


def split_two(value):
    high = value.astype(BF16)
    return high, (value - high.astype(F32)).astype(BF16)


def split_table(table):
    table = table.astype(np.float32)
    high = table.astype(jnp.bfloat16)
    low = (table - high.astype(np.float32)).astype(jnp.bfloat16)
    return np.concatenate([high, high, low], axis=1)


def stacked(value):
    high, low = split_two(value)
    return jnp.concatenate([high, low, high], axis=0)


def lower_half(shape):
    return lax.broadcasted_iota(jnp.int32, shape, len(shape) - 1) < HALF


def swap_halves(value):
    return pltpu.roll(value, HALF, value.ndim - 1)


def tables(outer):
    total = outer * INNER
    a = np.arange(outer)
    b = np.arange(INNER)
    c = np.arange(outer) + 0.25
    first = 2.0 * np.pi * np.outer(c, a) / outer
    second = 2.0 * np.pi * np.outer(b, b) / INNER
    forward_a = split_table(np.concatenate([np.cos(first), -np.sin(first)], axis=0))
    forward_b = split_table(
        np.block([[np.cos(second), np.sin(second)], [-np.sin(second), np.cos(second)]])
    )
    back_b = split_table(np.concatenate([np.cos(second), np.sin(second)], axis=0))
    back_a = split_table(np.concatenate([np.cos(first).T, -np.sin(first).T], axis=0) / total)

    def turns(steps):
        theta = 2.0 * np.pi * np.outer(steps, c) / total
        wide = np.stack([np.cos(theta), np.sin(theta)], axis=1).astype(np.float32)
        return np.ascontiguousarray(np.broadcast_to(wide[..., None], wide.shape + (LANES,)))

    coarse = turns(np.arange(0, INNER, STEP))
    fine = turns(np.arange(STEP))
    return forward_a, forward_b, back_b, back_a, coarse, fine


def pack_kernel(parts, k_ref, v_ref, h_ref, q_ref, kvh_ref, q_out_ref):
    length = k_ref.shape[0]
    rows = length // 2
    low = lower_half((rows, LANES))

    def pack(source, place):
        for e in range(parts // 2):
            tile = source[:, LANES * e : LANES * (e + 1)].astype(F32)
            early, late = tile[:rows], tile[rows:]
            place(2 * e, jnp.where(low, early, swap_halves(late)).astype(BF16))
            place(2 * e + 1, jnp.where(low, swap_halves(early), late).astype(BF16))

    for n, source in enumerate((k_ref, v_ref, h_ref)):

        def place(d, value, n=n):
            kvh_ref[d, n * rows : (n + 1) * rows, :] = value

        pack(source, place)

    def place_q(d, value):
        q_out_ref[d] = value

    pack(q_ref, place_q)


def unpack_kernel(parts, g_ref, out_ref):
    rows = g_ref.shape[1]
    low = lower_half((rows, LANES))
    for e in range(parts // 2):
        even, odd = g_ref[2 * e].astype(F32), g_ref[2 * e + 1].astype(F32)
        out_ref[:rows, LANES * e : LANES * (e + 1)] = jnp.where(low, even, swap_halves(odd)).astype(BF16)
        out_ref[rows:, LANES * e : LANES * (e + 1)] = jnp.where(low, swap_halves(even), odd).astype(BF16)


def convolve_kernel(
    parts, outer, kvh_ref, fa_ref, fb_ref, bb_ref, ba_ref, coarse_ref, fine_ref, y_ref, x_s, z_s, w_s
):
    rows = kvh_ref.shape[1] // 3
    per = rows // INNER
    low = lower_half((INNER, LANES))
    lowc = lower_half((outer, LANES))

    def load(part, carry):
        for m in range(per):
            at = m * INNER
            k = kvh_ref[part, at : at + INNER, :].astype(F32)
            v = kvh_ref[part, rows + at : rows + at + INNER, :].astype(F32)
            h = kvh_ref[part, 2 * rows + at : 2 * rows + at + INNER, :].astype(F32)
            p = k * v
            a = part * (2 * per) + m
            x_s[pl.ds(a, INNER, stride=outer), :] = jnp.where(low, p, swap_halves(h))
            x_s[pl.ds(a + per, INNER, stride=outer), :] = jnp.where(low, swap_halves(p), h)
        return carry

    lax.fori_loop(0, parts, load, 0)

    def turn(group, n):
        cos_1, sin_1 = coarse_ref[group, 0], coarse_ref[group, 1]
        if n == 0:
            return cos_1, sin_1
        cos_2, sin_2 = fine_ref[n, 0], fine_ref[n, 1]
        return cos_1 * cos_2 - sin_1 * sin_2, sin_1 * cos_2 + cos_1 * sin_2

    def forward_outer(group, carry):
        for n in range(0, STEP, 2):
            b = group * STEP + n
            data = jnp.concatenate(
                [
                    stacked(x_s[pl.ds(pl.multiple_of((b + j) * outer, outer), outer), :])
                    for j in range(2)
                ],
                axis=1,
            )
            both = jnp.dot(fa_ref[...], data, preferred_element_type=F32)
            for j in range(2):
                re = both[:outer, LANES * j : LANES * (j + 1)]
                im = both[outer:, LANES * j : LANES * (j + 1)]
                cos, sin = turn(group, n + j)
                z_s[pl.ds(b + j, outer, stride=2 * INNER), :] = re * cos + im * sin
                z_s[pl.ds(b + j + INNER, outer, stride=2 * INNER), :] = im * cos - re * sin
        return carry

    lax.fori_loop(0, INNER // STEP, forward_outer, 0)

    def middle(group, carry):
        for n in range(0, STEP, 2):
            c = group * STEP + n
            data = jnp.concatenate(
                [
                    stacked(z_s[pl.ds(pl.multiple_of((c + j) * 2 * INNER, 2 * INNER), 2 * INNER), :])
                    for j in range(2)
                ],
                axis=1,
            )
            both = jnp.dot(fb_ref[...], data, preferred_element_type=F32)
            mixed = []
            for j in range(2):
                re = both[:INNER, LANES * j : LANES * (j + 1)]
                im = both[INNER:, LANES * j : LANES * (j + 1)]
                re_2, im_2 = swap_halves(re), swap_halves(im)
                mixed.append(
                    stacked(jnp.where(low, re * re_2 - im * im_2, re * im_2 + im * re_2))
                )
            both = jnp.dot(bb_ref[...], jnp.concatenate(mixed, axis=1), preferred_element_type=F32)
            for j in range(2):
                straight = both[:INNER, LANES * j : LANES * (j + 1)]
                crossed = swap_halves(both[INNER:, LANES * j : LANES * (j + 1)])
                w_s[pl.ds(c + j, INNER, stride=outer), :] = jnp.where(
                    low, straight - crossed, straight + crossed
                )
        return carry

    lax.fori_loop(0, outer // STEP, middle, 0)

    def back_outer(group, carry):
        for n in range(0, STEP, 2):
            b = group * STEP + n
            data = []
            for j in range(2):
                value = w_s[pl.ds(pl.multiple_of((b + j) * outer, outer), outer), :]
                cos, sin = turn(group, n + j)
                other = swap_halves(value) * sin
                straight = value * cos
                data.append(stacked(jnp.where(lowc, straight - other, straight + other)))
            both = jnp.dot(ba_ref[...], jnp.concatenate(data, axis=1), preferred_element_type=F32)
            for j in range(2):
                re = both[:outer, LANES * j : LANES * (j + 1)]
                im = both[outer:, LANES * j : LANES * (j + 1)]
                y_ref[pl.ds(b + j, outer, stride=INNER), :] = re + swap_halves(im)
        return carry

    lax.fori_loop(0, INNER // STEP, back_outer, 0)


def gate_kernel(parts, y_ref, kvh_ref, q_ref, skip_ref, g_ref):
    rows = q_ref.shape[1]
    low = lower_half((rows, LANES))

    def one(part, carry):
        at = pl.multiple_of(part * 2 * rows, 2 * rows)
        early = y_ref[pl.ds(at, rows), :]
        late = y_ref[pl.ds(at + rows, rows), :]
        y = jnp.where(low, early, swap_halves(late))
        p = kvh_ref[part, :rows, :].astype(F32) * kvh_ref[part, rows : 2 * rows, :].astype(F32)
        g_ref[part] = (q_ref[part].astype(F32) * (y + skip_ref[...] * p)).astype(BF16)
        return carry

    lax.fori_loop(0, parts, one, 0)


def fast_on_device(query_stream, key_stream, value_stream, filter_taps, skip_weight):
    parts = lax.axis_size("ctx")
    device = lax.axis_index("ctx")
    length, channels = query_stream.shape[1:]
    rows = length // 2
    outer = parts * length // INNER
    kvh, q = pl.pallas_call(
        functools.partial(pack_kernel, parts),
        out_shape=(
            jax.ShapeDtypeStruct((parts, 3 * rows, LANES), BF16),
            jax.ShapeDtypeStruct((parts, rows, LANES), BF16),
        ),
    )(key_stream[0], value_stream[0], filter_taps[0], query_stream[0])

    def spread(value):
        return lax.all_to_all(value, "ctx", split_axis=0, concat_axis=0, tiled=True)

    kvh = spread(kvh)
    q = spread(q)
    consts = [jnp.asarray(t) for t in tables(outer)]
    y = pl.pallas_call(
        functools.partial(convolve_kernel, parts, outer),
        out_shape=jax.ShapeDtypeStruct((parts * length, LANES), F32),
        scratch_shapes=[
            pltpu.VMEM((outer * INNER, LANES), F32),
            pltpu.VMEM((2 * outer * INNER, LANES), F32),
            pltpu.VMEM((outer * INNER, LANES), F32),
        ],
        compiler_params=pltpu.CompilerParams(vmem_limit_bytes=40 * 2**20),
    )(kvh, *consts)
    skip = lax.dynamic_slice(skip_weight, (0, device * HALF), (1, HALF))
    g = pl.pallas_call(
        functools.partial(gate_kernel, parts),
        out_shape=jax.ShapeDtypeStruct((parts, rows, LANES), BF16),
        compiler_params=pltpu.CompilerParams(vmem_limit_bytes=40 * 2**20),
    )(y, kvh, q, jnp.concatenate([skip, skip], axis=1))
    g = spread(g)
    g = from_behind(g, "segment", 1)
    out = pl.pallas_call(
        functools.partial(unpack_kernel, parts),
        out_shape=jax.ShapeDtypeStruct((length, channels), BF16),
    )(g)
    return out[None]


def solution(mesh):
    placed = (
        P("segment", "ctx", None),
        P("segment", "ctx", None),
        P("segment", "ctx", None),
        P("segment", "ctx", None),
        P("segment", None),
    )

    def on_device(*arrays):
        parts = lax.axis_size("ctx")
        length, channels = arrays[0].shape[1:]
        small = parts * length <= 4096 and length % (2 * INNER) == 0 and parts % 2 == 0
        run = fast_on_device if small and channels == parts * HALF else general_on_device
        return run(*arrays)

    return jax.shard_map(
        on_device, mesh=mesh, in_specs=placed, out_specs=P("segment", "ctx", None), check_vma=False
    )
```

```python
import functools
import math

import jax
import jax.numpy as jnp
import numpy as np
from jax import lax
from jax.experimental import pallas as pl
from jax.experimental.pallas import tpu as pltpu
from jax.sharding import PartitionSpec as P

HIGHEST = lax.Precision.HIGHEST
LANES = 128
HALF = 64
INNER = 64
STEP = 16
WIDE = 16
F32 = jnp.float32
BF16 = jnp.bfloat16


def from_behind(value, axis, steps):
    count = lax.axis_size(axis)
    pairs = [(source, (source + steps) % count) for source in range(count)]
    return lax.ppermute(value, axis, pairs)


def angles(modulus, left, right):
    phase = left[:, None] * right[None, :] % modulus
    theta = phase.astype(jnp.float32) * (2.0 * math.pi / modulus)
    return (jnp.cos(theta), jnp.sin(theta))


def frequency_order(width):
    rows = jnp.arange(2 * width, dtype=jnp.int32)
    halves = rows // 2
    return jnp.where(rows % 2 == 0, halves, jnp.where(halves == 0, width, 2 * width - halves))


def across(table, data):
    return jnp.einsum("rd,dsc->rsc", table, data, precision=HIGHEST)


def along(table, data):
    return jnp.einsum("kb,rbc->rkc", table, data, precision=HIGHEST)


def rotate(real_part, imag_part, cosine, sine):
    return (real_part * cosine + imag_part * sine, imag_part * cosine - real_part * sine)


def general_on_device(query_stream, key_stream, value_stream, filter_taps, skip_weight):
    parts = lax.axis_size("ctx")
    device = lax.axis_index("ctx")
    length = query_stream.shape[1]
    channels = query_stream.shape[2]
    share = length // parts
    total = 2 * parts * length
    product = key_stream[0].astype(jnp.float32) * value_stream[0].astype(jnp.float32)
    taps = filter_taps[0].astype(jnp.float32)
    block_prod, block_taps = (
        lax.all_to_all(
            product.reshape(1, length, channels), "ctx", split_axis=1, concat_axis=0, tiled=True
        ),
        lax.all_to_all(
            taps.reshape(1, length, channels), "ctx", split_axis=1, concat_axis=0, tiled=True
        ),
    )
    order = frequency_order(parts)
    cos_cross, sin_cross = angles(2 * parts, order, jnp.arange(parts, dtype=jnp.int32))
    positions = device * share + jnp.arange(share, dtype=jnp.int32)
    cos_twist, sin_twist = angles(total, order, positions)
    cos_twist = cos_twist[:, :, None]
    sin_twist = sin_twist[:, :, None]
    span = jnp.arange(length, dtype=jnp.int32)
    cos_along, sin_along = angles(length, span, span)
    local_rows = lax.dynamic_slice(order, (2 * device,), (2,))
    cos_back, sin_back = angles(total, local_rows, span)
    cos_back = cos_back[:, :, None]
    sin_back = sin_back[:, :, None]

    def forward_along(real_part, imag_part):
        return (
            along(cos_along, real_part) + along(sin_along, imag_part),
            along(cos_along, imag_part) - along(sin_along, real_part),
        )

    prod_real, prod_imag = rotate(
        across(cos_cross, block_prod), -across(sin_cross, block_prod), cos_twist, sin_twist
    )
    taps_real, taps_imag = rotate(
        across(cos_cross, block_taps), -across(sin_cross, block_taps), cos_twist, sin_twist
    )
    first_real, first_imag = forward_along(
        lax.all_to_all(prod_real, "ctx", split_axis=0, concat_axis=1, tiled=True),
        lax.all_to_all(prod_imag, "ctx", split_axis=0, concat_axis=1, tiled=True),
    )
    second_real, second_imag = forward_along(
        lax.all_to_all(taps_real, "ctx", split_axis=0, concat_axis=1, tiled=True),
        lax.all_to_all(taps_imag, "ctx", split_axis=0, concat_axis=1, tiled=True),
    )
    result_real = first_real * second_real - first_imag * second_imag
    result_imag = first_real * second_imag + first_imag * second_real
    back_real = along(cos_along, result_real) - along(sin_along, result_imag)
    back_imag = along(cos_along, result_imag) + along(sin_along, result_real)
    spec_real, spec_imag = rotate(back_real, back_imag, cos_back, -sin_back)
    rows_real, rows_imag = (
        lax.all_to_all(spec_real, "ctx", split_axis=1, concat_axis=0, tiled=True),
        lax.all_to_all(spec_imag, "ctx", split_axis=1, concat_axis=0, tiled=True),
    )
    cos_final, sin_final = angles(2 * parts, jnp.arange(parts, dtype=jnp.int32), order)
    by_block = jnp.einsum("dr,rsc->dsc", cos_final, rows_real, precision=HIGHEST) - jnp.einsum(
        "dr,rsc->dsc", sin_final, rows_imag, precision=HIGHEST
    )
    by_block = by_block * (1.0 / total)
    convolved = lax.all_to_all(by_block, "ctx", split_axis=0, concat_axis=1, tiled=True)[0]
    gated = query_stream[0].astype(jnp.float32) * (convolved + skip_weight[0][None, :] * product)
    gated = gated.astype(jnp.bfloat16)[None]
    return from_behind(gated, "segment", 1)


def split_two(value):
    high = value.astype(BF16)
    return high, (value - high.astype(F32)).astype(BF16)


def split_table(table):
    table = table.astype(np.float32)
    high = table.astype(jnp.bfloat16)
    low = (table - high.astype(np.float32)).astype(jnp.bfloat16)
    return np.concatenate([high, high, low], axis=1)


def stacked(value):
    high, low = split_two(value)
    return jnp.concatenate([high, low, high], axis=0)


def lower_half(shape):
    return lax.broadcasted_iota(jnp.int32, shape, len(shape) - 1) < HALF


def swap_halves(value):
    return pltpu.roll(value, HALF, value.ndim - 1)


def tables(outer):
    total = outer * INNER
    a = np.arange(outer)
    b = np.arange(INNER)
    c = np.arange(outer) + 0.25
    first = 2.0 * np.pi * np.outer(c, a) / outer
    second = 2.0 * np.pi * np.outer(b, b) / INNER
    forward_a = split_table(np.concatenate([np.cos(first), -np.sin(first)], axis=0))
    forward_b = split_table(
        np.block([[np.cos(second), np.sin(second)], [-np.sin(second), np.cos(second)]])
    )
    back_b = split_table(np.concatenate([np.cos(second), np.sin(second)], axis=0))
    back_a = split_table(np.concatenate([np.cos(first).T, -np.sin(first).T], axis=0) / total)

    def turns(steps):
        theta = 2.0 * np.pi * np.outer(steps, c) / total
        wide = np.stack([np.cos(theta), np.sin(theta)], axis=1).astype(np.float32)
        return np.ascontiguousarray(np.broadcast_to(wide[..., None], wide.shape + (LANES,)))

    coarse = turns(np.arange(0, INNER, STEP))
    fine = turns(np.arange(STEP))
    return forward_a, forward_b, back_b, back_a, coarse, fine


def pack(parts, source, low, place):
    rows = source.shape[0] // 2
    for e in range(parts // 2):
        tile = source[:, LANES * e : LANES * (e + 1)].astype(F32)
        early, late = tile[:rows], tile[rows:]
        place(2 * e, jnp.where(low, early, swap_halves(late)).astype(BF16))
        place(2 * e + 1, jnp.where(low, swap_halves(early), late).astype(BF16))


def pack_kernel(parts, index_ref, k_ref, v_ref, h_ref, *refs):
    outs, held = refs[:-1], refs[-1]
    rows = k_ref.shape[0] // 2
    low = lower_half((rows, LANES))
    for n, source in enumerate((k_ref, v_ref, h_ref)):

        def place(d, value, n=n):
            held[d, n * rows : (n + 1) * rows, :] = value

        pack(parts, source, low, place)
    for n, out in enumerate(outs):
        out[...] = held[lax.rem(index_ref[0] + n, parts)]


def pack_gate_kernel(parts, q_ref, out_ref):
    low = lower_half((q_ref.shape[0] // 2, LANES))

    def place(d, value):
        out_ref[d] = value

    pack(parts, q_ref, low, place)


def unpack_kernel(parts, index_ref, *refs):
    blocks, out_ref, held = refs[:parts], refs[parts], refs[parts + 1]
    rows = held.shape[1]
    low = lower_half((rows, LANES))
    for n, block in enumerate(blocks):
        held[lax.rem(index_ref[0] + n, parts)] = block[...]
    for e in range(parts // 2):
        even, odd = held[2 * e].astype(F32), held[2 * e + 1].astype(F32)
        out_ref[:rows, LANES * e : LANES * (e + 1)] = jnp.where(low, even, swap_halves(odd)).astype(BF16)
        out_ref[rows:, LANES * e : LANES * (e + 1)] = jnp.where(low, swap_halves(even), odd).astype(BF16)


def convolve_kernel(parts, outer, index_ref, *refs):
    blocks = refs[:parts]
    skip_ref, fa_ref, fb_ref, bb_ref, ba_ref, coarse_ref, fine_ref, out_ref, x_s, z_s, w_s, y_s = refs[parts:]
    rows = out_ref.shape[1]
    per = rows // INNER
    low = lower_half((INNER, LANES))
    lowc = lower_half((outer, LANES))

    def origin(n):
        return lax.rem(index_ref[0] + parts - n, parts)

    for n, block in enumerate(blocks):
        for m in range(per):
            at = m * INNER
            k = block[at : at + INNER, :].astype(F32)
            v = block[rows + at : rows + at + INNER, :].astype(F32)
            h = block[2 * rows + at : 2 * rows + at + INNER, :].astype(F32)
            p = k * v
            a = origin(n) * (2 * per) + m
            x_s[pl.ds(a, INNER, stride=outer), :] = jnp.where(low, p, swap_halves(h))
            x_s[pl.ds(a + per, INNER, stride=outer), :] = jnp.where(low, swap_halves(p), h)

    def turn(group, n):
        cos_1, sin_1 = coarse_ref[group, 0], coarse_ref[group, 1]
        if n == 0:
            return cos_1, sin_1
        cos_2, sin_2 = fine_ref[n, 0], fine_ref[n, 1]
        return cos_1 * cos_2 - sin_1 * sin_2, sin_1 * cos_2 + cos_1 * sin_2

    def forward_outer(group, carry):
        for n in range(0, STEP, WIDE):
            b = group * STEP + n
            data = jnp.concatenate(
                [
                    stacked(x_s[pl.ds(pl.multiple_of((b + j) * outer, outer), outer), :])
                    for j in range(WIDE)
                ],
                axis=1,
            )
            both = jnp.dot(fa_ref[...], data, preferred_element_type=F32)
            for j in range(WIDE):
                re = both[:outer, LANES * j : LANES * (j + 1)]
                im = both[outer:, LANES * j : LANES * (j + 1)]
                cos, sin = turn(group, n + j)
                z_s[pl.ds(b + j, outer, stride=2 * INNER), :] = re * cos + im * sin
                z_s[pl.ds(b + j + INNER, outer, stride=2 * INNER), :] = im * cos - re * sin
        return carry

    lax.fori_loop(0, INNER // STEP, forward_outer, 0)

    def middle(group, carry):
        for n in range(0, STEP, WIDE):
            c = group * STEP + n
            data = jnp.concatenate(
                [
                    stacked(z_s[pl.ds(pl.multiple_of((c + j) * 2 * INNER, 2 * INNER), 2 * INNER), :])
                    for j in range(WIDE)
                ],
                axis=1,
            )
            both = jnp.dot(fb_ref[...], data, preferred_element_type=F32)
            mixed = []
            for j in range(WIDE):
                re = both[:INNER, LANES * j : LANES * (j + 1)]
                im = both[INNER:, LANES * j : LANES * (j + 1)]
                re_2, im_2 = swap_halves(re), swap_halves(im)
                mixed.append(
                    stacked(jnp.where(low, re * re_2 - im * im_2, re * im_2 + im * re_2))
                )
            both = jnp.dot(bb_ref[...], jnp.concatenate(mixed, axis=1), preferred_element_type=F32)
            for j in range(WIDE):
                straight = both[:INNER, LANES * j : LANES * (j + 1)]
                crossed = swap_halves(both[INNER:, LANES * j : LANES * (j + 1)])
                w_s[pl.ds(c + j, INNER, stride=outer), :] = jnp.where(
                    low, straight - crossed, straight + crossed
                )
        return carry

    lax.fori_loop(0, outer // STEP, middle, 0)

    def back_outer(group, carry):
        for n in range(0, STEP, WIDE):
            b = group * STEP + n
            data = []
            for j in range(WIDE):
                value = w_s[pl.ds(pl.multiple_of((b + j) * outer, outer), outer), :]
                cos, sin = turn(group, n + j)
                other = swap_halves(value) * sin
                straight = value * cos
                data.append(stacked(jnp.where(lowc, straight - other, straight + other)))
            both = jnp.dot(ba_ref[...], jnp.concatenate(data, axis=1), preferred_element_type=F32)
            for j in range(WIDE):
                re = both[:outer, LANES * j : LANES * (j + 1)]
                im = both[outer:, LANES * j : LANES * (j + 1)]
                y_s[pl.ds(b + j, outer, stride=INNER), :] = re + swap_halves(im)
        return carry

    lax.fori_loop(0, INNER // STEP, back_outer, 0)

    lowr = lower_half((rows, LANES))
    for n, block in enumerate(blocks):
        at = pl.multiple_of(origin(n) * 2 * rows, 2 * rows)
        early = y_s[pl.ds(at, rows), :]
        late = y_s[pl.ds(at + rows, rows), :]
        p = block[:rows, :].astype(F32) * block[rows : 2 * rows, :].astype(F32)
        out_ref[n] = jnp.where(lowr, early, swap_halves(late)) + skip_ref[...] * p


def gate_kernel(parts, index_ref, y_ref, q_ref, *outs):
    for n, out in enumerate(outs):
        q = q_ref[lax.rem(index_ref[0] + parts - n, parts)]
        out[...] = (q.astype(F32) * y_ref[n]).astype(BF16)


def joint_shift(value, segment_step, ctx_step):
    segments, parts = lax.axis_size("segment"), lax.axis_size("ctx")
    pairs = [
        (s * parts + c, (s + segment_step) % segments * parts + (c + ctx_step) % parts)
        for s in range(segments)
        for c in range(parts)
    ]
    return lax.ppermute(value, ("segment", "ctx"), pairs)


def fast_on_device(query_stream, key_stream, value_stream, filter_taps, skip_weight):
    parts = lax.axis_size("ctx")
    device = lax.axis_index("ctx")
    length, channels = query_stream.shape[1:]
    rows = length // 2
    outer = parts * length // INNER
    index = jnp.full((1,), device, jnp.int32)
    scalar = pl.BlockSpec(memory_space=pltpu.SMEM)
    whole = pl.BlockSpec(memory_space=pltpu.VMEM)
    small = pltpu.CompilerParams(vmem_limit_bytes=24 * 2**20)

    def block(*shape, dtype=BF16):
        return jax.ShapeDtypeStruct(shape, dtype)

    sent = pl.pallas_call(
        functools.partial(pack_kernel, parts),
        out_shape=(block(3 * rows, LANES),) * parts,
        in_specs=[scalar, whole, whole, whole],
        scratch_shapes=[pltpu.VMEM((parts, 3 * rows, LANES), BF16)],
        compiler_params=small,
    )(index, key_stream[0], value_stream[0], filter_taps[0])
    slabs = [sent[0]] + [joint_shift(sent[n], 0, n) for n in range(1, parts)]
    q = pl.pallas_call(
        functools.partial(pack_gate_kernel, parts),
        out_shape=block(parts, rows, LANES),
        compiler_params=small,
    )(query_stream[0])
    q, *_ = lax.optimization_barrier((q, *slabs))
    q = lax.all_to_all(q, "ctx", split_axis=0, concat_axis=0, tiled=True)
    skip = lax.dynamic_slice(skip_weight, (0, device * HALF), (1, HALF))
    consts = [jnp.asarray(t) for t in tables(outer)]
    y = pl.pallas_call(
        functools.partial(convolve_kernel, parts, outer),
        out_shape=block(parts, rows, LANES, dtype=F32),
        in_specs=[scalar] + [whole] * (parts + 1 + len(consts)),
        scratch_shapes=[
            pltpu.VMEM((outer * INNER, LANES), F32),
            pltpu.VMEM((2 * outer * INNER, LANES), F32),
            pltpu.VMEM((outer * INNER, LANES), F32),
            pltpu.VMEM((outer * INNER, LANES), F32),
        ],
        compiler_params=pltpu.CompilerParams(vmem_limit_bytes=40 * 2**20),
    )(index, *slabs, jnp.concatenate([skip, skip], axis=1), *consts)
    gated = pl.pallas_call(
        functools.partial(gate_kernel, parts),
        out_shape=(block(rows, LANES),) * parts,
        in_specs=[scalar, whole, whole],
        compiler_params=small,
    )(index, y, q)
    gated = [joint_shift(gated[n], 1, -n) for n in range(parts)]
    out = pl.pallas_call(
        functools.partial(unpack_kernel, parts),
        out_shape=block(length, channels),
        in_specs=[scalar] + [whole] * parts,
        scratch_shapes=[pltpu.VMEM((parts, rows, LANES), BF16)],
        compiler_params=small,
    )(index, *gated)
    return out[None]


def solution(mesh):
    placed = (
        P("segment", "ctx", None),
        P("segment", "ctx", None),
        P("segment", "ctx", None),
        P("segment", "ctx", None),
        P("segment", None),
    )

    def on_device(*arrays):
        parts = lax.axis_size("ctx")
        length, channels = arrays[0].shape[1:]
        small = parts * length <= 4096 and length % (2 * INNER) == 0 and parts % 2 == 0
        run = fast_on_device if small and channels == parts * HALF else general_on_device
        return run(*arrays)

    return jax.shard_map(
        on_device, mesh=mesh, in_specs=placed, out_specs=P("segment", "ctx", None), check_vma=False
    )
```

```python
import functools
import math

import jax
import jax.numpy as jnp
import numpy as np
from jax import lax
from jax.experimental import pallas as pl
from jax.experimental.pallas import tpu as pltpu
from jax.sharding import PartitionSpec as P

HIGHEST = lax.Precision.HIGHEST
LANES = 128
HALF = 64
INNER = 64
SPAN = INNER // 2
QUARTER = LANES // 4
WIDE = 16
F32 = jnp.float32
BF16 = jnp.bfloat16


def from_behind(value, axis, steps):
    count = lax.axis_size(axis)
    pairs = [(source, (source + steps) % count) for source in range(count)]
    return lax.ppermute(value, axis, pairs)


def angles(modulus, left, right):
    phase = left[:, None] * right[None, :] % modulus
    theta = phase.astype(jnp.float32) * (2.0 * math.pi / modulus)
    return (jnp.cos(theta), jnp.sin(theta))


def frequency_order(width):
    rows = jnp.arange(2 * width, dtype=jnp.int32)
    halves = rows // 2
    return jnp.where(rows % 2 == 0, halves, jnp.where(halves == 0, width, 2 * width - halves))


def across(table, data):
    return jnp.einsum("rd,dsc->rsc", table, data, precision=HIGHEST)


def along(table, data):
    return jnp.einsum("kb,rbc->rkc", table, data, precision=HIGHEST)


def rotate(real_part, imag_part, cosine, sine):
    return (real_part * cosine + imag_part * sine, imag_part * cosine - real_part * sine)


def general_on_device(query_stream, key_stream, value_stream, filter_taps, skip_weight):
    parts = lax.axis_size("ctx")
    device = lax.axis_index("ctx")
    length = query_stream.shape[1]
    channels = query_stream.shape[2]
    share = length // parts
    total = 2 * parts * length
    product = key_stream[0].astype(jnp.float32) * value_stream[0].astype(jnp.float32)
    taps = filter_taps[0].astype(jnp.float32)
    block_prod, block_taps = (
        lax.all_to_all(
            product.reshape(1, length, channels), "ctx", split_axis=1, concat_axis=0, tiled=True
        ),
        lax.all_to_all(
            taps.reshape(1, length, channels), "ctx", split_axis=1, concat_axis=0, tiled=True
        ),
    )
    order = frequency_order(parts)
    cos_cross, sin_cross = angles(2 * parts, order, jnp.arange(parts, dtype=jnp.int32))
    positions = device * share + jnp.arange(share, dtype=jnp.int32)
    cos_twist, sin_twist = angles(total, order, positions)
    cos_twist = cos_twist[:, :, None]
    sin_twist = sin_twist[:, :, None]
    span = jnp.arange(length, dtype=jnp.int32)
    cos_along, sin_along = angles(length, span, span)
    local_rows = lax.dynamic_slice(order, (2 * device,), (2,))
    cos_back, sin_back = angles(total, local_rows, span)
    cos_back = cos_back[:, :, None]
    sin_back = sin_back[:, :, None]

    def forward_along(real_part, imag_part):
        return (
            along(cos_along, real_part) + along(sin_along, imag_part),
            along(cos_along, imag_part) - along(sin_along, real_part),
        )

    prod_real, prod_imag = rotate(
        across(cos_cross, block_prod), -across(sin_cross, block_prod), cos_twist, sin_twist
    )
    taps_real, taps_imag = rotate(
        across(cos_cross, block_taps), -across(sin_cross, block_taps), cos_twist, sin_twist
    )
    first_real, first_imag = forward_along(
        lax.all_to_all(prod_real, "ctx", split_axis=0, concat_axis=1, tiled=True),
        lax.all_to_all(prod_imag, "ctx", split_axis=0, concat_axis=1, tiled=True),
    )
    second_real, second_imag = forward_along(
        lax.all_to_all(taps_real, "ctx", split_axis=0, concat_axis=1, tiled=True),
        lax.all_to_all(taps_imag, "ctx", split_axis=0, concat_axis=1, tiled=True),
    )
    result_real = first_real * second_real - first_imag * second_imag
    result_imag = first_real * second_imag + first_imag * second_real
    back_real = along(cos_along, result_real) - along(sin_along, result_imag)
    back_imag = along(cos_along, result_imag) + along(sin_along, result_real)
    spec_real, spec_imag = rotate(back_real, back_imag, cos_back, -sin_back)
    rows_real, rows_imag = (
        lax.all_to_all(spec_real, "ctx", split_axis=1, concat_axis=0, tiled=True),
        lax.all_to_all(spec_imag, "ctx", split_axis=1, concat_axis=0, tiled=True),
    )
    cos_final, sin_final = angles(2 * parts, jnp.arange(parts, dtype=jnp.int32), order)
    by_block = jnp.einsum("dr,rsc->dsc", cos_final, rows_real, precision=HIGHEST) - jnp.einsum(
        "dr,rsc->dsc", sin_final, rows_imag, precision=HIGHEST
    )
    by_block = by_block * (1.0 / total)
    convolved = lax.all_to_all(by_block, "ctx", split_axis=0, concat_axis=1, tiled=True)[0]
    gated = query_stream[0].astype(jnp.float32) * (convolved + skip_weight[0][None, :] * product)
    gated = gated.astype(jnp.bfloat16)[None]
    return from_behind(gated, "segment", 1)


def split_two(value):
    high = value.astype(BF16)
    return high, (value - high.astype(F32)).astype(BF16)


def stacked(value):
    high, low = split_two(value)
    return jnp.concatenate([high, low, high], axis=0)


def split_table(table):
    table = table.astype(np.float32)
    high = table.astype(jnp.bfloat16)
    low = (table - high.astype(np.float32)).astype(jnp.bfloat16)
    return np.concatenate([high, high, low], axis=1)


def group(shape):
    return lax.broadcasted_iota(jnp.int32, shape, len(shape) - 1) // QUARTER


def turned(value, groups):
    groups %= LANES // QUARTER
    return pltpu.roll(value, groups * QUARTER, value.ndim - 1) if groups else value


def chosen(where, values):
    result = values[0]
    for i in range(1, len(values)):
        result = jnp.where(where == i, values[i], result)
    return result


def tables(outer):
    total = outer * INNER
    a = np.arange(outer)
    b = np.arange(INNER)
    c = np.arange(outer) + 0.25
    first = 2.0 * np.pi * np.outer(c, a) / outer
    second = 2.0 * np.pi * np.outer(b, b) / INNER
    forward_a = split_table(np.concatenate([np.cos(first), -np.sin(first)], axis=0))
    back_a = split_table(np.concatenate([np.cos(first).T, -np.sin(first).T], axis=0) / total)
    forward_b, back_b = [], []
    for half in (second[:, :SPAN], second[:, SPAN:]):
        cos, sin = np.cos(half), np.sin(half)
        forward_b.append(split_table(np.block([[cos, sin], [-sin, cos]])))
        back_b.append(split_table(np.concatenate([cos, sin], axis=0)))
    theta = 2.0 * np.pi * np.outer(b, c) / total
    wide = np.stack([np.cos(theta), np.sin(theta)], axis=1).astype(np.float32)
    wide = np.broadcast_to(wide[..., None], wide.shape + (LANES // 2,))
    turns = np.concatenate([wide[:SPAN], wide[SPAN:]], axis=-1)
    return forward_a, np.concatenate(forward_b), np.concatenate(back_b), back_a, turns


def pack_kernel(parts, chunk, index_ref, k_ref, v_ref, h_ref, q_ref, *refs):
    outs, held = refs[:-1], refs[-1]
    length = k_ref.shape[0]
    rows = length // 2
    where = group((rows, LANES))

    def halves(ref, e):
        tile = ref[:, LANES * e : LANES * (e + 1)].astype(F32).reshape(length // INNER, INNER, LANES)
        return tile[:, :SPAN].reshape(rows, LANES), tile[:, SPAN:].reshape(rows, LANES)

    for e in range(parts // 2):
        for at, (even_ref, odd_ref) in enumerate(((k_ref, h_ref), (v_ref, q_ref))):
            even_lo, even_hi = halves(even_ref, e)
            odd_lo, odd_hi = halves(odd_ref, e)
            for side in range(2):
                g = 2 * side + chunk
                moved = [turned(x, j - g) for j, x in enumerate((even_lo, odd_lo, even_hi, odd_hi))]
                held[2 * e + side, at * rows : (at + 1) * rows, :] = chosen(where, moved).astype(BF16)
    for n, out in enumerate(outs):
        out[...] = held[lax.rem(index_ref[0] + n, parts)]


def unpack_kernel(parts, index_ref, *refs):
    blocks, out_ref, held = refs[: 2 * parts], refs[2 * parts], refs[2 * parts + 1]
    for chunk in range(2):
        for n in range(parts):
            held[chunk, lax.rem(index_ref[0] + n, parts)] = blocks[chunk * parts + n][...].astype(F32)
    rows = held.shape[2]
    spans = rows // SPAN
    where = group((rows, LANES))
    for e in range(parts // 2):
        pieces = [held[g % 2, 2 * e + g // 2] for g in range(4)]
        for j in range(4):
            value = chosen(where, [turned(piece, g - j) for g, piece in enumerate(pieces)])
            out_ref[
                spans * (j % 2) : spans * (j % 2 + 1),
                SPAN * (j // 2) : SPAN * (j // 2 + 1),
                LANES * e : LANES * (e + 1),
            ] = value.astype(BF16).reshape(spans, SPAN, LANES)


def convolve_kernel(parts, outer, index_ref, *refs):
    blocks, refs = refs[:parts], refs[parts:]
    skip_ref, fa_ref, fb_ref, bb_ref, ba_ref, turn_ref = refs[:6]
    outs, (x_s, z_s, w_s, y_s) = refs[6 : 6 + parts], refs[6 + parts :]
    rows = blocks[0].shape[0] // 2
    per = rows // SPAN

    def even(count):
        return group((count, LANES)) % 2 == 0

    def low(count):
        return group((count, LANES)) < 2

    def origin(n):
        return lax.rem(index_ref[0] + parts - n, parts)

    def folded(both):
        half = both.shape[0] // 2
        value = jnp.where(low(half), both[:half], both[half:])
        return value + turned(value, 2)

    def lanes(value, j):
        return value[:, LANES * j : LANES * (j + 1)]

    for n, block in enumerate(blocks):
        value = block[:rows, :].astype(F32) * jnp.where(even(rows), block[rows:, :].astype(F32), 1.0)
        for m in range(per):
            x_s[pl.ds(origin(n) * per + m, SPAN, stride=outer), :] = value[m * SPAN : (m + 1) * SPAN]

    def forward_outer(step, carry):
        at = step * WIDE
        data = [
            stacked(x_s[pl.ds(pl.multiple_of((at + j) * outer, outer), outer), :]) for j in range(WIDE)
        ]
        both = jnp.dot(fa_ref[...], jnp.concatenate(data, axis=1), preferred_element_type=F32)
        for j in range(WIDE):
            re, im = lanes(both[:outer], j), lanes(both[outer:], j)
            cos, sin = turn_ref[at + j, 0], turn_ref[at + j, 1]
            z_s[pl.ds(at + j, outer, stride=2 * SPAN), :] = re * cos + im * sin
            z_s[pl.ds(at + j + SPAN, outer, stride=2 * SPAN), :] = im * cos - re * sin
        return carry

    lax.fori_loop(0, SPAN // WIDE, forward_outer, 0)

    def middle(step, carry):
        at = step * WIDE
        data = [
            stacked(z_s[pl.ds(pl.multiple_of((at + j) * 2 * SPAN, 2 * SPAN), 2 * SPAN), :])
            for j in range(WIDE)
        ]
        both = jnp.dot(fb_ref[...], jnp.concatenate(data, axis=1), preferred_element_type=F32)
        data = []
        for j in range(WIDE):
            value = folded(lanes(both, j))
            re, im = value[:INNER], value[INNER:]
            re_2, im_2 = turned(re, 1), turned(im, 1)
            value = jnp.where(even(INNER), re * re_2 - im * im_2, re * im_2 + im * re_2)
            data.append(stacked(jnp.where(low(SPAN), value[:SPAN], value[SPAN:])))
        both = jnp.dot(bb_ref[...], jnp.concatenate(data, axis=1), preferred_element_type=F32)
        for j in range(WIDE):
            value = folded(lanes(both, j))
            straight, crossed = value[:INNER], turned(value[INNER:], 1)
            value = jnp.where(even(INNER), straight - crossed, straight + crossed)
            w_s[pl.ds(at + j, SPAN, stride=outer), :] = jnp.where(low(SPAN), value[:SPAN], value[SPAN:])
        return carry

    lax.fori_loop(0, outer // WIDE, middle, 0)

    def back_outer(step, carry):
        at = step * WIDE
        data = []
        for j in range(WIDE):
            value = w_s[pl.ds(pl.multiple_of((at + j) * outer, outer), outer), :]
            other = jnp.where(even(outer), -turned(value, -1), turned(value, 1))
            data.append(stacked(value * turn_ref[at + j, 0] + other * turn_ref[at + j, 1]))
        both = jnp.dot(ba_ref[...], jnp.concatenate(data, axis=1), preferred_element_type=F32)
        for j in range(WIDE):
            y_s[pl.ds(at + j, outer, stride=SPAN), :] = lanes(both[:outer], j) + turned(
                lanes(both[outer:], j), -1
            )
        return carry

    lax.fori_loop(0, SPAN // WIDE, back_outer, 0)

    for n, (block, out) in enumerate(zip(blocks, outs)):
        y = y_s[pl.ds(pl.multiple_of(origin(n) * rows, rows), rows), :]
        second = block[rows:, :].astype(F32)
        product = block[:rows, :].astype(F32) * second
        gated = turned(second, -1) * (y + skip_ref[...] * product)
        half = rows // 2
        out[...] = jnp.where(even(half), gated[:half], turned(gated[half:], 1)).astype(BF16)


def joint_shift(value, segment_step, ctx_step):
    segments, parts = lax.axis_size("segment"), lax.axis_size("ctx")
    pairs = [
        (s * parts + c, (s + segment_step) % segments * parts + (c + ctx_step) % parts)
        for s in range(segments)
        for c in range(parts)
    ]
    return lax.ppermute(value, ("segment", "ctx"), pairs)


def fast_on_device(query_stream, key_stream, value_stream, filter_taps, skip_weight):
    parts = lax.axis_size("ctx")
    device = lax.axis_index("ctx")
    length, channels = query_stream.shape[1:]
    rows = length // 2
    outer = parts * length // INNER
    index = jnp.full((1,), device, jnp.int32)
    scalar = pl.BlockSpec(memory_space=pltpu.SMEM)
    whole = pl.BlockSpec(memory_space=pltpu.VMEM)
    consts = [jnp.asarray(t) for t in tables(outer)]
    back = []
    packed = []
    for chunk in range(2):
        sent = pl.pallas_call(
            functools.partial(pack_kernel, parts, chunk),
            out_shape=(jax.ShapeDtypeStruct((length, LANES), BF16),) * parts,
            in_specs=[scalar] + [whole] * 4,
            scratch_shapes=[pltpu.VMEM((parts, length, LANES), BF16)],
            compiler_params=pltpu.CompilerParams(vmem_limit_bytes=20 * 2**20),
        )(index, key_stream[0], value_stream[0], filter_taps[0], query_stream[0])
        packed.append([sent[0]] + [joint_shift(sent[n], 0, n) for n in range(1, parts)])
    for chunk in range(2):
        skip = lax.dynamic_slice(skip_weight, (0, device * HALF + chunk * QUARTER), (1, QUARTER))
        gated = pl.pallas_call(
            functools.partial(convolve_kernel, parts, outer),
            out_shape=(jax.ShapeDtypeStruct((rows // 2, LANES), BF16),) * parts,
            in_specs=[scalar] + [whole] * (parts + 1 + len(consts)),
            scratch_shapes=[
                pltpu.VMEM((outer * SPAN, LANES), F32),
                pltpu.VMEM((2 * outer * SPAN, LANES), F32),
                pltpu.VMEM((outer * SPAN, LANES), F32),
                pltpu.VMEM((outer * SPAN, LANES), F32),
            ],
            compiler_params=pltpu.CompilerParams(vmem_limit_bytes=24 * 2**20),
            cost_estimate=pl.CostEstimate(flops=6 * 10**9, bytes_accessed=4 * 10**6, transcendentals=0),
        )(index, *packed[chunk], jnp.concatenate([skip] * 4, axis=1), *consts)
        back += [joint_shift(gated[n], 1, -n) for n in range(parts)]
    out = pl.pallas_call(
        functools.partial(unpack_kernel, parts),
        out_shape=jax.ShapeDtypeStruct((length // INNER, INNER, channels), BF16),
        in_specs=[scalar] + [whole] * (2 * parts),
        scratch_shapes=[pltpu.VMEM((2, parts, rows // 2, LANES), F32)],
        compiler_params=pltpu.CompilerParams(vmem_limit_bytes=20 * 2**20),
    )(index, *back)
    return out.reshape(1, length, channels)


def solution(mesh):
    placed = (
        P("segment", "ctx", None),
        P("segment", "ctx", None),
        P("segment", "ctx", None),
        P("segment", "ctx", None),
        P("segment", None),
    )

    def on_device(*arrays):
        parts = lax.axis_size("ctx")
        length, channels = arrays[0].shape[1:]
        small = parts * length <= 4096 and length % (2 * INNER) == 0 and parts % 2 == 0
        run = fast_on_device if small and channels == parts * HALF else general_on_device
        return run(*arrays)

    return jax.shard_map(
        on_device, mesh=mesh, in_specs=placed, out_specs=P("segment", "ctx", None), check_vma=False
    )
```

```python
import functools
import math

import jax
import jax.numpy as jnp
import numpy as np
from jax import lax
from jax.experimental import pallas as pl
from jax.experimental.pallas import tpu as pltpu
from jax.sharding import PartitionSpec as P

HIGHEST = lax.Precision.HIGHEST
LANES = 128
HALF = 64
INNER = 64
STEP = 16
EXTRA = 16
DOUBLINGS = 4
SCALE = 215.0
SMALLEST = 1e-30
WIDE = 16
F32 = jnp.float32
BF16 = jnp.bfloat16


def from_behind(value, axis, steps):
    count = lax.axis_size(axis)
    pairs = [(source, (source + steps) % count) for source in range(count)]
    return lax.ppermute(value, axis, pairs)


def angles(modulus, left, right):
    phase = left[:, None] * right[None, :] % modulus
    theta = phase.astype(jnp.float32) * (2.0 * math.pi / modulus)
    return (jnp.cos(theta), jnp.sin(theta))


def frequency_order(width):
    rows = jnp.arange(2 * width, dtype=jnp.int32)
    halves = rows // 2
    return jnp.where(rows % 2 == 0, halves, jnp.where(halves == 0, width, 2 * width - halves))


def across(table, data):
    return jnp.einsum("rd,dsc->rsc", table, data, precision=HIGHEST)


def along(table, data):
    return jnp.einsum("kb,rbc->rkc", table, data, precision=HIGHEST)


def rotate(real_part, imag_part, cosine, sine):
    return (real_part * cosine + imag_part * sine, imag_part * cosine - real_part * sine)


def general_on_device(query_stream, key_stream, value_stream, filter_taps, skip_weight):
    parts = lax.axis_size("ctx")
    device = lax.axis_index("ctx")
    length = query_stream.shape[1]
    channels = query_stream.shape[2]
    share = length // parts
    total = 2 * parts * length
    product = key_stream[0].astype(jnp.float32) * value_stream[0].astype(jnp.float32)
    taps = filter_taps[0].astype(jnp.float32)
    block_prod, block_taps = (
        lax.all_to_all(
            product.reshape(1, length, channels), "ctx", split_axis=1, concat_axis=0, tiled=True
        ),
        lax.all_to_all(
            taps.reshape(1, length, channels), "ctx", split_axis=1, concat_axis=0, tiled=True
        ),
    )
    order = frequency_order(parts)
    cos_cross, sin_cross = angles(2 * parts, order, jnp.arange(parts, dtype=jnp.int32))
    positions = device * share + jnp.arange(share, dtype=jnp.int32)
    cos_twist, sin_twist = angles(total, order, positions)
    cos_twist = cos_twist[:, :, None]
    sin_twist = sin_twist[:, :, None]
    span = jnp.arange(length, dtype=jnp.int32)
    cos_along, sin_along = angles(length, span, span)
    local_rows = lax.dynamic_slice(order, (2 * device,), (2,))
    cos_back, sin_back = angles(total, local_rows, span)
    cos_back = cos_back[:, :, None]
    sin_back = sin_back[:, :, None]

    def forward_along(real_part, imag_part):
        return (
            along(cos_along, real_part) + along(sin_along, imag_part),
            along(cos_along, imag_part) - along(sin_along, real_part),
        )

    prod_real, prod_imag = rotate(
        across(cos_cross, block_prod), -across(sin_cross, block_prod), cos_twist, sin_twist
    )
    taps_real, taps_imag = rotate(
        across(cos_cross, block_taps), -across(sin_cross, block_taps), cos_twist, sin_twist
    )
    first_real, first_imag = forward_along(
        lax.all_to_all(prod_real, "ctx", split_axis=0, concat_axis=1, tiled=True),
        lax.all_to_all(prod_imag, "ctx", split_axis=0, concat_axis=1, tiled=True),
    )
    second_real, second_imag = forward_along(
        lax.all_to_all(taps_real, "ctx", split_axis=0, concat_axis=1, tiled=True),
        lax.all_to_all(taps_imag, "ctx", split_axis=0, concat_axis=1, tiled=True),
    )
    result_real = first_real * second_real - first_imag * second_imag
    result_imag = first_real * second_imag + first_imag * second_real
    back_real = along(cos_along, result_real) - along(sin_along, result_imag)
    back_imag = along(cos_along, result_imag) + along(sin_along, result_real)
    spec_real, spec_imag = rotate(back_real, back_imag, cos_back, -sin_back)
    rows_real, rows_imag = (
        lax.all_to_all(spec_real, "ctx", split_axis=1, concat_axis=0, tiled=True),
        lax.all_to_all(spec_imag, "ctx", split_axis=1, concat_axis=0, tiled=True),
    )
    cos_final, sin_final = angles(2 * parts, jnp.arange(parts, dtype=jnp.int32), order)
    by_block = jnp.einsum("dr,rsc->dsc", cos_final, rows_real, precision=HIGHEST) - jnp.einsum(
        "dr,rsc->dsc", sin_final, rows_imag, precision=HIGHEST
    )
    by_block = by_block * (1.0 / total)
    convolved = lax.all_to_all(by_block, "ctx", split_axis=0, concat_axis=1, tiled=True)[0]
    gated = query_stream[0].astype(jnp.float32) * (convolved + skip_weight[0][None, :] * product)
    gated = gated.astype(jnp.bfloat16)[None]
    return from_behind(gated, "segment", 1)


def split_two(value):
    high = value.astype(BF16)
    return high, (value - high.astype(F32)).astype(BF16)


def split_table(table):
    table = table.astype(np.float32)
    high = table.astype(jnp.bfloat16)
    low = (table - high.astype(np.float32)).astype(jnp.bfloat16)
    return np.concatenate([high, high, low], axis=1)


def stacked(value):
    high, low = split_two(value)
    return jnp.concatenate([high, low, high], axis=0)


def lower_half(shape):
    return lax.broadcasted_iota(jnp.int32, shape, len(shape) - 1) < HALF


def swap_halves(value):
    return pltpu.roll(value, HALF, value.ndim - 1)


def tables(outer):
    total = outer * INNER
    a = np.arange(outer)
    b = np.arange(INNER)
    c = np.arange(outer) + 0.25
    first = 2.0 * np.pi * np.outer(c, a) / outer
    second = 2.0 * np.pi * np.outer(b, b) / INNER
    forward_a = split_table(np.concatenate([np.cos(first), -np.sin(first)], axis=0))
    forward_b = split_table(
        np.block([[np.cos(second), np.sin(second)], [-np.sin(second), np.cos(second)]])
    )
    back_b = split_table(np.concatenate([np.cos(second), np.sin(second)], axis=0))
    back_a = split_table(np.concatenate([np.cos(first).T, -np.sin(first).T], axis=0) / total)

    def turns(steps):
        theta = 2.0 * np.pi * np.outer(steps, c) / total
        wide = np.stack([np.cos(theta), np.sin(theta)], axis=1).astype(np.float32)
        return np.ascontiguousarray(np.broadcast_to(wide[..., None], wide.shape + (LANES,)))

    return np.concatenate([forward_a, back_a, forward_b, back_b], axis=1), turns(b)


def fetched(sources, targets, sems):
    copies = [pltpu.make_async_copy(a, b, sems.at[i]) for i, (a, b) in enumerate(zip(sources, targets))]
    for copy in copies:
        copy.start()
    return copies


def pack_kernel(parts, index_ref, *refs):
    sources, outs, held, arrived, sems = refs[:4], refs[4 : 4 + parts], refs[-6], refs[-5:-1], refs[-1]
    k_ref, v_ref, h_ref, q_ref = arrived
    rows = k_ref.shape[0] // 2
    low = lower_half((rows, LANES))
    for copy in fetched(sources, arrived, sems):
        copy.wait()

    def place(e, at, tile, low):
        half = tile.shape[0] // 2
        early, late = tile[:half], tile[half:]
        held[2 * e, at : at + half, :] = jnp.where(low, early, swap_halves(late)).astype(BF16)
        held[2 * e + 1, at : at + half, :] = jnp.where(low, swap_halves(early), late).astype(BF16)

    for e in range(parts // 2):
        lanes = slice(LANES * e, LANES * (e + 1))
        product = k_ref[:, lanes].astype(F32) * v_ref[:, lanes].astype(F32)
        largest = jnp.max(jnp.abs(product), axis=0, keepdims=True)
        largest = jnp.maximum(largest * 1.01, SMALLEST).astype(BF16).astype(F32)
        code = product * (SCALE / largest)
        power = code * code
        for _ in range(DOUBLINGS - 1):
            power = power * power
        place(e, 0, jnp.where(code < 0.0, -power, power), low)
        place(e, rows, h_ref[:, lanes].astype(F32), low)
        place(e, 2 * rows, q_ref[:, lanes].astype(F32), low)
        place(e, 3 * rows, jnp.broadcast_to(largest, (2 * EXTRA, LANES)), low[:EXTRA])
    for n, out in enumerate(outs):
        out[...] = held[lax.rem(index_ref[0] + n, parts)]


def unpack_kernel(parts, index_ref, *refs):
    blocks, out_ref, held = refs[:parts], refs[parts], refs[parts + 1]
    rows = held.shape[1]
    low = lower_half((rows, LANES))
    for n, block in enumerate(blocks):
        held[lax.rem(index_ref[0] + n, parts)] = block[...]
    for e in range(parts // 2):
        even, odd = held[2 * e].astype(F32), held[2 * e + 1].astype(F32)
        out_ref[:rows, LANES * e : LANES * (e + 1)] = jnp.where(low, even, swap_halves(odd)).astype(BF16)
        out_ref[rows:, LANES * e : LANES * (e + 1)] = jnp.where(low, swap_halves(even), odd).astype(BF16)


def convolve_kernel(parts, outer, index_ref, *refs):
    blocks = refs[:parts]
    skip_ref, sources = refs[parts], refs[parts + 1 : parts + 3]
    outs, (x_s, z_s, w_s, y_s, p_s) = refs[parts + 3 : 2 * parts + 3], refs[2 * parts + 3 : 2 * parts + 8]
    matrix_ref, turn_ref = arrived = refs[2 * parts + 8 : 2 * parts + 10]
    copies = fetched(sources, arrived, refs[-1])
    edges = (0, 3 * outer, 6 * outer, 6 * outer + 6 * INNER, 6 * outer + 9 * INNER)
    rows = outs[0].shape[0]
    per = rows // INNER
    low = lower_half((INNER, LANES))
    lowc = lower_half((outer, LANES))

    def origin(n):
        return lax.rem(index_ref[0] + parts - n, parts)

    for n, block in enumerate(blocks):
        scale = block[3 * rows : 3 * rows + EXTRA, :].astype(F32)[:1] * (1.0 / SCALE)
        for m in range(per):
            at = m * INNER
            code = block[at : at + INNER, :].astype(F32)
            size = jnp.exp(jnp.log(jnp.abs(code)) * (0.5**DOUBLINGS)) * scale
            p = jnp.where(code == 0.0, 0.0, jnp.where(code < 0.0, -size, size))
            p_s[n, at : at + INNER, :] = p
            h = block[rows + at : rows + at + INNER, :].astype(F32)
            a = origin(n) * (2 * per) + m
            x_s[pl.ds(a, INNER, stride=outer), :] = jnp.where(low, p, swap_halves(h))
            x_s[pl.ds(a + per, INNER, stride=outer), :] = jnp.where(low, swap_halves(p), h)

    for copy in copies:
        copy.wait()

    def matrix(i):
        return matrix_ref[:, edges[i] : edges[i + 1]]

    def turn(group, n):
        return turn_ref[group * STEP + n, 0], turn_ref[group * STEP + n, 1]

    def forward_outer(group, carry):
        for n in range(0, STEP, WIDE):
            b = group * STEP + n
            data = jnp.concatenate(
                [
                    stacked(x_s[pl.ds(pl.multiple_of((b + j) * outer, outer), outer), :])
                    for j in range(WIDE)
                ],
                axis=1,
            )
            both = jnp.dot(matrix(0), data, preferred_element_type=F32)
            for j in range(WIDE):
                re = both[:outer, LANES * j : LANES * (j + 1)]
                im = both[outer:, LANES * j : LANES * (j + 1)]
                cos, sin = turn(group, n + j)
                z_s[pl.ds(b + j, outer, stride=2 * INNER), :] = re * cos + im * sin
                z_s[pl.ds(b + j + INNER, outer, stride=2 * INNER), :] = im * cos - re * sin
        return carry

    lax.fori_loop(0, INNER // STEP, forward_outer, 0)

    def middle(group, carry):
        for n in range(0, STEP, WIDE):
            c = group * STEP + n
            data = jnp.concatenate(
                [
                    stacked(z_s[pl.ds(pl.multiple_of((c + j) * 2 * INNER, 2 * INNER), 2 * INNER), :])
                    for j in range(WIDE)
                ],
                axis=1,
            )
            both = jnp.dot(matrix(2), data, preferred_element_type=F32)
            mixed = []
            for j in range(WIDE):
                re = both[:INNER, LANES * j : LANES * (j + 1)]
                im = both[INNER:, LANES * j : LANES * (j + 1)]
                re_2, im_2 = swap_halves(re), swap_halves(im)
                mixed.append(
                    stacked(jnp.where(low, re * re_2 - im * im_2, re * im_2 + im * re_2))
                )
            both = jnp.dot(matrix(3), jnp.concatenate(mixed, axis=1), preferred_element_type=F32)
            for j in range(WIDE):
                straight = both[:INNER, LANES * j : LANES * (j + 1)]
                crossed = swap_halves(both[INNER:, LANES * j : LANES * (j + 1)])
                w_s[pl.ds(c + j, INNER, stride=outer), :] = jnp.where(
                    low, straight - crossed, straight + crossed
                )
        return carry

    lax.fori_loop(0, outer // STEP, middle, 0)

    def back_outer(group, carry):
        for n in range(0, STEP, WIDE):
            b = group * STEP + n
            data = []
            for j in range(WIDE):
                value = w_s[pl.ds(pl.multiple_of((b + j) * outer, outer), outer), :]
                cos, sin = turn(group, n + j)
                other = swap_halves(value) * sin
                straight = value * cos
                data.append(stacked(jnp.where(lowc, straight - other, straight + other)))
            both = jnp.dot(matrix(1), jnp.concatenate(data, axis=1), preferred_element_type=F32)
            for j in range(WIDE):
                re = both[:outer, LANES * j : LANES * (j + 1)]
                im = both[outer:, LANES * j : LANES * (j + 1)]
                y_s[pl.ds(b + j, outer, stride=INNER), :] = re + swap_halves(im)
        return carry

    lax.fori_loop(0, INNER // STEP, back_outer, 0)

    lowr = lower_half((rows, LANES))
    for n, (block, out) in enumerate(zip(blocks, outs)):
        at = pl.multiple_of(origin(n) * 2 * rows, 2 * rows)
        early = y_s[pl.ds(at, rows), :]
        late = y_s[pl.ds(at + rows, rows), :]
        y = jnp.where(lowr, early, swap_halves(late)) + skip_ref[...] * p_s[n]
        out[...] = (block[2 * rows : 3 * rows, :].astype(F32) * y).astype(BF16)


def joint_shift(value, segment_step, ctx_step):
    segments, parts = lax.axis_size("segment"), lax.axis_size("ctx")
    pairs = [
        (s * parts + c, (s + segment_step) % segments * parts + (c + ctx_step) % parts)
        for s in range(segments)
        for c in range(parts)
    ]
    return lax.ppermute(value, ("segment", "ctx"), pairs)


def fast_on_device(query_stream, key_stream, value_stream, filter_taps, skip_weight):
    parts = lax.axis_size("ctx")
    device = lax.axis_index("ctx")
    length, channels = query_stream.shape[1:]
    rows = length // 2
    outer = parts * length // INNER
    index = jnp.full((1,), device, jnp.int32)
    scalar = pl.BlockSpec(memory_space=pltpu.SMEM)
    whole = pl.BlockSpec(memory_space=pltpu.VMEM)
    far = pl.BlockSpec(memory_space=pltpu.HBM)
    small = pltpu.CompilerParams(vmem_limit_bytes=24 * 2**20)
    large = pltpu.CompilerParams(vmem_limit_bytes=60 * 2**20)

    def block(*shape, dtype=BF16):
        return jax.ShapeDtypeStruct(shape, dtype)

    size = 3 * rows + EXTRA
    sent = pl.pallas_call(
        functools.partial(pack_kernel, parts),
        out_shape=(block(size, LANES),) * parts,
        in_specs=[scalar] + [far] * 4,
        scratch_shapes=[pltpu.VMEM((parts, size, LANES), BF16)]
        + [pltpu.VMEM((length, channels), BF16)] * 4
        + [pltpu.SemaphoreType.DMA((4,))],
        compiler_params=large,
    )(index, key_stream[0], value_stream[0], filter_taps[0], query_stream[0])
    slabs = [sent[0]] + [joint_shift(sent[n], 0, n) for n in range(1, parts)]
    skip = lax.dynamic_slice(skip_weight, (0, device * HALF), (1, HALF))
    consts = [jnp.asarray(t) for t in tables(outer)]
    gated = pl.pallas_call(
        functools.partial(convolve_kernel, parts, outer),
        out_shape=(block(rows, LANES),) * parts,
        in_specs=[scalar] + [whole] * (parts + 1) + [far] * len(consts),
        scratch_shapes=[
            pltpu.VMEM((outer * INNER, LANES), F32),
            pltpu.VMEM((2 * outer * INNER, LANES), F32),
            pltpu.VMEM((outer * INNER, LANES), F32),
            pltpu.VMEM((outer * INNER, LANES), F32),
            pltpu.VMEM((parts, rows, LANES), F32),
        ]
        + [pltpu.VMEM(t.shape, t.dtype) for t in consts]
        + [pltpu.SemaphoreType.DMA((len(consts),))],
        compiler_params=large,
    )(index, *slabs, jnp.concatenate([skip, skip], axis=1), *consts)
    gated = [joint_shift(gated[n], 1, -n) for n in range(parts)]
    out = pl.pallas_call(
        functools.partial(unpack_kernel, parts),
        out_shape=block(length, channels),
        in_specs=[scalar] + [whole] * parts,
        scratch_shapes=[pltpu.VMEM((parts, rows, LANES), BF16)],
        compiler_params=small,
    )(index, *gated)
    return out[None]


def solution(mesh):
    placed = (
        P("segment", "ctx", None),
        P("segment", "ctx", None),
        P("segment", "ctx", None),
        P("segment", "ctx", None),
        P("segment", None),
    )

    def on_device(*arrays):
        parts = lax.axis_size("ctx")
        length, channels = arrays[0].shape[1:]
        square = parts * length == INNER * INNER
        run = fast_on_device if square and channels == parts * HALF else general_on_device
        return run(*arrays)

    return jax.shard_map(
        on_device, mesh=mesh, in_specs=placed, out_specs=P("segment", "ctx", None), check_vma=False
    )
```

```python
import functools
import math

import jax
import jax.numpy as jnp
import numpy as np
from jax import lax
from jax.experimental import pallas as pl
from jax.experimental.pallas import tpu as pltpu
from jax.sharding import PartitionSpec as P

HIGHEST = lax.Precision.HIGHEST
LANES = 128
HALF = 64
INNER = 64
STEP = 16
EXTRA = 16
DOUBLINGS = 4
SCALE = 215.0
SMALLEST = 1e-30
WIDE = 16
F32 = jnp.float32
BF16 = jnp.bfloat16


def from_behind(value, axis, steps):
    count = lax.axis_size(axis)
    pairs = [(source, (source + steps) % count) for source in range(count)]
    return lax.ppermute(value, axis, pairs)


def angles(modulus, left, right):
    phase = left[:, None] * right[None, :] % modulus
    theta = phase.astype(jnp.float32) * (2.0 * math.pi / modulus)
    return (jnp.cos(theta), jnp.sin(theta))


def frequency_order(width):
    rows = jnp.arange(2 * width, dtype=jnp.int32)
    halves = rows // 2
    return jnp.where(rows % 2 == 0, halves, jnp.where(halves == 0, width, 2 * width - halves))


def across(table, data):
    return jnp.einsum("rd,dsc->rsc", table, data, precision=HIGHEST)


def along(table, data):
    return jnp.einsum("kb,rbc->rkc", table, data, precision=HIGHEST)


def rotate(real_part, imag_part, cosine, sine):
    return (real_part * cosine + imag_part * sine, imag_part * cosine - real_part * sine)


def general_on_device(query_stream, key_stream, value_stream, filter_taps, skip_weight):
    parts = lax.axis_size("ctx")
    device = lax.axis_index("ctx")
    length = query_stream.shape[1]
    channels = query_stream.shape[2]
    share = length // parts
    total = 2 * parts * length
    product = key_stream[0].astype(jnp.float32) * value_stream[0].astype(jnp.float32)
    taps = filter_taps[0].astype(jnp.float32)
    block_prod, block_taps = (
        lax.all_to_all(
            product.reshape(1, length, channels), "ctx", split_axis=1, concat_axis=0, tiled=True
        ),
        lax.all_to_all(
            taps.reshape(1, length, channels), "ctx", split_axis=1, concat_axis=0, tiled=True
        ),
    )
    order = frequency_order(parts)
    cos_cross, sin_cross = angles(2 * parts, order, jnp.arange(parts, dtype=jnp.int32))
    positions = device * share + jnp.arange(share, dtype=jnp.int32)
    cos_twist, sin_twist = angles(total, order, positions)
    cos_twist = cos_twist[:, :, None]
    sin_twist = sin_twist[:, :, None]
    span = jnp.arange(length, dtype=jnp.int32)
    cos_along, sin_along = angles(length, span, span)
    local_rows = lax.dynamic_slice(order, (2 * device,), (2,))
    cos_back, sin_back = angles(total, local_rows, span)
    cos_back = cos_back[:, :, None]
    sin_back = sin_back[:, :, None]

    def forward_along(real_part, imag_part):
        return (
            along(cos_along, real_part) + along(sin_along, imag_part),
            along(cos_along, imag_part) - along(sin_along, real_part),
        )

    prod_real, prod_imag = rotate(
        across(cos_cross, block_prod), -across(sin_cross, block_prod), cos_twist, sin_twist
    )
    taps_real, taps_imag = rotate(
        across(cos_cross, block_taps), -across(sin_cross, block_taps), cos_twist, sin_twist
    )
    first_real, first_imag = forward_along(
        lax.all_to_all(prod_real, "ctx", split_axis=0, concat_axis=1, tiled=True),
        lax.all_to_all(prod_imag, "ctx", split_axis=0, concat_axis=1, tiled=True),
    )
    second_real, second_imag = forward_along(
        lax.all_to_all(taps_real, "ctx", split_axis=0, concat_axis=1, tiled=True),
        lax.all_to_all(taps_imag, "ctx", split_axis=0, concat_axis=1, tiled=True),
    )
    result_real = first_real * second_real - first_imag * second_imag
    result_imag = first_real * second_imag + first_imag * second_real
    back_real = along(cos_along, result_real) - along(sin_along, result_imag)
    back_imag = along(cos_along, result_imag) + along(sin_along, result_real)
    spec_real, spec_imag = rotate(back_real, back_imag, cos_back, -sin_back)
    rows_real, rows_imag = (
        lax.all_to_all(spec_real, "ctx", split_axis=1, concat_axis=0, tiled=True),
        lax.all_to_all(spec_imag, "ctx", split_axis=1, concat_axis=0, tiled=True),
    )
    cos_final, sin_final = angles(2 * parts, jnp.arange(parts, dtype=jnp.int32), order)
    by_block = jnp.einsum("dr,rsc->dsc", cos_final, rows_real, precision=HIGHEST) - jnp.einsum(
        "dr,rsc->dsc", sin_final, rows_imag, precision=HIGHEST
    )
    by_block = by_block * (1.0 / total)
    convolved = lax.all_to_all(by_block, "ctx", split_axis=0, concat_axis=1, tiled=True)[0]
    gated = query_stream[0].astype(jnp.float32) * (convolved + skip_weight[0][None, :] * product)
    gated = gated.astype(jnp.bfloat16)[None]
    return from_behind(gated, "segment", 1)


def split_two(value):
    high = value.astype(BF16)
    return high, (value - high.astype(F32)).astype(BF16)


def split_table(table):
    table = table.astype(np.float32)
    high = table.astype(jnp.bfloat16)
    low = (table - high.astype(np.float32)).astype(jnp.bfloat16)
    return np.concatenate([high, high, low], axis=1)


def stacked(value):
    high, low = split_two(value)
    return jnp.concatenate([high, low, high], axis=0)


def lower_half(shape):
    return lax.broadcasted_iota(jnp.int32, shape, len(shape) - 1) < HALF


def swap_halves(value):
    return pltpu.roll(value, HALF, value.ndim - 1)


def tables(outer):
    total = outer * INNER
    a = np.arange(outer)
    b = np.arange(INNER)
    c = np.arange(outer) + 0.25
    first = 2.0 * np.pi * np.outer(c, a) / outer
    second = 2.0 * np.pi * np.outer(b, b) / INNER
    forward_a = split_table(np.concatenate([np.cos(first), -np.sin(first)], axis=0))
    forward_b = split_table(
        np.block([[np.cos(second), np.sin(second)], [-np.sin(second), np.cos(second)]])
    )
    back_b = split_table(np.concatenate([np.cos(second), np.sin(second)], axis=0))
    back_a = split_table(np.concatenate([np.cos(first).T, -np.sin(first).T], axis=0) / total)

    def turns(steps):
        theta = 2.0 * np.pi * np.outer(steps, c) / total
        wide = np.stack([np.cos(theta), np.sin(theta)], axis=1).astype(np.float32)
        return np.ascontiguousarray(np.broadcast_to(wide[..., None], wide.shape + (LANES,)))

    return np.concatenate([forward_a, back_a, forward_b, back_b], axis=1), turns(b)


def fetched(sources, targets, sems):
    copies = [pltpu.make_async_copy(a, b, sems.at[i]) for i, (a, b) in enumerate(zip(sources, targets))]
    for copy in copies:
        copy.start()
    return copies


def pack_kernel(parts, index_ref, *refs):
    sources, outs, held, arrived, sems = refs[:3], refs[3 : 3 + parts], refs[-5], refs[-4:-1], refs[-1]
    k_ref, v_ref, h_ref = arrived
    rows = k_ref.shape[0] // 2
    low = lower_half((rows, LANES))
    for copy in fetched(sources, arrived, sems):
        copy.wait()

    def place(e, at, tile, low):
        half = tile.shape[0] // 2
        early, late = tile[:half], tile[half:]
        held[2 * e, at : at + half, :] = jnp.where(low, early, swap_halves(late)).astype(BF16)
        held[2 * e + 1, at : at + half, :] = jnp.where(low, swap_halves(early), late).astype(BF16)

    for e in range(parts // 2):
        lanes = slice(LANES * e, LANES * (e + 1))
        product = k_ref[:, lanes].astype(F32) * v_ref[:, lanes].astype(F32)
        largest = jnp.max(jnp.abs(product), axis=0, keepdims=True)
        largest = jnp.maximum(largest * 1.01, SMALLEST).astype(BF16).astype(F32)
        code = product * (SCALE / largest)
        power = code * code
        for _ in range(DOUBLINGS - 1):
            power = power * power
        place(e, 0, jnp.where(code < 0.0, -power, power), low)
        place(e, rows, h_ref[:, lanes].astype(F32), low)
        place(e, 2 * rows, jnp.broadcast_to(largest, (2 * EXTRA, LANES)), low[:EXTRA])
    for n, out in enumerate(outs):
        out[...] = held[lax.rem(index_ref[0] + n, parts)]


def pack_gate_kernel(parts, q_ref, out_ref):
    rows = q_ref.shape[0] // 2
    low = lower_half((rows, LANES))
    for e in range(parts // 2):
        tile = q_ref[:, LANES * e : LANES * (e + 1)].astype(F32)
        early, late = tile[:rows], tile[rows:]
        out_ref[2 * e] = jnp.where(low, early, swap_halves(late)).astype(BF16)
        out_ref[2 * e + 1] = jnp.where(low, swap_halves(early), late).astype(BF16)


def unpack_kernel(parts, index_ref, *refs):
    blocks, out_ref, held = refs[:parts], refs[parts], refs[parts + 1]
    rows = held.shape[1]
    low = lower_half((rows, LANES))
    for n, block in enumerate(blocks):
        held[lax.rem(index_ref[0] + n, parts)] = block[...]
    for e in range(parts // 2):
        even, odd = held[2 * e].astype(F32), held[2 * e + 1].astype(F32)
        out_ref[:rows, LANES * e : LANES * (e + 1)] = jnp.where(low, even, swap_halves(odd)).astype(BF16)
        out_ref[rows:, LANES * e : LANES * (e + 1)] = jnp.where(low, swap_halves(even), odd).astype(BF16)


def convolve_kernel(parts, outer, index_ref, *refs):
    blocks = refs[:parts]
    skip_ref, sources = refs[parts], refs[parts + 1 : parts + 3]
    out_ref, x_s, z_s, w_s, y_s, p_s = refs[parts + 3 : parts + 9]
    matrix_ref, turn_ref = arrived = refs[parts + 9 : parts + 11]
    copies = fetched(sources, arrived, refs[-1])
    edges = (0, 3 * outer, 6 * outer, 6 * outer + 6 * INNER, 6 * outer + 9 * INNER)
    rows = out_ref.shape[1]
    per = rows // INNER
    low = lower_half((INNER, LANES))
    lowc = lower_half((outer, LANES))

    def origin(n):
        return lax.rem(index_ref[0] + parts - n, parts)

    for n, block in enumerate(blocks):
        scale = block[2 * rows : 2 * rows + EXTRA, :].astype(F32)[:1] * (1.0 / SCALE)
        for m in range(per):
            at = m * INNER
            code = block[at : at + INNER, :].astype(F32)
            size = jnp.exp(jnp.log(jnp.abs(code)) * (0.5**DOUBLINGS)) * scale
            p = jnp.where(code == 0.0, 0.0, jnp.where(code < 0.0, -size, size))
            p_s[n, at : at + INNER, :] = p
            h = block[rows + at : rows + at + INNER, :].astype(F32)
            a = origin(n) * (2 * per) + m
            x_s[pl.ds(a, INNER, stride=outer), :] = jnp.where(low, p, swap_halves(h))
            x_s[pl.ds(a + per, INNER, stride=outer), :] = jnp.where(low, swap_halves(p), h)

    for copy in copies:
        copy.wait()

    def matrix(i):
        return matrix_ref[:, edges[i] : edges[i + 1]]

    def turn(group, n):
        return turn_ref[group * STEP + n, 0], turn_ref[group * STEP + n, 1]

    def forward_outer(group, carry):
        for n in range(0, STEP, WIDE):
            b = group * STEP + n
            data = jnp.concatenate(
                [
                    stacked(x_s[pl.ds(pl.multiple_of((b + j) * outer, outer), outer), :])
                    for j in range(WIDE)
                ],
                axis=1,
            )
            both = jnp.dot(matrix(0), data, preferred_element_type=F32)
            for j in range(WIDE):
                re = both[:outer, LANES * j : LANES * (j + 1)]
                im = both[outer:, LANES * j : LANES * (j + 1)]
                cos, sin = turn(group, n + j)
                z_s[pl.ds(b + j, outer, stride=2 * INNER), :] = re * cos + im * sin
                z_s[pl.ds(b + j + INNER, outer, stride=2 * INNER), :] = im * cos - re * sin
        return carry

    lax.fori_loop(0, INNER // STEP, forward_outer, 0)

    def middle(group, carry):
        for n in range(0, STEP, WIDE):
            c = group * STEP + n
            data = jnp.concatenate(
                [
                    stacked(z_s[pl.ds(pl.multiple_of((c + j) * 2 * INNER, 2 * INNER), 2 * INNER), :])
                    for j in range(WIDE)
                ],
                axis=1,
            )
            both = jnp.dot(matrix(2), data, preferred_element_type=F32)
            mixed = []
            for j in range(WIDE):
                re = both[:INNER, LANES * j : LANES * (j + 1)]
                im = both[INNER:, LANES * j : LANES * (j + 1)]
                re_2, im_2 = swap_halves(re), swap_halves(im)
                mixed.append(
                    stacked(jnp.where(low, re * re_2 - im * im_2, re * im_2 + im * re_2))
                )
            both = jnp.dot(matrix(3), jnp.concatenate(mixed, axis=1), preferred_element_type=F32)
            for j in range(WIDE):
                straight = both[:INNER, LANES * j : LANES * (j + 1)]
                crossed = swap_halves(both[INNER:, LANES * j : LANES * (j + 1)])
                w_s[pl.ds(c + j, INNER, stride=outer), :] = jnp.where(
                    low, straight - crossed, straight + crossed
                )
        return carry

    lax.fori_loop(0, outer // STEP, middle, 0)

    def back_outer(group, carry):
        for n in range(0, STEP, WIDE):
            b = group * STEP + n
            data = []
            for j in range(WIDE):
                value = w_s[pl.ds(pl.multiple_of((b + j) * outer, outer), outer), :]
                cos, sin = turn(group, n + j)
                other = swap_halves(value) * sin
                straight = value * cos
                data.append(stacked(jnp.where(lowc, straight - other, straight + other)))
            both = jnp.dot(matrix(1), jnp.concatenate(data, axis=1), preferred_element_type=F32)
            for j in range(WIDE):
                re = both[:outer, LANES * j : LANES * (j + 1)]
                im = both[outer:, LANES * j : LANES * (j + 1)]
                y_s[pl.ds(b + j, outer, stride=INNER), :] = re + swap_halves(im)
        return carry

    lax.fori_loop(0, INNER // STEP, back_outer, 0)

    lowr = lower_half((rows, LANES))
    for n in range(parts):
        at = pl.multiple_of(origin(n) * 2 * rows, 2 * rows)
        early = y_s[pl.ds(at, rows), :]
        late = y_s[pl.ds(at + rows, rows), :]
        out_ref[n] = jnp.where(lowr, early, swap_halves(late)) + skip_ref[...] * p_s[n]


def gate_kernel(parts, index_ref, y_ref, q_ref, *outs):
    for n, out in enumerate(outs):
        q = q_ref[lax.rem(index_ref[0] + parts - n, parts)]
        out[...] = (q.astype(F32) * y_ref[n]).astype(BF16)


def joint_shift(value, segment_step, ctx_step):
    segments, parts = lax.axis_size("segment"), lax.axis_size("ctx")
    pairs = [
        (s * parts + c, (s + segment_step) % segments * parts + (c + ctx_step) % parts)
        for s in range(segments)
        for c in range(parts)
    ]
    return lax.ppermute(value, ("segment", "ctx"), pairs)


def fast_on_device(query_stream, key_stream, value_stream, filter_taps, skip_weight):
    parts = lax.axis_size("ctx")
    device = lax.axis_index("ctx")
    length, channels = query_stream.shape[1:]
    rows = length // 2
    outer = parts * length // INNER
    index = jnp.full((1,), device, jnp.int32)
    scalar = pl.BlockSpec(memory_space=pltpu.SMEM)
    whole = pl.BlockSpec(memory_space=pltpu.VMEM)
    far = pl.BlockSpec(memory_space=pltpu.HBM)
    small = pltpu.CompilerParams(vmem_limit_bytes=24 * 2**20)
    large = pltpu.CompilerParams(vmem_limit_bytes=60 * 2**20)

    def block(*shape, dtype=BF16):
        return jax.ShapeDtypeStruct(shape, dtype)

    size = 2 * rows + EXTRA
    sent = pl.pallas_call(
        functools.partial(pack_kernel, parts),
        out_shape=(block(size, LANES),) * parts,
        in_specs=[scalar] + [far] * 3,
        scratch_shapes=[pltpu.VMEM((parts, size, LANES), BF16)]
        + [pltpu.VMEM((length, channels), BF16)] * 3
        + [pltpu.SemaphoreType.DMA((3,))],
        compiler_params=large,
    )(index, key_stream[0], value_stream[0], filter_taps[0])
    slabs = [sent[0]] + [joint_shift(sent[n], 0, n) for n in range(1, parts)]
    q = pl.pallas_call(
        functools.partial(pack_gate_kernel, parts),
        out_shape=block(parts, rows, LANES),
        compiler_params=large,
    )(query_stream[0])
    q, *_ = lax.optimization_barrier((q, *slabs))
    q = lax.all_to_all(q, "ctx", split_axis=0, concat_axis=0, tiled=True)
    skip = lax.dynamic_slice(skip_weight, (0, device * HALF), (1, HALF))
    consts = [jnp.asarray(t) for t in tables(outer)]
    y = pl.pallas_call(
        functools.partial(convolve_kernel, parts, outer),
        out_shape=block(parts, rows, LANES, dtype=F32),
        in_specs=[scalar] + [whole] * (parts + 1) + [far] * len(consts),
        scratch_shapes=[
            pltpu.VMEM((outer * INNER, LANES), F32),
            pltpu.VMEM((2 * outer * INNER, LANES), F32),
            pltpu.VMEM((outer * INNER, LANES), F32),
            pltpu.VMEM((outer * INNER, LANES), F32),
            pltpu.VMEM((parts, rows, LANES), F32),
        ]
        + [pltpu.VMEM(t.shape, t.dtype) for t in consts]
        + [pltpu.SemaphoreType.DMA((len(consts),))],
        compiler_params=large,
    )(index, *slabs, jnp.concatenate([skip, skip], axis=1), *consts)
    gated = pl.pallas_call(
        functools.partial(gate_kernel, parts),
        out_shape=(block(rows, LANES),) * parts,
        in_specs=[scalar, whole, whole],
        compiler_params=small,
    )(index, y, q)
    gated = [joint_shift(gated[n], 1, -n) for n in range(parts)]
    out = pl.pallas_call(
        functools.partial(unpack_kernel, parts),
        out_shape=block(length, channels),
        in_specs=[scalar] + [whole] * parts,
        scratch_shapes=[pltpu.VMEM((parts, rows, LANES), BF16)],
        compiler_params=small,
    )(index, *gated)
    return out[None]


def solution(mesh):
    placed = (
        P("segment", "ctx", None),
        P("segment", "ctx", None),
        P("segment", "ctx", None),
        P("segment", "ctx", None),
        P("segment", None),
    )

    def on_device(*arrays):
        parts = lax.axis_size("ctx")
        length, channels = arrays[0].shape[1:]
        square = parts * length == INNER * INNER
        run = fast_on_device if square and channels == parts * HALF else general_on_device
        return run(*arrays)

    return jax.shard_map(
        on_device, mesh=mesh, in_specs=placed, out_specs=P("segment", "ctx", None), check_vma=False
    )
```

```python
import functools
import math

import jax
import jax.numpy as jnp
import numpy as np
from jax import lax
from jax.experimental import pallas as pl
from jax.experimental.pallas import tpu as pltpu
from jax.sharding import PartitionSpec as P

HIGHEST = lax.Precision.HIGHEST
LANES = 128
HALF = 64
INNER = 64
STEP = 16
EXTRA = 16
DOUBLINGS = 4
SCALE = 215.0
SMALLEST = 1e-30
LIMIT = 30
WIDE = 16
F32 = jnp.float32
BF16 = jnp.bfloat16


def from_behind(value, axis, steps):
    count = lax.axis_size(axis)
    pairs = [(source, (source + steps) % count) for source in range(count)]
    return lax.ppermute(value, axis, pairs)


def angles(modulus, left, right):
    phase = left[:, None] * right[None, :] % modulus
    theta = phase.astype(jnp.float32) * (2.0 * math.pi / modulus)
    return (jnp.cos(theta), jnp.sin(theta))


def frequency_order(width):
    rows = jnp.arange(2 * width, dtype=jnp.int32)
    halves = rows // 2
    return jnp.where(rows % 2 == 0, halves, jnp.where(halves == 0, width, 2 * width - halves))


def across(table, data):
    return jnp.einsum("rd,dsc->rsc", table, data, precision=HIGHEST)


def along(table, data):
    return jnp.einsum("kb,rbc->rkc", table, data, precision=HIGHEST)


def rotate(real_part, imag_part, cosine, sine):
    return (real_part * cosine + imag_part * sine, imag_part * cosine - real_part * sine)


def general_on_device(query_stream, key_stream, value_stream, filter_taps, skip_weight):
    parts = lax.axis_size("ctx")
    device = lax.axis_index("ctx")
    length = query_stream.shape[1]
    channels = query_stream.shape[2]
    share = length // parts
    total = 2 * parts * length
    product = key_stream[0].astype(jnp.float32) * value_stream[0].astype(jnp.float32)
    taps = filter_taps[0].astype(jnp.float32)
    block_prod, block_taps = (
        lax.all_to_all(
            product.reshape(1, length, channels), "ctx", split_axis=1, concat_axis=0, tiled=True
        ),
        lax.all_to_all(
            taps.reshape(1, length, channels), "ctx", split_axis=1, concat_axis=0, tiled=True
        ),
    )
    order = frequency_order(parts)
    cos_cross, sin_cross = angles(2 * parts, order, jnp.arange(parts, dtype=jnp.int32))
    positions = device * share + jnp.arange(share, dtype=jnp.int32)
    cos_twist, sin_twist = angles(total, order, positions)
    cos_twist = cos_twist[:, :, None]
    sin_twist = sin_twist[:, :, None]
    span = jnp.arange(length, dtype=jnp.int32)
    cos_along, sin_along = angles(length, span, span)
    local_rows = lax.dynamic_slice(order, (2 * device,), (2,))
    cos_back, sin_back = angles(total, local_rows, span)
    cos_back = cos_back[:, :, None]
    sin_back = sin_back[:, :, None]

    def forward_along(real_part, imag_part):
        return (
            along(cos_along, real_part) + along(sin_along, imag_part),
            along(cos_along, imag_part) - along(sin_along, real_part),
        )

    prod_real, prod_imag = rotate(
        across(cos_cross, block_prod), -across(sin_cross, block_prod), cos_twist, sin_twist
    )
    taps_real, taps_imag = rotate(
        across(cos_cross, block_taps), -across(sin_cross, block_taps), cos_twist, sin_twist
    )
    first_real, first_imag = forward_along(
        lax.all_to_all(prod_real, "ctx", split_axis=0, concat_axis=1, tiled=True),
        lax.all_to_all(prod_imag, "ctx", split_axis=0, concat_axis=1, tiled=True),
    )
    second_real, second_imag = forward_along(
        lax.all_to_all(taps_real, "ctx", split_axis=0, concat_axis=1, tiled=True),
        lax.all_to_all(taps_imag, "ctx", split_axis=0, concat_axis=1, tiled=True),
    )
    result_real = first_real * second_real - first_imag * second_imag
    result_imag = first_real * second_imag + first_imag * second_real
    back_real = along(cos_along, result_real) - along(sin_along, result_imag)
    back_imag = along(cos_along, result_imag) + along(sin_along, result_real)
    spec_real, spec_imag = rotate(back_real, back_imag, cos_back, -sin_back)
    rows_real, rows_imag = (
        lax.all_to_all(spec_real, "ctx", split_axis=1, concat_axis=0, tiled=True),
        lax.all_to_all(spec_imag, "ctx", split_axis=1, concat_axis=0, tiled=True),
    )
    cos_final, sin_final = angles(2 * parts, jnp.arange(parts, dtype=jnp.int32), order)
    by_block = jnp.einsum("dr,rsc->dsc", cos_final, rows_real, precision=HIGHEST) - jnp.einsum(
        "dr,rsc->dsc", sin_final, rows_imag, precision=HIGHEST
    )
    by_block = by_block * (1.0 / total)
    convolved = lax.all_to_all(by_block, "ctx", split_axis=0, concat_axis=1, tiled=True)[0]
    gated = query_stream[0].astype(jnp.float32) * (convolved + skip_weight[0][None, :] * product)
    gated = gated.astype(jnp.bfloat16)[None]
    return from_behind(gated, "segment", 1)


def split_two(value):
    high = value.astype(BF16)
    return high, (value - high.astype(F32)).astype(BF16)


def split_table(table):
    table = table.astype(np.float32)
    high = table.astype(jnp.bfloat16)
    low = (table - high.astype(np.float32)).astype(jnp.bfloat16)
    return np.concatenate([high, high, low], axis=1)


def stacked(value):
    high, low = split_two(value)
    return jnp.concatenate([high, low, high], axis=0)


def lower_half(shape):
    return lax.broadcasted_iota(jnp.int32, shape, len(shape) - 1) < HALF


def swap_halves(value):
    return pltpu.roll(value, HALF, value.ndim - 1)


def tables(outer):
    total = outer * INNER
    a = np.arange(outer)
    b = np.arange(INNER)
    c = np.arange(outer) + 0.25
    first = 2.0 * np.pi * np.outer(c, a) / outer
    second = 2.0 * np.pi * np.outer(b, b) / INNER
    forward_a = split_table(np.concatenate([np.cos(first), -np.sin(first)], axis=0))
    forward_b = split_table(
        np.block([[np.cos(second), np.sin(second)], [-np.sin(second), np.cos(second)]])
    )
    back_b = split_table(np.concatenate([np.cos(second), np.sin(second)], axis=0))
    back_a = split_table(np.concatenate([np.cos(first).T, -np.sin(first).T], axis=0) / total)

    def turns(steps):
        theta = 2.0 * np.pi * np.outer(steps, c) / total
        wide = np.stack([np.cos(theta), np.sin(theta)], axis=1).astype(np.float32)
        return np.ascontiguousarray(np.broadcast_to(wide[..., None], wide.shape + (LANES,)))

    return forward_a, forward_b, back_b, back_a, turns(b)


def fetched(sources, targets, sems):
    copies = [pltpu.make_async_copy(a, b, sems.at[i]) for i, (a, b) in enumerate(zip(sources, targets))]
    for copy in copies:
        copy.start()
    return copies


def pack_kernel(parts, index_ref, *refs):
    sources, outs, held, arrived, sems = refs[:3], refs[3 : 3 + parts], refs[-5], refs[-4:-1], refs[-1]
    k_ref, v_ref, h_ref = arrived
    rows = k_ref.shape[0] // 2
    low = lower_half((rows, LANES))
    for copy in fetched(sources, arrived, sems):
        copy.wait()

    def place(e, at, tile, low):
        half = tile.shape[0] // 2
        early, late = tile[:half], tile[half:]
        held[2 * e, at : at + half, :] = jnp.where(low, early, swap_halves(late)).astype(BF16)
        held[2 * e + 1, at : at + half, :] = jnp.where(low, swap_halves(early), late).astype(BF16)

    for e in range(parts // 2):
        lanes = slice(LANES * e, LANES * (e + 1))
        product = k_ref[:, lanes].astype(F32) * v_ref[:, lanes].astype(F32)
        largest = jnp.max(jnp.abs(product), axis=0, keepdims=True)
        largest = jnp.maximum(largest * 1.01, SMALLEST).astype(BF16).astype(F32)
        code = product * (SCALE / largest)
        power = code * code
        for _ in range(DOUBLINGS - 1):
            power = power * power
        place(e, 0, jnp.where(code < 0.0, -power, power), low)
        place(e, rows, h_ref[:, lanes].astype(F32), low)
        place(e, 2 * rows, jnp.broadcast_to(largest, (2 * EXTRA, LANES)), low[:EXTRA])
    for n, out in enumerate(outs):
        out[...] = held[lax.rem(index_ref[0] + n, parts)]


def pack_gate_kernel(parts, q_ref, out_ref):
    rows = q_ref.shape[0] // 2
    low = lower_half((rows, LANES))
    for e in range(parts // 2):
        tile = q_ref[:, LANES * e : LANES * (e + 1)].astype(F32)
        early, late = tile[:rows], tile[rows:]
        out_ref[2 * e] = jnp.where(low, early, swap_halves(late)).astype(BF16)
        out_ref[2 * e + 1] = jnp.where(low, swap_halves(early), late).astype(BF16)


def unpack_kernel(parts, index_ref, *refs):
    blocks, out_ref, held = refs[:parts], refs[parts], refs[parts + 1]
    rows = held.shape[1]
    low = lower_half((rows, LANES))
    for n, block in enumerate(blocks):
        held[lax.rem(index_ref[0] + n, parts)] = block[...]
    for e in range(parts // 2):
        even, odd = held[2 * e].astype(F32), held[2 * e + 1].astype(F32)
        out_ref[:rows, LANES * e : LANES * (e + 1)] = jnp.where(low, even, swap_halves(odd)).astype(BF16)
        out_ref[rows:, LANES * e : LANES * (e + 1)] = jnp.where(low, swap_halves(even), odd).astype(BF16)


def forward_kernel(parts, outer, index_ref, *refs):
    blocks = refs[:parts]
    matrix_ref, turn_ref, z_s, p_s, x_s = refs[parts:]
    rows = p_s.shape[1]
    per = rows // INNER
    low = lower_half((INNER, LANES))

    def origin(n):
        return lax.rem(index_ref[0] + parts - n, parts)

    for n, block in enumerate(blocks):
        scale = block[2 * rows : 2 * rows + EXTRA, :].astype(F32)[:1] * (1.0 / SCALE)
        for m in range(per):
            at = m * INNER
            code = block[at : at + INNER, :].astype(F32)
            size = jnp.exp(jnp.log(jnp.abs(code)) * (0.5**DOUBLINGS)) * scale
            p = jnp.where(code == 0.0, 0.0, jnp.where(code < 0.0, -size, size))
            p_s[n, at : at + INNER, :] = p
            h = block[rows + at : rows + at + INNER, :].astype(F32)
            a = origin(n) * (2 * per) + m
            x_s[pl.ds(a, INNER, stride=outer), :] = jnp.where(low, p, swap_halves(h))
            x_s[pl.ds(a + per, INNER, stride=outer), :] = jnp.where(low, swap_halves(p), h)

    def turn(group, n):
        return turn_ref[group * STEP + n, 0], turn_ref[group * STEP + n, 1]

    def forward_outer(group, carry):
        for n in range(0, STEP, WIDE):
            b = group * STEP + n
            data = jnp.concatenate(
                [
                    stacked(x_s[pl.ds(pl.multiple_of((b + j) * outer, outer), outer), :])
                    for j in range(WIDE)
                ],
                axis=1,
            )
            both = jnp.dot(matrix_ref[...], data, preferred_element_type=F32)
            for j in range(WIDE):
                re = both[:outer, LANES * j : LANES * (j + 1)]
                im = both[outer:, LANES * j : LANES * (j + 1)]
                cos, sin = turn(group, n + j)
                z_s[pl.ds(b + j, outer, stride=2 * INNER), :] = re * cos + im * sin
                z_s[pl.ds(b + j + INNER, outer, stride=2 * INNER), :] = im * cos - re * sin
        return carry

    lax.fori_loop(0, INNER // STEP, forward_outer, 0)


def middle_kernel(outer, z_s, forward_ref, back_ref, w_s):
    low = lower_half((INNER, LANES))

    def middle(group, carry):
        for n in range(0, STEP, WIDE):
            c = group * STEP + n
            data = jnp.concatenate(
                [
                    stacked(z_s[pl.ds(pl.multiple_of((c + j) * 2 * INNER, 2 * INNER), 2 * INNER), :])
                    for j in range(WIDE)
                ],
                axis=1,
            )
            both = jnp.dot(forward_ref[...], data, preferred_element_type=F32)
            mixed = []
            for j in range(WIDE):
                re = both[:INNER, LANES * j : LANES * (j + 1)]
                im = both[INNER:, LANES * j : LANES * (j + 1)]
                re_2, im_2 = swap_halves(re), swap_halves(im)
                mixed.append(
                    stacked(jnp.where(low, re * re_2 - im * im_2, re * im_2 + im * re_2))
                )
            both = jnp.dot(back_ref[...], jnp.concatenate(mixed, axis=1), preferred_element_type=F32)
            for j in range(WIDE):
                straight = both[:INNER, LANES * j : LANES * (j + 1)]
                crossed = swap_halves(both[INNER:, LANES * j : LANES * (j + 1)])
                w_s[pl.ds(c + j, INNER, stride=outer), :] = jnp.where(
                    low, straight - crossed, straight + crossed
                )
        return carry

    lax.fori_loop(0, outer // STEP, middle, 0)


def back_kernel(parts, outer, index_ref, skip_ref, w_s, p_s, *refs):
    matrix_ref, turn_ref, out_ref, y_s = refs
    rows = out_ref.shape[1]
    lowc = lower_half((outer, LANES))

    def origin(n):
        return lax.rem(index_ref[0] + parts - n, parts)

    def turn(group, n):
        return turn_ref[group * STEP + n, 0], turn_ref[group * STEP + n, 1]

    def back_outer(group, carry):
        for n in range(0, STEP, WIDE):
            b = group * STEP + n
            data = []
            for j in range(WIDE):
                value = w_s[pl.ds(pl.multiple_of((b + j) * outer, outer), outer), :]
                cos, sin = turn(group, n + j)
                other = swap_halves(value) * sin
                straight = value * cos
                data.append(stacked(jnp.where(lowc, straight - other, straight + other)))
            both = jnp.dot(matrix_ref[...], jnp.concatenate(data, axis=1), preferred_element_type=F32)
            for j in range(WIDE):
                re = both[:outer, LANES * j : LANES * (j + 1)]
                im = both[outer:, LANES * j : LANES * (j + 1)]
                y_s[pl.ds(b + j, outer, stride=INNER), :] = re + swap_halves(im)
        return carry

    lax.fori_loop(0, INNER // STEP, back_outer, 0)

    lowr = lower_half((rows, LANES))
    pair = pl.multiple_of(index_ref[0] // 2 * LANES, LANES)
    wide = skip_ref[:, pl.ds(pair, LANES)]
    mine = lower_half((1, LANES)) == (index_ref[0] % 2 == 0)
    skip = jnp.where(mine, wide, swap_halves(wide))
    for n in range(parts):
        at = pl.multiple_of(origin(n) * 2 * rows, 2 * rows)
        early = y_s[pl.ds(at, rows), :]
        late = y_s[pl.ds(at + rows, rows), :]
        out_ref[n] = jnp.where(lowr, early, swap_halves(late)) + skip * p_s[n]


def gate_kernel(parts, index_ref, y_ref, q_ref, *outs):
    for n, out in enumerate(outs):
        q = q_ref[lax.rem(index_ref[0] + parts - n, parts)]
        out[...] = (q.astype(F32) * y_ref[n]).astype(BF16)


def joint_shift(value, segment_step, ctx_step):
    segments, parts = lax.axis_size("segment"), lax.axis_size("ctx")
    pairs = [
        (s * parts + c, (s + segment_step) % segments * parts + (c + ctx_step) % parts)
        for s in range(segments)
        for c in range(parts)
    ]
    return lax.ppermute(value, ("segment", "ctx"), pairs)


def convolved(parts, length, index, slabs, skip_weight):
    rows = length // 2
    outer = parts * length // INNER
    forward_a, forward_b, back_b, back_a, turns = [jnp.asarray(t) for t in tables(outer)]
    scalar = pl.BlockSpec(memory_space=pltpu.SMEM)
    whole = pl.BlockSpec(memory_space=pltpu.VMEM)

    def block(*shape):
        return jax.ShapeDtypeStruct(shape, F32)

    z, p = pl.pallas_call(
        functools.partial(forward_kernel, parts, outer),
        out_shape=(block(2 * outer * INNER, LANES), block(parts, rows, LANES)),
        in_specs=[scalar] + [whole] * (parts + 2),
        scratch_shapes=[pltpu.VMEM((outer * INNER, LANES), F32)],
        compiler_params=pltpu.CompilerParams(vmem_limit_bytes=LIMIT * 2**20),
    )(index, *slabs, forward_a, turns)
    w = pl.pallas_call(
        functools.partial(middle_kernel, outer),
        out_shape=block(outer * INNER, LANES),
        compiler_params=pltpu.CompilerParams(vmem_limit_bytes=LIMIT * 2**20),
    )(z, forward_b, back_b)
    return pl.pallas_call(
        functools.partial(back_kernel, parts, outer),
        out_shape=block(parts, rows, LANES),
        in_specs=[scalar] + [whole] * 5,
        scratch_shapes=[pltpu.VMEM((outer * INNER, LANES), F32)],
        compiler_params=pltpu.CompilerParams(vmem_limit_bytes=LIMIT * 2**20),
    )(index, skip_weight, w, p, back_a, turns)


def fast_on_device(query_stream, key_stream, value_stream, filter_taps, skip_weight):
    parts = lax.axis_size("ctx")
    device = lax.axis_index("ctx")
    length, channels = query_stream.shape[1:]
    rows = length // 2
    index = jnp.full((1,), device, jnp.int32)
    scalar = pl.BlockSpec(memory_space=pltpu.SMEM)
    whole = pl.BlockSpec(memory_space=pltpu.VMEM)
    far = pl.BlockSpec(memory_space=pltpu.HBM)
    small = pltpu.CompilerParams(vmem_limit_bytes=24 * 2**20)
    large = pltpu.CompilerParams(vmem_limit_bytes=60 * 2**20)

    def block(*shape, dtype=BF16):
        return jax.ShapeDtypeStruct(shape, dtype)

    size = 2 * rows + EXTRA
    sent = pl.pallas_call(
        functools.partial(pack_kernel, parts),
        out_shape=(block(size, LANES),) * parts,
        in_specs=[scalar] + [far] * 3,
        scratch_shapes=[pltpu.VMEM((parts, size, LANES), BF16)]
        + [pltpu.VMEM((length, channels), BF16)] * 3
        + [pltpu.SemaphoreType.DMA((3,))],
        compiler_params=large,
    )(index, key_stream[0], value_stream[0], filter_taps[0])
    slabs = [sent[0]] + [joint_shift(sent[n], 0, n) for n in range(1, parts)]
    q = pl.pallas_call(
        functools.partial(pack_gate_kernel, parts),
        out_shape=block(parts, rows, LANES),
        compiler_params=large,
    )(query_stream[0])
    q, *_ = lax.optimization_barrier((q, *slabs[: parts - 0]))
    q = lax.all_to_all(q, "ctx", split_axis=0, concat_axis=0, tiled=True)
    y = convolved(parts, length, index, slabs, skip_weight)
    gated = pl.pallas_call(
        functools.partial(gate_kernel, parts),
        out_shape=(block(rows, LANES),) * parts,
        in_specs=[scalar, whole, whole],
        compiler_params=small,
    )(index, y, q)
    gated = [joint_shift(gated[n], 1, -n) for n in range(parts)]
    out = pl.pallas_call(
        functools.partial(unpack_kernel, parts),
        out_shape=block(length, channels),
        in_specs=[scalar] + [whole] * parts,
        scratch_shapes=[pltpu.VMEM((parts, rows, LANES), BF16)],
        compiler_params=small,
    )(index, *gated)
    return out[None]


def solution(mesh):
    placed = (
        P("segment", "ctx", None),
        P("segment", "ctx", None),
        P("segment", "ctx", None),
        P("segment", "ctx", None),
        P("segment", None),
    )

    def on_device(*arrays):
        parts = lax.axis_size("ctx")
        length, channels = arrays[0].shape[1:]
        square = parts * length == INNER * INNER
        run = fast_on_device if square and channels == parts * HALF else general_on_device
        return run(*arrays)

    return jax.shard_map(
        on_device, mesh=mesh, in_specs=placed, out_specs=P("segment", "ctx", None), check_vma=False
    )
```

```python
import functools
import math

import jax
import jax.numpy as jnp
import numpy as np
from jax import lax
from jax.experimental import pallas as pl
from jax.experimental.pallas import tpu as pltpu
from jax.sharding import PartitionSpec as P

HIGHEST = lax.Precision.HIGHEST
LANES = 128
HALF = 64
INNER = 64
STEP = 16
EXTRA = 16
DOUBLINGS = 4
SCALE = 215.0
SMALLEST = 1e-30
LIMIT = 30
WIDE = 16
F32 = jnp.float32
BF16 = jnp.bfloat16


def from_behind(value, axis, steps):
    count = lax.axis_size(axis)
    pairs = [(source, (source + steps) % count) for source in range(count)]
    return lax.ppermute(value, axis, pairs)


def angles(modulus, left, right):
    phase = left[:, None] * right[None, :] % modulus
    theta = phase.astype(jnp.float32) * (2.0 * math.pi / modulus)
    return (jnp.cos(theta), jnp.sin(theta))


def frequency_order(width):
    rows = jnp.arange(2 * width, dtype=jnp.int32)
    halves = rows // 2
    return jnp.where(rows % 2 == 0, halves, jnp.where(halves == 0, width, 2 * width - halves))


def across(table, data):
    return jnp.einsum("rd,dsc->rsc", table, data, precision=HIGHEST)


def along(table, data):
    return jnp.einsum("kb,rbc->rkc", table, data, precision=HIGHEST)


def rotate(real_part, imag_part, cosine, sine):
    return (real_part * cosine + imag_part * sine, imag_part * cosine - real_part * sine)


def general_on_device(query_stream, key_stream, value_stream, filter_taps, skip_weight):
    parts = lax.axis_size("ctx")
    device = lax.axis_index("ctx")
    length = query_stream.shape[1]
    channels = query_stream.shape[2]
    share = length // parts
    total = 2 * parts * length
    product = key_stream[0].astype(jnp.float32) * value_stream[0].astype(jnp.float32)
    taps = filter_taps[0].astype(jnp.float32)
    block_prod, block_taps = (
        lax.all_to_all(
            product.reshape(1, length, channels), "ctx", split_axis=1, concat_axis=0, tiled=True
        ),
        lax.all_to_all(
            taps.reshape(1, length, channels), "ctx", split_axis=1, concat_axis=0, tiled=True
        ),
    )
    order = frequency_order(parts)
    cos_cross, sin_cross = angles(2 * parts, order, jnp.arange(parts, dtype=jnp.int32))
    positions = device * share + jnp.arange(share, dtype=jnp.int32)
    cos_twist, sin_twist = angles(total, order, positions)
    cos_twist = cos_twist[:, :, None]
    sin_twist = sin_twist[:, :, None]
    span = jnp.arange(length, dtype=jnp.int32)
    cos_along, sin_along = angles(length, span, span)
    local_rows = lax.dynamic_slice(order, (2 * device,), (2,))
    cos_back, sin_back = angles(total, local_rows, span)
    cos_back = cos_back[:, :, None]
    sin_back = sin_back[:, :, None]

    def forward_along(real_part, imag_part):
        return (
            along(cos_along, real_part) + along(sin_along, imag_part),
            along(cos_along, imag_part) - along(sin_along, real_part),
        )

    prod_real, prod_imag = rotate(
        across(cos_cross, block_prod), -across(sin_cross, block_prod), cos_twist, sin_twist
    )
    taps_real, taps_imag = rotate(
        across(cos_cross, block_taps), -across(sin_cross, block_taps), cos_twist, sin_twist
    )
    first_real, first_imag = forward_along(
        lax.all_to_all(prod_real, "ctx", split_axis=0, concat_axis=1, tiled=True),
        lax.all_to_all(prod_imag, "ctx", split_axis=0, concat_axis=1, tiled=True),
    )
    second_real, second_imag = forward_along(
        lax.all_to_all(taps_real, "ctx", split_axis=0, concat_axis=1, tiled=True),
        lax.all_to_all(taps_imag, "ctx", split_axis=0, concat_axis=1, tiled=True),
    )
    result_real = first_real * second_real - first_imag * second_imag
    result_imag = first_real * second_imag + first_imag * second_real
    back_real = along(cos_along, result_real) - along(sin_along, result_imag)
    back_imag = along(cos_along, result_imag) + along(sin_along, result_real)
    spec_real, spec_imag = rotate(back_real, back_imag, cos_back, -sin_back)
    rows_real, rows_imag = (
        lax.all_to_all(spec_real, "ctx", split_axis=1, concat_axis=0, tiled=True),
        lax.all_to_all(spec_imag, "ctx", split_axis=1, concat_axis=0, tiled=True),
    )
    cos_final, sin_final = angles(2 * parts, jnp.arange(parts, dtype=jnp.int32), order)
    by_block = jnp.einsum("dr,rsc->dsc", cos_final, rows_real, precision=HIGHEST) - jnp.einsum(
        "dr,rsc->dsc", sin_final, rows_imag, precision=HIGHEST
    )
    by_block = by_block * (1.0 / total)
    convolved = lax.all_to_all(by_block, "ctx", split_axis=0, concat_axis=1, tiled=True)[0]
    gated = query_stream[0].astype(jnp.float32) * (convolved + skip_weight[0][None, :] * product)
    gated = gated.astype(jnp.bfloat16)[None]
    return from_behind(gated, "segment", 1)


def split_two(value):
    high = value.astype(BF16)
    return high, (value - high.astype(F32)).astype(BF16)


def split_table(table):
    table = table.astype(np.float32)
    high = table.astype(jnp.bfloat16)
    low = (table - high.astype(np.float32)).astype(jnp.bfloat16)
    return np.concatenate([high, high, low], axis=1)


def stacked(value):
    high, low = split_two(value)
    return jnp.concatenate([high, low, high], axis=0)


def lower_half(shape):
    return lax.broadcasted_iota(jnp.int32, shape, len(shape) - 1) < HALF


def swap_halves(value):
    return pltpu.roll(value, HALF, value.ndim - 1)


def tables(outer):
    total = outer * INNER
    a = np.arange(outer)
    b = np.arange(INNER)
    c = np.arange(outer) + 0.25
    first = 2.0 * np.pi * np.outer(c, a) / outer
    second = 2.0 * np.pi * np.outer(b, b) / INNER
    forward_a = split_table(np.concatenate([np.cos(first), -np.sin(first)], axis=0))
    forward_b = split_table(
        np.block([[np.cos(second), np.sin(second)], [-np.sin(second), np.cos(second)]])
    )
    back_b = split_table(np.concatenate([np.cos(second), np.sin(second)], axis=0))
    back_a = split_table(np.concatenate([np.cos(first).T, -np.sin(first).T], axis=0) / total)

    def turns(steps):
        theta = 2.0 * np.pi * np.outer(steps, c) / total
        wide = np.stack([np.cos(theta), np.sin(theta)], axis=1).astype(np.float32)
        return np.ascontiguousarray(np.broadcast_to(wide[..., None], wide.shape + (LANES,)))

    return forward_a, forward_b, back_b, back_a, turns(b), turns(np.concatenate([b[:STEP], b[::STEP]]))


def fetched(sources, targets, sems):
    copies = [pltpu.make_async_copy(a, b, sems.at[i]) for i, (a, b) in enumerate(zip(sources, targets))]
    for copy in copies:
        copy.start()
    return copies


def pack_kernel(parts, index_ref, *refs):
    sources, outs, held, arrived, sems = refs[:3], refs[3 : 3 + parts], refs[-5], refs[-4:-1], refs[-1]
    k_ref, v_ref, h_ref = arrived
    rows = k_ref.shape[0] // 2
    low = lower_half((rows, LANES))
    for copy in fetched(sources, arrived, sems):
        copy.wait()

    def place(e, at, tile, low):
        half = tile.shape[0] // 2
        early, late = tile[:half], tile[half:]
        held[2 * e, at : at + half, :] = jnp.where(low, early, swap_halves(late)).astype(BF16)
        held[2 * e + 1, at : at + half, :] = jnp.where(low, swap_halves(early), late).astype(BF16)

    for e in range(parts // 2):
        lanes = slice(LANES * e, LANES * (e + 1))
        product = k_ref[:, lanes].astype(F32) * v_ref[:, lanes].astype(F32)
        largest = jnp.max(jnp.abs(product), axis=0, keepdims=True)
        largest = jnp.maximum(largest * 1.01, SMALLEST).astype(BF16).astype(F32)
        code = product * (SCALE / largest)
        power = code * code
        for _ in range(DOUBLINGS - 1):
            power = power * power
        place(e, 0, jnp.where(code < 0.0, -power, power), low)
        place(e, rows, h_ref[:, lanes].astype(F32), low)
        place(e, 2 * rows, jnp.broadcast_to(largest, (2 * EXTRA, LANES)), low[:EXTRA])
    for n, out in enumerate(outs):
        out[...] = held[lax.rem(index_ref[0] + n, parts)]


def pack_gate_kernel(parts, q_ref, out_ref):
    rows = q_ref.shape[0] // 2
    low = lower_half((rows, LANES))
    for e in range(parts // 2):
        tile = q_ref[:, LANES * e : LANES * (e + 1)].astype(F32)
        early, late = tile[:rows], tile[rows:]
        out_ref[2 * e] = jnp.where(low, early, swap_halves(late)).astype(BF16)
        out_ref[2 * e + 1] = jnp.where(low, swap_halves(early), late).astype(BF16)


def hold_kernel(*refs):
    half = len(refs) // 2
    for source, target in zip(refs[:half], refs[half:]):
        target[...] = source[...]


def unpack_kernel(parts, index_ref, *refs):
    blocks, out_ref, held = refs[:parts], refs[parts], refs[parts + 1]
    rows = held.shape[1]
    low = lower_half((rows, LANES))
    for n, block in enumerate(blocks):
        held[lax.rem(index_ref[0] + n, parts)] = block[...]
    for e in range(parts // 2):
        even, odd = held[2 * e].astype(F32), held[2 * e + 1].astype(F32)
        out_ref[:rows, LANES * e : LANES * (e + 1)] = jnp.where(low, even, swap_halves(odd)).astype(BF16)
        out_ref[rows:, LANES * e : LANES * (e + 1)] = jnp.where(low, swap_halves(even), odd).astype(BF16)


def forward_kernel(parts, outer, index_ref, *refs):
    blocks = refs[:parts]
    matrix_ref, turn_ref, z_s, p_s, x_s = refs[parts:]
    rows = p_s.shape[1]
    per = rows // INNER
    low = lower_half((INNER, LANES))

    def origin(n):
        return lax.rem(index_ref[0] + parts - n, parts)

    for n, block in enumerate(blocks):
        scale = block[2 * rows : 2 * rows + EXTRA, :].astype(F32)[:1] * (1.0 / SCALE)
        for m in range(per):
            at = m * INNER
            code = block[at : at + INNER, :].astype(F32)
            size = jnp.exp(jnp.log(jnp.abs(code)) * (0.5**DOUBLINGS)) * scale
            p = jnp.where(code == 0.0, 0.0, jnp.where(code < 0.0, -size, size))
            p_s[n, at : at + INNER, :] = p
            h = block[rows + at : rows + at + INNER, :].astype(F32)
            a = origin(n) * (2 * per) + m
            x_s[pl.ds(a, INNER, stride=outer), :] = jnp.where(low, p, swap_halves(h))
            x_s[pl.ds(a + per, INNER, stride=outer), :] = jnp.where(low, swap_halves(p), h)

    def turn(group, n):
        cos_1, sin_1 = turn_ref[STEP + group, 0], turn_ref[STEP + group, 1]
        if n == 0:
            return cos_1, sin_1
        cos_2, sin_2 = turn_ref[n, 0], turn_ref[n, 1]
        return cos_1 * cos_2 - sin_1 * sin_2, sin_1 * cos_2 + cos_1 * sin_2

    def forward_outer(group, carry):
        for n in range(0, STEP, WIDE):
            b = group * STEP + n
            data = jnp.concatenate(
                [
                    stacked(x_s[pl.ds(pl.multiple_of((b + j) * outer, outer), outer), :])
                    for j in range(WIDE)
                ],
                axis=1,
            )
            both = jnp.dot(matrix_ref[...], data, preferred_element_type=F32)
            for j in range(WIDE):
                re = both[:outer, LANES * j : LANES * (j + 1)]
                im = both[outer:, LANES * j : LANES * (j + 1)]
                cos, sin = turn(group, n + j)
                z_s[pl.ds(b + j, outer, stride=2 * INNER), :] = re * cos + im * sin
                z_s[pl.ds(b + j + INNER, outer, stride=2 * INNER), :] = im * cos - re * sin
        return carry

    lax.fori_loop(0, INNER // STEP, forward_outer, 0)


def middle_kernel(outer, z_s, forward_ref, back_ref, w_s):
    low = lower_half((INNER, LANES))

    def middle(group, carry):
        for n in range(0, STEP, WIDE):
            c = group * STEP + n
            data = jnp.concatenate(
                [
                    stacked(z_s[pl.ds(pl.multiple_of((c + j) * 2 * INNER, 2 * INNER), 2 * INNER), :])
                    for j in range(WIDE)
                ],
                axis=1,
            )
            both = jnp.dot(forward_ref[...], data, preferred_element_type=F32)
            mixed = []
            for j in range(WIDE):
                re = both[:INNER, LANES * j : LANES * (j + 1)]
                im = both[INNER:, LANES * j : LANES * (j + 1)]
                re_2, im_2 = swap_halves(re), swap_halves(im)
                mixed.append(
                    stacked(jnp.where(low, re * re_2 - im * im_2, re * im_2 + im * re_2))
                )
            both = jnp.dot(back_ref[...], jnp.concatenate(mixed, axis=1), preferred_element_type=F32)
            for j in range(WIDE):
                straight = both[:INNER, LANES * j : LANES * (j + 1)]
                crossed = swap_halves(both[INNER:, LANES * j : LANES * (j + 1)])
                w_s[pl.ds(c + j, INNER, stride=outer), :] = jnp.where(
                    low, straight - crossed, straight + crossed
                )
        return carry

    lax.fori_loop(0, outer // STEP, middle, 0)


def back_kernel(parts, outer, index_ref, skip_ref, w_s, p_s, *refs):
    matrix_ref, turn_ref, out_ref, y_s = refs
    rows = out_ref.shape[1]
    lowc = lower_half((outer, LANES))

    def origin(n):
        return lax.rem(index_ref[0] + parts - n, parts)

    def turn(group, n):
        return turn_ref[group * STEP + n, 0], turn_ref[group * STEP + n, 1]

    def back_outer(group, carry):
        for n in range(0, STEP, WIDE):
            b = group * STEP + n
            data = []
            for j in range(WIDE):
                value = w_s[pl.ds(pl.multiple_of((b + j) * outer, outer), outer), :]
                cos, sin = turn(group, n + j)
                other = swap_halves(value) * sin
                straight = value * cos
                data.append(stacked(jnp.where(lowc, straight - other, straight + other)))
            both = jnp.dot(matrix_ref[...], jnp.concatenate(data, axis=1), preferred_element_type=F32)
            for j in range(WIDE):
                re = both[:outer, LANES * j : LANES * (j + 1)]
                im = both[outer:, LANES * j : LANES * (j + 1)]
                y_s[pl.ds(b + j, outer, stride=INNER), :] = re + swap_halves(im)
        return carry

    lax.fori_loop(0, INNER // STEP, back_outer, 0)

    lowr = lower_half((rows, LANES))
    pair = pl.multiple_of(index_ref[0] // 2 * LANES, LANES)
    wide = skip_ref[:, pl.ds(pair, LANES)]
    mine = lower_half((1, LANES)) == (index_ref[0] % 2 == 0)
    skip = jnp.where(mine, wide, swap_halves(wide))
    for n in range(parts):
        at = pl.multiple_of(origin(n) * 2 * rows, 2 * rows)
        early = y_s[pl.ds(at, rows), :]
        late = y_s[pl.ds(at + rows, rows), :]
        out_ref[n] = jnp.where(lowr, early, swap_halves(late)) + skip * p_s[n]


def gate_kernel(parts, index_ref, y_ref, q_ref, *outs):
    for n, out in enumerate(outs):
        q = q_ref[lax.rem(index_ref[0] + parts - n, parts)]
        out[...] = (q.astype(F32) * y_ref[n]).astype(BF16)


def joint_shift(value, segment_step, ctx_step):
    segments, parts = lax.axis_size("segment"), lax.axis_size("ctx")
    pairs = [
        (s * parts + c, (s + segment_step) % segments * parts + (c + ctx_step) % parts)
        for s in range(segments)
        for c in range(parts)
    ]
    return lax.ppermute(value, ("segment", "ctx"), pairs)


def convolved(parts, length, index, slabs, skip_weight, consts):
    rows = length // 2
    outer = parts * length // INNER
    first_turns, forward_a, turns, forward_b, back_b, back_a = consts
    scalar = pl.BlockSpec(memory_space=pltpu.SMEM)
    whole = pl.BlockSpec(memory_space=pltpu.VMEM)

    def block(*shape):
        return jax.ShapeDtypeStruct(shape, F32)

    z, p = pl.pallas_call(
        functools.partial(forward_kernel, parts, outer),
        out_shape=(block(2 * outer * INNER, LANES), block(parts, rows, LANES)),
        in_specs=[scalar] + [whole] * (parts + 2),
        scratch_shapes=[pltpu.VMEM((outer * INNER, LANES), F32)],
        compiler_params=pltpu.CompilerParams(vmem_limit_bytes=LIMIT * 2**20),
    )(index, *slabs, forward_a, first_turns)
    w = pl.pallas_call(
        functools.partial(middle_kernel, outer),
        out_shape=block(outer * INNER, LANES),
        compiler_params=pltpu.CompilerParams(vmem_limit_bytes=LIMIT * 2**20),
    )(z, forward_b, back_b)
    return pl.pallas_call(
        functools.partial(back_kernel, parts, outer),
        out_shape=block(parts, rows, LANES),
        in_specs=[scalar] + [whole] * 5,
        scratch_shapes=[pltpu.VMEM((outer * INNER, LANES), F32)],
        compiler_params=pltpu.CompilerParams(vmem_limit_bytes=LIMIT * 2**20),
    )(index, skip_weight, w, p, back_a, turns)


def fast_on_device(query_stream, key_stream, value_stream, filter_taps, skip_weight):
    parts = lax.axis_size("ctx")
    device = lax.axis_index("ctx")
    length, channels = query_stream.shape[1:]
    rows = length // 2
    index = jnp.full((1,), device, jnp.int32)
    scalar = pl.BlockSpec(memory_space=pltpu.SMEM)
    whole = pl.BlockSpec(memory_space=pltpu.VMEM)
    far = pl.BlockSpec(memory_space=pltpu.HBM)
    small = pltpu.CompilerParams(vmem_limit_bytes=24 * 2**20)
    large = pltpu.CompilerParams(vmem_limit_bytes=60 * 2**20)

    def block(*shape, dtype=BF16):
        return jax.ShapeDtypeStruct(shape, dtype)

    size = 2 * rows + EXTRA
    sent = pl.pallas_call(
        functools.partial(pack_kernel, parts),
        out_shape=(block(size, LANES),) * parts,
        in_specs=[scalar] + [far] * 3,
        scratch_shapes=[pltpu.VMEM((parts, size, LANES), BF16)]
        + [pltpu.VMEM((length, channels), BF16)] * 3
        + [pltpu.SemaphoreType.DMA((3,))],
        compiler_params=large,
    )(index, key_stream[0], value_stream[0], filter_taps[0])
    slabs = [sent[0]] + [joint_shift(sent[n], 0, n) for n in range(1, parts)]
    q = pl.pallas_call(
        functools.partial(pack_gate_kernel, parts),
        out_shape=block(parts, rows, LANES),
        compiler_params=large,
    )(query_stream[0])
    forward_a, forward_b, back_b, back_a, turns, two_turns = [
        jnp.asarray(t) for t in tables(parts * length // INNER)
    ]
    held = (sent[0], forward_a)
    held = pl.pallas_call(
        hold_kernel,
        out_shape=tuple(jax.ShapeDtypeStruct(x.shape, x.dtype) for x in held),
        compiler_params=small,
    )(*held)
    q, *_ = lax.optimization_barrier((q, *slabs, *held))
    slabs = [held[0]] + slabs[1:]
    consts = (two_turns, held[1], turns, forward_b, back_b, back_a)
    q = lax.all_to_all(q, "ctx", split_axis=0, concat_axis=0, tiled=True)
    y = convolved(parts, length, index, slabs, skip_weight, consts)
    gated = pl.pallas_call(
        functools.partial(gate_kernel, parts),
        out_shape=(block(rows, LANES),) * parts,
        in_specs=[scalar, whole, whole],
        compiler_params=small,
    )(index, y, q)
    gated = [joint_shift(gated[n], 1, -n) for n in range(parts)]
    out = pl.pallas_call(
        functools.partial(unpack_kernel, parts),
        out_shape=block(length, channels),
        in_specs=[scalar] + [whole] * parts,
        scratch_shapes=[pltpu.VMEM((parts, rows, LANES), BF16)],
        compiler_params=small,
    )(index, *gated)
    return out[None]


def solution(mesh):
    placed = (
        P("segment", "ctx", None),
        P("segment", "ctx", None),
        P("segment", "ctx", None),
        P("segment", "ctx", None),
        P("segment", None),
    )

    def on_device(*arrays):
        parts = lax.axis_size("ctx")
        length, channels = arrays[0].shape[1:]
        square = parts * length == INNER * INNER
        run = fast_on_device if square and channels == parts * HALF else general_on_device
        return run(*arrays)

    return jax.shard_map(
        on_device, mesh=mesh, in_specs=placed, out_specs=P("segment", "ctx", None), check_vma=False
    )
```

```python
import functools
import math

import jax
import jax.numpy as jnp
import numpy as np
from jax import lax
from jax.experimental import pallas as pl
from jax.experimental.pallas import tpu as pltpu
from jax.sharding import PartitionSpec as P

HIGHEST = lax.Precision.HIGHEST
LANES = 128
HALF = 64
INNER = 64
STEP = 16
EXTRA = 16
DOUBLINGS = 4
SCALE = 215.0
SMALLEST = 1e-30
LIMIT = 30
PAD = 8
WIDE = 16
F32 = jnp.float32
BF16 = jnp.bfloat16


def from_behind(value, axis, steps):
    count = lax.axis_size(axis)
    pairs = [(source, (source + steps) % count) for source in range(count)]
    return lax.ppermute(value, axis, pairs)


def angles(modulus, left, right):
    phase = left[:, None] * right[None, :] % modulus
    theta = phase.astype(jnp.float32) * (2.0 * math.pi / modulus)
    return (jnp.cos(theta), jnp.sin(theta))


def frequency_order(width):
    rows = jnp.arange(2 * width, dtype=jnp.int32)
    halves = rows // 2
    return jnp.where(rows % 2 == 0, halves, jnp.where(halves == 0, width, 2 * width - halves))


def across(table, data):
    return jnp.einsum("rd,dsc->rsc", table, data, precision=HIGHEST)


def along(table, data):
    return jnp.einsum("kb,rbc->rkc", table, data, precision=HIGHEST)


def rotate(real_part, imag_part, cosine, sine):
    return (real_part * cosine + imag_part * sine, imag_part * cosine - real_part * sine)


def general_on_device(query_stream, key_stream, value_stream, filter_taps, skip_weight):
    parts = lax.axis_size("ctx")
    device = lax.axis_index("ctx")
    length = query_stream.shape[1]
    channels = query_stream.shape[2]
    share = length // parts
    total = 2 * parts * length
    product = key_stream[0].astype(jnp.float32) * value_stream[0].astype(jnp.float32)
    taps = filter_taps[0].astype(jnp.float32)
    block_prod, block_taps = (
        lax.all_to_all(
            product.reshape(1, length, channels), "ctx", split_axis=1, concat_axis=0, tiled=True
        ),
        lax.all_to_all(
            taps.reshape(1, length, channels), "ctx", split_axis=1, concat_axis=0, tiled=True
        ),
    )
    order = frequency_order(parts)
    cos_cross, sin_cross = angles(2 * parts, order, jnp.arange(parts, dtype=jnp.int32))
    positions = device * share + jnp.arange(share, dtype=jnp.int32)
    cos_twist, sin_twist = angles(total, order, positions)
    cos_twist = cos_twist[:, :, None]
    sin_twist = sin_twist[:, :, None]
    span = jnp.arange(length, dtype=jnp.int32)
    cos_along, sin_along = angles(length, span, span)
    local_rows = lax.dynamic_slice(order, (2 * device,), (2,))
    cos_back, sin_back = angles(total, local_rows, span)
    cos_back = cos_back[:, :, None]
    sin_back = sin_back[:, :, None]

    def forward_along(real_part, imag_part):
        return (
            along(cos_along, real_part) + along(sin_along, imag_part),
            along(cos_along, imag_part) - along(sin_along, real_part),
        )

    prod_real, prod_imag = rotate(
        across(cos_cross, block_prod), -across(sin_cross, block_prod), cos_twist, sin_twist
    )
    taps_real, taps_imag = rotate(
        across(cos_cross, block_taps), -across(sin_cross, block_taps), cos_twist, sin_twist
    )
    first_real, first_imag = forward_along(
        lax.all_to_all(prod_real, "ctx", split_axis=0, concat_axis=1, tiled=True),
        lax.all_to_all(prod_imag, "ctx", split_axis=0, concat_axis=1, tiled=True),
    )
    second_real, second_imag = forward_along(
        lax.all_to_all(taps_real, "ctx", split_axis=0, concat_axis=1, tiled=True),
        lax.all_to_all(taps_imag, "ctx", split_axis=0, concat_axis=1, tiled=True),
    )
    result_real = first_real * second_real - first_imag * second_imag
    result_imag = first_real * second_imag + first_imag * second_real
    back_real = along(cos_along, result_real) - along(sin_along, result_imag)
    back_imag = along(cos_along, result_imag) + along(sin_along, result_real)
    spec_real, spec_imag = rotate(back_real, back_imag, cos_back, -sin_back)
    rows_real, rows_imag = (
        lax.all_to_all(spec_real, "ctx", split_axis=1, concat_axis=0, tiled=True),
        lax.all_to_all(spec_imag, "ctx", split_axis=1, concat_axis=0, tiled=True),
    )
    cos_final, sin_final = angles(2 * parts, jnp.arange(parts, dtype=jnp.int32), order)
    by_block = jnp.einsum("dr,rsc->dsc", cos_final, rows_real, precision=HIGHEST) - jnp.einsum(
        "dr,rsc->dsc", sin_final, rows_imag, precision=HIGHEST
    )
    by_block = by_block * (1.0 / total)
    convolved = lax.all_to_all(by_block, "ctx", split_axis=0, concat_axis=1, tiled=True)[0]
    gated = query_stream[0].astype(jnp.float32) * (convolved + skip_weight[0][None, :] * product)
    gated = gated.astype(jnp.bfloat16)[None]
    return from_behind(gated, "segment", 1)


def split_two(value):
    high = value.astype(BF16)
    return high, (value - high.astype(F32)).astype(BF16)


def split_table(table):
    table = table.astype(np.float32)
    high = table.astype(jnp.bfloat16)
    low = (table - high.astype(np.float32)).astype(jnp.bfloat16)
    return np.concatenate([high, high, low], axis=1)


def stacked(value):
    high, low = split_two(value)
    return jnp.concatenate([high, low, high], axis=0)


def lower_half(shape):
    return lax.broadcasted_iota(jnp.int32, shape, len(shape) - 1) < HALF


def swap_halves(value):
    return pltpu.roll(value, HALF, value.ndim - 1)


def tables(outer):
    total = outer * INNER
    a = np.arange(outer)
    b = np.arange(INNER)
    c = np.arange(outer) + 0.25
    first = 2.0 * np.pi * np.outer(c, a) / outer
    second = 2.0 * np.pi * np.outer(b, b) / INNER
    forward_a = split_table(np.concatenate([np.cos(first), -np.sin(first)], axis=0))
    forward_b = split_table(
        np.block([[np.cos(second), np.sin(second)], [-np.sin(second), np.cos(second)]])
    )
    back_b = split_table(np.concatenate([np.cos(second), np.sin(second)], axis=0))
    back_a = split_table(np.concatenate([np.cos(first).T, -np.sin(first).T], axis=0) / total)

    def turns(steps):
        theta = 2.0 * np.pi * np.outer(steps, c) / total
        wide = np.stack([np.cos(theta), np.sin(theta)], axis=1).astype(np.float32)
        return np.ascontiguousarray(np.broadcast_to(wide[..., None], wide.shape + (LANES,)))

    return forward_a, forward_b, back_b, back_a, turns(b), turns(np.concatenate([b[:STEP], b[::STEP]]))


def fetched(sources, targets, sems):
    copies = [pltpu.make_async_copy(a, b, sems.at[i]) for i, (a, b) in enumerate(zip(sources, targets))]
    for copy in copies:
        copy.start()
    return copies


def pack_kernel(parts, index_ref, *refs):
    sources, outs, held, arrived, sems = refs[:3], refs[3 : 3 + parts], refs[-5], refs[-4:-1], refs[-1]
    k_ref, v_ref, h_ref = arrived
    rows = k_ref.shape[0] // 2
    low = lower_half((rows, LANES))
    for copy in fetched(sources, arrived, sems):
        copy.wait()

    def place(e, at, tile, low):
        half = tile.shape[0] // 2
        early, late = tile[:half], tile[half:]
        held[2 * e, at : at + half, :] = jnp.where(low, early, swap_halves(late)).astype(BF16)
        held[2 * e + 1, at : at + half, :] = jnp.where(low, swap_halves(early), late).astype(BF16)

    for e in range(parts // 2):
        lanes = slice(LANES * e, LANES * (e + 1))
        product = k_ref[:, lanes].astype(F32) * v_ref[:, lanes].astype(F32)
        largest = jnp.max(jnp.abs(product), axis=0, keepdims=True)
        largest = jnp.maximum(largest * 1.01, SMALLEST).astype(BF16).astype(F32)
        code = product * (SCALE / largest)
        power = code * code
        for _ in range(DOUBLINGS - 1):
            power = power * power
        place(e, 0, jnp.where(code < 0.0, -power, power), low)
        place(e, rows, h_ref[:, lanes].astype(F32), low)
        place(e, 2 * rows, jnp.broadcast_to(largest, (2 * EXTRA, LANES)), low[:EXTRA])
    for n, out in enumerate(outs):
        out[...] = held[lax.rem(index_ref[0] + n, parts)]


def pack_gate_kernel(parts, q_ref, out_ref):
    rows = q_ref.shape[0] // 2
    low = lower_half((rows, LANES))
    for e in range(parts // 2):
        tile = q_ref[:, LANES * e : LANES * (e + 1)].astype(F32)
        early, late = tile[:rows], tile[rows:]
        out_ref[2 * e] = jnp.where(low, early, swap_halves(late)).astype(BF16)
        out_ref[2 * e + 1] = jnp.where(low, swap_halves(early), late).astype(BF16)


def hold_kernel(*refs):
    half = len(refs) // 2
    for source, target in zip(refs[:half], refs[half:]):
        target[...] = source[...]


def unpack_kernel(parts, index_ref, *refs):
    blocks, out_ref, held = refs[:parts], refs[parts], refs[parts + 1]
    rows = held.shape[1]
    low = lower_half((rows, LANES))
    for n, block in enumerate(blocks):
        held[lax.rem(index_ref[0] + n, parts)] = block[...]
    for e in range(parts // 2):
        even, odd = held[2 * e].astype(F32), held[2 * e + 1].astype(F32)
        out_ref[:rows, LANES * e : LANES * (e + 1)] = jnp.where(low, even, swap_halves(odd)).astype(BF16)
        out_ref[rows:, LANES * e : LANES * (e + 1)] = jnp.where(low, swap_halves(even), odd).astype(BF16)


def forward_kernel(parts, outer, index_ref, *refs):
    blocks = refs[:parts]
    matrix_ref, turn_ref, z_s, p_s, x_s = refs[parts:]
    rows = p_s.shape[1]
    per = rows // INNER
    low = lower_half((INNER, LANES))

    def origin(n):
        return lax.rem(index_ref[0] + parts - n, parts)

    for n, block in enumerate(blocks):
        scale = block[2 * rows : 2 * rows + EXTRA, :].astype(F32)[:1] * (1.0 / SCALE)
        for m in range(per):
            at = m * INNER
            code = block[at : at + INNER, :].astype(F32)
            size = jnp.exp(jnp.log(jnp.abs(code)) * (0.5**DOUBLINGS)) * scale
            p = jnp.where(code == 0.0, 0.0, jnp.where(code < 0.0, -size, size))
            p_s[n, at : at + INNER, :] = p
            h = block[rows + at : rows + at + INNER, :].astype(F32)
            a = origin(n) * (2 * per) + m
            x_s[pl.ds(a, INNER, stride=outer + PAD), :] = jnp.where(low, p, swap_halves(h))
            x_s[pl.ds(a + per, INNER, stride=outer + PAD), :] = jnp.where(low, swap_halves(p), h)

    def turn(group, n):
        cos_1, sin_1 = turn_ref[STEP + group, 0], turn_ref[STEP + group, 1]
        if n == 0:
            return cos_1, sin_1
        cos_2, sin_2 = turn_ref[n, 0], turn_ref[n, 1]
        return cos_1 * cos_2 - sin_1 * sin_2, sin_1 * cos_2 + cos_1 * sin_2

    def forward_outer(group, carry):
        for n in range(0, STEP, WIDE):
            b = group * STEP + n
            data = jnp.concatenate(
                [
                    stacked(x_s[pl.ds(pl.multiple_of((b + j) * (outer + PAD), PAD), outer), :])
                    for j in range(WIDE)
                ],
                axis=1,
            )
            both = jnp.dot(matrix_ref[...], data, preferred_element_type=F32)
            for j in range(WIDE):
                re = both[:outer, LANES * j : LANES * (j + 1)]
                im = both[outer:, LANES * j : LANES * (j + 1)]
                cos, sin = turn(group, n + j)
                z_s[pl.ds(b + j, outer, stride=2 * INNER + PAD), :] = re * cos + im * sin
                z_s[pl.ds(b + j + INNER, outer, stride=2 * INNER + PAD), :] = im * cos - re * sin
        return carry

    lax.fori_loop(0, INNER // STEP, forward_outer, 0)


def middle_kernel(outer, z_s, forward_ref, back_ref, w_s):
    low = lower_half((INNER, LANES))

    def middle(group, carry):
        for n in range(0, STEP, WIDE):
            c = group * STEP + n
            data = jnp.concatenate(
                [
                    stacked(z_s[pl.ds(pl.multiple_of((c + j) * (2 * INNER + PAD), PAD), 2 * INNER), :])
                    for j in range(WIDE)
                ],
                axis=1,
            )
            both = jnp.dot(forward_ref[...], data, preferred_element_type=F32)
            mixed = []
            for j in range(WIDE):
                re = both[:INNER, LANES * j : LANES * (j + 1)]
                im = both[INNER:, LANES * j : LANES * (j + 1)]
                re_2, im_2 = swap_halves(re), swap_halves(im)
                mixed.append(
                    stacked(jnp.where(low, re * re_2 - im * im_2, re * im_2 + im * re_2))
                )
            both = jnp.dot(back_ref[...], jnp.concatenate(mixed, axis=1), preferred_element_type=F32)
            for j in range(WIDE):
                straight = both[:INNER, LANES * j : LANES * (j + 1)]
                crossed = swap_halves(both[INNER:, LANES * j : LANES * (j + 1)])
                w_s[pl.ds(c + j, INNER, stride=outer + PAD), :] = jnp.where(
                    low, straight - crossed, straight + crossed
                )
        return carry

    lax.fori_loop(0, outer // STEP, middle, 0)


def back_kernel(parts, outer, index_ref, skip_ref, w_s, p_s, *refs):
    matrix_ref, turn_ref, out_ref, y_s = refs
    rows = out_ref.shape[1]
    lowc = lower_half((outer, LANES))

    def origin(n):
        return lax.rem(index_ref[0] + parts - n, parts)

    def turn(group, n):
        return turn_ref[group * STEP + n, 0], turn_ref[group * STEP + n, 1]

    def back_outer(group, carry):
        for n in range(0, STEP, WIDE):
            b = group * STEP + n
            data = []
            for j in range(WIDE):
                value = w_s[pl.ds(pl.multiple_of((b + j) * (outer + PAD), PAD), outer), :]
                cos, sin = turn(group, n + j)
                other = swap_halves(value) * sin
                straight = value * cos
                data.append(stacked(jnp.where(lowc, straight - other, straight + other)))
            both = jnp.dot(matrix_ref[...], jnp.concatenate(data, axis=1), preferred_element_type=F32)
            for j in range(WIDE):
                re = both[:outer, LANES * j : LANES * (j + 1)]
                im = both[outer:, LANES * j : LANES * (j + 1)]
                y_s[pl.ds(b + j, outer, stride=INNER), :] = re + swap_halves(im)
        return carry

    lax.fori_loop(0, INNER // STEP, back_outer, 0)

    lowr = lower_half((rows, LANES))
    pair = pl.multiple_of(index_ref[0] // 2 * LANES, LANES)
    wide = skip_ref[:, pl.ds(pair, LANES)]
    mine = lower_half((1, LANES)) == (index_ref[0] % 2 == 0)
    skip = jnp.where(mine, wide, swap_halves(wide))
    for n in range(parts):
        at = pl.multiple_of(origin(n) * 2 * rows, 2 * rows)
        early = y_s[pl.ds(at, rows), :]
        late = y_s[pl.ds(at + rows, rows), :]
        out_ref[n] = jnp.where(lowr, early, swap_halves(late)) + skip * p_s[n]


def gate_kernel(parts, index_ref, y_ref, q_ref, *outs):
    for n, out in enumerate(outs):
        q = q_ref[lax.rem(index_ref[0] + parts - n, parts)]
        out[...] = (q.astype(F32) * y_ref[n]).astype(BF16)


def joint_shift(value, segment_step, ctx_step):
    segments, parts = lax.axis_size("segment"), lax.axis_size("ctx")
    pairs = [
        (s * parts + c, (s + segment_step) % segments * parts + (c + ctx_step) % parts)
        for s in range(segments)
        for c in range(parts)
    ]
    return lax.ppermute(value, ("segment", "ctx"), pairs)


def convolved(parts, length, index, slabs, skip_weight, consts):
    rows = length // 2
    outer = parts * length // INNER
    first_turns, forward_a, turns, forward_b, back_b, back_a = consts
    scalar = pl.BlockSpec(memory_space=pltpu.SMEM)
    whole = pl.BlockSpec(memory_space=pltpu.VMEM)

    def block(*shape):
        return jax.ShapeDtypeStruct(shape, F32)

    z, p = pl.pallas_call(
        functools.partial(forward_kernel, parts, outer),
        out_shape=(block(outer * (2 * INNER + PAD), LANES), block(parts, rows, LANES)),
        in_specs=[scalar] + [whole] * (parts + 2),
        scratch_shapes=[pltpu.VMEM((INNER * (outer + PAD), LANES), F32)],
        compiler_params=pltpu.CompilerParams(vmem_limit_bytes=LIMIT * 2**20),
    )(index, *slabs, forward_a, first_turns)
    w = pl.pallas_call(
        functools.partial(middle_kernel, outer),
        out_shape=block(INNER * (outer + PAD), LANES),
        compiler_params=pltpu.CompilerParams(vmem_limit_bytes=LIMIT * 2**20),
    )(z, forward_b, back_b)
    return pl.pallas_call(
        functools.partial(back_kernel, parts, outer),
        out_shape=block(parts, rows, LANES),
        in_specs=[scalar] + [whole] * 5,
        scratch_shapes=[pltpu.VMEM((outer * INNER, LANES), F32)],
        compiler_params=pltpu.CompilerParams(vmem_limit_bytes=LIMIT * 2**20),
    )(index, skip_weight, w, p, back_a, turns)


def fast_on_device(query_stream, key_stream, value_stream, filter_taps, skip_weight):
    parts = lax.axis_size("ctx")
    device = lax.axis_index("ctx")
    length, channels = query_stream.shape[1:]
    rows = length // 2
    index = jnp.full((1,), device, jnp.int32)
    scalar = pl.BlockSpec(memory_space=pltpu.SMEM)
    whole = pl.BlockSpec(memory_space=pltpu.VMEM)
    far = pl.BlockSpec(memory_space=pltpu.HBM)
    small = pltpu.CompilerParams(vmem_limit_bytes=24 * 2**20)
    large = pltpu.CompilerParams(vmem_limit_bytes=60 * 2**20)

    def block(*shape, dtype=BF16):
        return jax.ShapeDtypeStruct(shape, dtype)

    size = 2 * rows + EXTRA
    sent = pl.pallas_call(
        functools.partial(pack_kernel, parts),
        out_shape=(block(size, LANES),) * parts,
        in_specs=[scalar] + [far] * 3,
        scratch_shapes=[pltpu.VMEM((parts, size, LANES), BF16)]
        + [pltpu.VMEM((length, channels), BF16)] * 3
        + [pltpu.SemaphoreType.DMA((3,))],
        compiler_params=large,
    )(index, key_stream[0], value_stream[0], filter_taps[0])
    slabs = [sent[0]] + [joint_shift(sent[n], 0, n) for n in range(1, parts)]
    q = pl.pallas_call(
        functools.partial(pack_gate_kernel, parts),
        out_shape=block(parts, rows, LANES),
        compiler_params=large,
    )(query_stream[0])
    forward_a, forward_b, back_b, back_a, turns, two_turns = [
        jnp.asarray(t) for t in tables(parts * length // INNER)
    ]
    held = (sent[0], forward_a)
    held = pl.pallas_call(
        hold_kernel,
        out_shape=tuple(jax.ShapeDtypeStruct(x.shape, x.dtype) for x in held),
        compiler_params=small,
    )(*held)
    q, *_ = lax.optimization_barrier((q, *slabs, *held))
    slabs = [held[0]] + slabs[1:]
    consts = (two_turns, held[1], turns, forward_b, back_b, back_a)
    q = lax.all_to_all(q, "ctx", split_axis=0, concat_axis=0, tiled=True)
    y = convolved(parts, length, index, slabs, skip_weight, consts)
    gated = pl.pallas_call(
        functools.partial(gate_kernel, parts),
        out_shape=(block(rows, LANES),) * parts,
        in_specs=[scalar, whole, whole],
        compiler_params=small,
    )(index, y, q)
    gated = [joint_shift(gated[n], 1, -n) for n in range(parts)]
    out = pl.pallas_call(
        functools.partial(unpack_kernel, parts),
        out_shape=block(length, channels),
        in_specs=[scalar] + [whole] * parts,
        scratch_shapes=[pltpu.VMEM((parts, rows, LANES), BF16)],
        compiler_params=small,
    )(index, *gated)
    return out[None]


def solution(mesh):
    placed = (
        P("segment", "ctx", None),
        P("segment", "ctx", None),
        P("segment", "ctx", None),
        P("segment", "ctx", None),
        P("segment", None),
    )

    def on_device(*arrays):
        parts = lax.axis_size("ctx")
        length, channels = arrays[0].shape[1:]
        square = parts * length == INNER * INNER
        run = fast_on_device if square and channels == parts * HALF else general_on_device
        return run(*arrays)

    return jax.shard_map(
        on_device, mesh=mesh, in_specs=placed, out_specs=P("segment", "ctx", None), check_vma=False
    )
```

```python
import functools
import math

import jax
import jax.numpy as jnp
import numpy as np
from jax import lax
from jax.experimental import pallas as pl
from jax.experimental.pallas import tpu as pltpu
from jax.sharding import PartitionSpec as P

HIGHEST = lax.Precision.HIGHEST
LANES = 128
HALF = 64
INNER = 64
STEP = 16
EXTRA = 16
DOUBLINGS = 4
SCALE = 215.0
SMALLEST = 1e-30
LIMIT = 30
PAD = 8
WIDE = 16
F32 = jnp.float32
BF16 = jnp.bfloat16


def from_behind(value, axis, steps):
    count = lax.axis_size(axis)
    pairs = [(source, (source + steps) % count) for source in range(count)]
    return lax.ppermute(value, axis, pairs)


def angles(modulus, left, right):
    phase = left[:, None] * right[None, :] % modulus
    theta = phase.astype(jnp.float32) * (2.0 * math.pi / modulus)
    return (jnp.cos(theta), jnp.sin(theta))


def frequency_order(width):
    rows = jnp.arange(2 * width, dtype=jnp.int32)
    halves = rows // 2
    return jnp.where(rows % 2 == 0, halves, jnp.where(halves == 0, width, 2 * width - halves))


def across(table, data):
    return jnp.einsum("rd,dsc->rsc", table, data, precision=HIGHEST)


def along(table, data):
    return jnp.einsum("kb,rbc->rkc", table, data, precision=HIGHEST)


def rotate(real_part, imag_part, cosine, sine):
    return (real_part * cosine + imag_part * sine, imag_part * cosine - real_part * sine)


def general_on_device(query_stream, key_stream, value_stream, filter_taps, skip_weight):
    parts = lax.axis_size("ctx")
    device = lax.axis_index("ctx")
    length = query_stream.shape[1]
    channels = query_stream.shape[2]
    share = length // parts
    total = 2 * parts * length
    product = key_stream[0].astype(jnp.float32) * value_stream[0].astype(jnp.float32)
    taps = filter_taps[0].astype(jnp.float32)
    block_prod, block_taps = (
        lax.all_to_all(
            product.reshape(1, length, channels), "ctx", split_axis=1, concat_axis=0, tiled=True
        ),
        lax.all_to_all(
            taps.reshape(1, length, channels), "ctx", split_axis=1, concat_axis=0, tiled=True
        ),
    )
    order = frequency_order(parts)
    cos_cross, sin_cross = angles(2 * parts, order, jnp.arange(parts, dtype=jnp.int32))
    positions = device * share + jnp.arange(share, dtype=jnp.int32)
    cos_twist, sin_twist = angles(total, order, positions)
    cos_twist = cos_twist[:, :, None]
    sin_twist = sin_twist[:, :, None]
    span = jnp.arange(length, dtype=jnp.int32)
    cos_along, sin_along = angles(length, span, span)
    local_rows = lax.dynamic_slice(order, (2 * device,), (2,))
    cos_back, sin_back = angles(total, local_rows, span)
    cos_back = cos_back[:, :, None]
    sin_back = sin_back[:, :, None]

    def forward_along(real_part, imag_part):
        return (
            along(cos_along, real_part) + along(sin_along, imag_part),
            along(cos_along, imag_part) - along(sin_along, real_part),
        )

    prod_real, prod_imag = rotate(
        across(cos_cross, block_prod), -across(sin_cross, block_prod), cos_twist, sin_twist
    )
    taps_real, taps_imag = rotate(
        across(cos_cross, block_taps), -across(sin_cross, block_taps), cos_twist, sin_twist
    )
    first_real, first_imag = forward_along(
        lax.all_to_all(prod_real, "ctx", split_axis=0, concat_axis=1, tiled=True),
        lax.all_to_all(prod_imag, "ctx", split_axis=0, concat_axis=1, tiled=True),
    )
    second_real, second_imag = forward_along(
        lax.all_to_all(taps_real, "ctx", split_axis=0, concat_axis=1, tiled=True),
        lax.all_to_all(taps_imag, "ctx", split_axis=0, concat_axis=1, tiled=True),
    )
    result_real = first_real * second_real - first_imag * second_imag
    result_imag = first_real * second_imag + first_imag * second_real
    back_real = along(cos_along, result_real) - along(sin_along, result_imag)
    back_imag = along(cos_along, result_imag) + along(sin_along, result_real)
    spec_real, spec_imag = rotate(back_real, back_imag, cos_back, -sin_back)
    rows_real, rows_imag = (
        lax.all_to_all(spec_real, "ctx", split_axis=1, concat_axis=0, tiled=True),
        lax.all_to_all(spec_imag, "ctx", split_axis=1, concat_axis=0, tiled=True),
    )
    cos_final, sin_final = angles(2 * parts, jnp.arange(parts, dtype=jnp.int32), order)
    by_block = jnp.einsum("dr,rsc->dsc", cos_final, rows_real, precision=HIGHEST) - jnp.einsum(
        "dr,rsc->dsc", sin_final, rows_imag, precision=HIGHEST
    )
    by_block = by_block * (1.0 / total)
    convolved = lax.all_to_all(by_block, "ctx", split_axis=0, concat_axis=1, tiled=True)[0]
    gated = query_stream[0].astype(jnp.float32) * (convolved + skip_weight[0][None, :] * product)
    gated = gated.astype(jnp.bfloat16)[None]
    return from_behind(gated, "segment", 1)


def split_two(value):
    high = value.astype(BF16)
    return high, (value - high.astype(F32)).astype(BF16)


def split_table(table):
    table = table.astype(np.float32)
    high = table.astype(jnp.bfloat16)
    low = (table - high.astype(np.float32)).astype(jnp.bfloat16)
    return np.concatenate([high, high, low], axis=1)


def stacked(value):
    high, low = split_two(value)
    return jnp.concatenate([high, low, high], axis=0)


def lower_half(shape):
    return lax.broadcasted_iota(jnp.int32, shape, len(shape) - 1) < HALF


def swap_halves(value):
    return pltpu.roll(value, HALF, value.ndim - 1)


def tables(outer):
    total = outer * INNER
    a = np.arange(outer)
    b = np.arange(INNER)
    c = np.arange(outer) + 0.25
    first = 2.0 * np.pi * np.outer(c, a) / outer
    second = 2.0 * np.pi * np.outer(b, b) / INNER
    forward_a = split_table(np.concatenate([np.cos(first), -np.sin(first)], axis=0))
    forward_b = split_table(
        np.block([[np.cos(second), np.sin(second)], [-np.sin(second), np.cos(second)]])
    )
    back_b = split_table(np.concatenate([np.cos(second), np.sin(second)], axis=0))
    back_a = split_table(np.concatenate([np.cos(first).T, -np.sin(first).T], axis=0) / total)

    def turns(steps):
        theta = 2.0 * np.pi * np.outer(steps, c) / total
        wide = np.stack([np.cos(theta), np.sin(theta)], axis=1).astype(np.float32)
        return np.ascontiguousarray(np.broadcast_to(wide[..., None], wide.shape + (LANES,)))

    return forward_a, forward_b, back_b, back_a, turns(b), turns(np.concatenate([b[:STEP], b[::STEP]]))


def fetched(sources, targets, sems):
    copies = [pltpu.make_async_copy(a, b, sems.at[i]) for i, (a, b) in enumerate(zip(sources, targets))]
    for copy in copies:
        copy.start()
    return copies


def pack_kernel(parts, index_ref, *refs):
    sources, outs, held, arrived, sems = refs[:3], refs[3 : 3 + parts], refs[-6], refs[-5:-2], refs[-2]
    out_sems = refs[-1]
    k_ref, v_ref, h_ref = arrived
    rows = k_ref.shape[0] // 2
    low = lower_half((rows, LANES))
    k_copy, v_copy, h_copy = fetched(sources, arrived, sems)
    k_copy.wait()
    v_copy.wait()

    def place(e, at, tile, low):
        half = tile.shape[0] // 2
        early, late = tile[:half], tile[half:]
        held[2 * e, at : at + half, :] = jnp.where(low, early, swap_halves(late)).astype(BF16)
        held[2 * e + 1, at : at + half, :] = jnp.where(low, swap_halves(early), late).astype(BF16)

    for e in range(parts // 2):
        lanes = slice(LANES * e, LANES * (e + 1))
        product = k_ref[:, lanes].astype(F32) * v_ref[:, lanes].astype(F32)
        largest = jnp.max(jnp.abs(product), axis=0, keepdims=True)
        largest = jnp.maximum(largest * 1.01, SMALLEST).astype(BF16).astype(F32)
        code = product * (SCALE / largest)
        power = code * code
        for _ in range(DOUBLINGS - 1):
            power = power * power
        place(e, 0, jnp.where(code < 0.0, -power, power), low)
        place(e, 2 * rows, jnp.broadcast_to(largest, (2 * EXTRA, LANES)), low[:EXTRA])
    h_copy.wait()
    for e in range(parts // 2):
        place(e, rows, h_ref[:, LANES * e : LANES * (e + 1)].astype(F32), low)
    ready = [held.at[lax.rem(index_ref[0] + n, parts)] for n in range(parts)]
    for copy in fetched(ready, outs, out_sems):
        copy.wait()


def pack_gate_kernel(parts, q_ref, out_ref):
    rows = q_ref.shape[0] // 2
    low = lower_half((rows, LANES))
    for e in range(parts // 2):
        tile = q_ref[:, LANES * e : LANES * (e + 1)].astype(F32)
        early, late = tile[:rows], tile[rows:]
        out_ref[2 * e] = jnp.where(low, early, swap_halves(late)).astype(BF16)
        out_ref[2 * e + 1] = jnp.where(low, swap_halves(early), late).astype(BF16)


def hold_kernel(*refs):
    half = len(refs) // 2
    for source, target in zip(refs[:half], refs[half:]):
        target[...] = source[...]


def unpack_kernel(parts, index_ref, *refs):
    blocks, out_ref, held = refs[:parts], refs[parts], refs[parts + 1]
    rows = held.shape[1]
    low = lower_half((rows, LANES))
    for n, block in enumerate(blocks):
        held[lax.rem(index_ref[0] + n, parts)] = block[...]
    for e in range(parts // 2):
        even, odd = held[2 * e].astype(F32), held[2 * e + 1].astype(F32)
        out_ref[:rows, LANES * e : LANES * (e + 1)] = jnp.where(low, even, swap_halves(odd)).astype(BF16)
        out_ref[rows:, LANES * e : LANES * (e + 1)] = jnp.where(low, swap_halves(even), odd).astype(BF16)


def forward_kernel(parts, outer, index_ref, *refs):
    blocks = refs[:parts]
    matrix_ref, turn_ref, z_s, p_s, x_s = refs[parts:]
    rows = p_s.shape[1]
    per = rows // INNER
    low = lower_half((INNER, LANES))

    def origin(n):
        return lax.rem(index_ref[0] + parts - n, parts)

    for n, block in enumerate(blocks):
        scale = block[2 * rows : 2 * rows + EXTRA, :].astype(F32)[:1] * (1.0 / SCALE)
        for m in range(per):
            at = m * INNER
            code = block[at : at + INNER, :].astype(F32)
            size = jnp.exp(jnp.log(jnp.abs(code)) * (0.5**DOUBLINGS)) * scale
            p = jnp.where(code == 0.0, 0.0, jnp.where(code < 0.0, -size, size))
            p_s[n, at : at + INNER, :] = p
            h = block[rows + at : rows + at + INNER, :].astype(F32)
            a = origin(n) * (2 * per) + m
            x_s[pl.ds(a, INNER, stride=outer + PAD), :] = jnp.where(low, p, swap_halves(h))
            x_s[pl.ds(a + per, INNER, stride=outer + PAD), :] = jnp.where(low, swap_halves(p), h)

    def turn(group, n):
        cos_1, sin_1 = turn_ref[STEP + group, 0], turn_ref[STEP + group, 1]
        if n == 0:
            return cos_1, sin_1
        cos_2, sin_2 = turn_ref[n, 0], turn_ref[n, 1]
        return cos_1 * cos_2 - sin_1 * sin_2, sin_1 * cos_2 + cos_1 * sin_2

    def forward_outer(group, carry):
        for n in range(0, STEP, WIDE):
            b = group * STEP + n
            data = jnp.concatenate(
                [
                    stacked(x_s[pl.ds(pl.multiple_of((b + j) * (outer + PAD), PAD), outer), :])
                    for j in range(WIDE)
                ],
                axis=1,
            )
            both = jnp.dot(matrix_ref[...], data, preferred_element_type=F32)
            for j in range(WIDE):
                re = both[:outer, LANES * j : LANES * (j + 1)]
                im = both[outer:, LANES * j : LANES * (j + 1)]
                cos, sin = turn(group, n + j)
                z_s[pl.ds(b + j, outer, stride=2 * INNER + PAD), :] = re * cos + im * sin
                z_s[pl.ds(b + j + INNER, outer, stride=2 * INNER + PAD), :] = im * cos - re * sin
        return carry

    lax.fori_loop(0, INNER // STEP, forward_outer, 0)


def middle_kernel(outer, z_s, forward_ref, back_ref, w_s):
    low = lower_half((INNER, LANES))

    def middle(group, carry):
        for n in range(0, STEP, WIDE):
            c = group * STEP + n
            data = jnp.concatenate(
                [
                    stacked(z_s[pl.ds(pl.multiple_of((c + j) * (2 * INNER + PAD), PAD), 2 * INNER), :])
                    for j in range(WIDE)
                ],
                axis=1,
            )
            both = jnp.dot(forward_ref[...], data, preferred_element_type=F32)
            mixed = []
            for j in range(WIDE):
                re = both[:INNER, LANES * j : LANES * (j + 1)]
                im = both[INNER:, LANES * j : LANES * (j + 1)]
                re_2, im_2 = swap_halves(re), swap_halves(im)
                mixed.append(
                    stacked(jnp.where(low, re * re_2 - im * im_2, re * im_2 + im * re_2))
                )
            both = jnp.dot(back_ref[...], jnp.concatenate(mixed, axis=1), preferred_element_type=F32)
            for j in range(WIDE):
                straight = both[:INNER, LANES * j : LANES * (j + 1)]
                crossed = swap_halves(both[INNER:, LANES * j : LANES * (j + 1)])
                w_s[pl.ds(c + j, INNER, stride=outer + PAD), :] = jnp.where(
                    low, straight - crossed, straight + crossed
                )
        return carry

    lax.fori_loop(0, outer // STEP, middle, 0)


def back_kernel(parts, outer, index_ref, skip_ref, w_s, p_s, *refs):
    matrix_ref, turn_ref, out_ref, y_s = refs
    rows = out_ref.shape[1]
    lowc = lower_half((outer, LANES))

    def origin(n):
        return lax.rem(index_ref[0] + parts - n, parts)

    def turn(group, n):
        return turn_ref[group * STEP + n, 0], turn_ref[group * STEP + n, 1]

    def back_outer(group, carry):
        for n in range(0, STEP, WIDE):
            b = group * STEP + n
            data = []
            for j in range(WIDE):
                value = w_s[pl.ds(pl.multiple_of((b + j) * (outer + PAD), PAD), outer), :]
                cos, sin = turn(group, n + j)
                other = swap_halves(value) * sin
                straight = value * cos
                data.append(stacked(jnp.where(lowc, straight - other, straight + other)))
            both = jnp.dot(matrix_ref[...], jnp.concatenate(data, axis=1), preferred_element_type=F32)
            for j in range(WIDE):
                re = both[:outer, LANES * j : LANES * (j + 1)]
                im = both[outer:, LANES * j : LANES * (j + 1)]
                y_s[pl.ds(b + j, outer, stride=INNER), :] = re + swap_halves(im)
        return carry

    lax.fori_loop(0, INNER // STEP, back_outer, 0)

    lowr = lower_half((rows, LANES))
    pair = pl.multiple_of(index_ref[0] // 2 * LANES, LANES)
    wide = skip_ref[:, pl.ds(pair, LANES)]
    mine = lower_half((1, LANES)) == (index_ref[0] % 2 == 0)
    skip = jnp.where(mine, wide, swap_halves(wide))
    for n in range(parts):
        at = pl.multiple_of(origin(n) * 2 * rows, 2 * rows)
        early = y_s[pl.ds(at, rows), :]
        late = y_s[pl.ds(at + rows, rows), :]
        out_ref[n] = jnp.where(lowr, early, swap_halves(late)) + skip * p_s[n]


def gate_kernel(parts, index_ref, y_ref, q_ref, *outs):
    for n, out in enumerate(outs):
        q = q_ref[lax.rem(index_ref[0] + parts - n, parts)]
        out[...] = (q.astype(F32) * y_ref[n]).astype(BF16)


def joint_shift(value, segment_step, ctx_step):
    segments, parts = lax.axis_size("segment"), lax.axis_size("ctx")
    pairs = [
        (s * parts + c, (s + segment_step) % segments * parts + (c + ctx_step) % parts)
        for s in range(segments)
        for c in range(parts)
    ]
    return lax.ppermute(value, ("segment", "ctx"), pairs)


def convolved(parts, length, index, slabs, skip_weight, consts):
    rows = length // 2
    outer = parts * length // INNER
    first_turns, forward_a, turns, forward_b, back_b, back_a = consts
    scalar = pl.BlockSpec(memory_space=pltpu.SMEM)
    whole = pl.BlockSpec(memory_space=pltpu.VMEM)

    def block(*shape):
        return jax.ShapeDtypeStruct(shape, F32)

    z, p = pl.pallas_call(
        functools.partial(forward_kernel, parts, outer),
        out_shape=(block(outer * (2 * INNER + PAD), LANES), block(parts, rows, LANES)),
        in_specs=[scalar] + [whole] * (parts + 2),
        scratch_shapes=[pltpu.VMEM((INNER * (outer + PAD), LANES), F32)],
        compiler_params=pltpu.CompilerParams(vmem_limit_bytes=LIMIT * 2**20),
    )(index, *slabs, forward_a, first_turns)
    w = pl.pallas_call(
        functools.partial(middle_kernel, outer),
        out_shape=block(INNER * (outer + PAD), LANES),
        compiler_params=pltpu.CompilerParams(vmem_limit_bytes=LIMIT * 2**20),
    )(z, forward_b, back_b)
    return pl.pallas_call(
        functools.partial(back_kernel, parts, outer),
        out_shape=block(parts, rows, LANES),
        in_specs=[scalar] + [whole] * 5,
        scratch_shapes=[pltpu.VMEM((outer * INNER, LANES), F32)],
        compiler_params=pltpu.CompilerParams(vmem_limit_bytes=LIMIT * 2**20),
    )(index, skip_weight, w, p, back_a, turns)


def fast_on_device(query_stream, key_stream, value_stream, filter_taps, skip_weight):
    parts = lax.axis_size("ctx")
    device = lax.axis_index("ctx")
    length, channels = query_stream.shape[1:]
    rows = length // 2
    index = jnp.full((1,), device, jnp.int32)
    scalar = pl.BlockSpec(memory_space=pltpu.SMEM)
    whole = pl.BlockSpec(memory_space=pltpu.VMEM)
    far = pl.BlockSpec(memory_space=pltpu.HBM)
    small = pltpu.CompilerParams(vmem_limit_bytes=24 * 2**20)
    large = pltpu.CompilerParams(vmem_limit_bytes=60 * 2**20)

    def block(*shape, dtype=BF16):
        return jax.ShapeDtypeStruct(shape, dtype)

    size = 2 * rows + EXTRA
    sent = pl.pallas_call(
        functools.partial(pack_kernel, parts),
        out_shape=(block(size, LANES),) * parts,
        in_specs=[scalar] + [far] * 3,
        out_specs=(far,) * parts,
        scratch_shapes=[pltpu.VMEM((parts, size, LANES), BF16)]
        + [pltpu.VMEM((length, channels), BF16)] * 3
        + [pltpu.SemaphoreType.DMA((3,)), pltpu.SemaphoreType.DMA((parts,))],
        compiler_params=large,
    )(index, key_stream[0], value_stream[0], filter_taps[0])
    slabs = [sent[0]] + [joint_shift(sent[n], 0, n) for n in range(1, parts)]
    q = pl.pallas_call(
        functools.partial(pack_gate_kernel, parts),
        out_shape=block(parts, rows, LANES),
        compiler_params=large,
    )(query_stream[0])
    forward_a, forward_b, back_b, back_a, turns, two_turns = [
        jnp.asarray(t) for t in tables(parts * length // INNER)
    ]
    held = (sent[0], forward_a)
    held = pl.pallas_call(
        hold_kernel,
        out_shape=tuple(jax.ShapeDtypeStruct(x.shape, x.dtype) for x in held),
        compiler_params=small,
    )(*held)
    q, *_ = lax.optimization_barrier((q, *slabs, *held))
    slabs = [held[0]] + slabs[1:]
    consts = (two_turns, held[1], turns, forward_b, back_b, back_a)
    q = lax.all_to_all(q, "ctx", split_axis=0, concat_axis=0, tiled=True)
    y = convolved(parts, length, index, slabs, skip_weight, consts)
    gated = pl.pallas_call(
        functools.partial(gate_kernel, parts),
        out_shape=(block(rows, LANES),) * parts,
        in_specs=[scalar, whole, whole],
        compiler_params=small,
    )(index, y, q)
    gated = [joint_shift(gated[n], 1, -n) for n in range(parts)]
    out = pl.pallas_call(
        functools.partial(unpack_kernel, parts),
        out_shape=block(length, channels),
        in_specs=[scalar] + [whole] * parts,
        scratch_shapes=[pltpu.VMEM((parts, rows, LANES), BF16)],
        compiler_params=small,
    )(index, *gated)
    return out[None]


def solution(mesh):
    placed = (
        P("segment", "ctx", None),
        P("segment", "ctx", None),
        P("segment", "ctx", None),
        P("segment", "ctx", None),
        P("segment", None),
    )

    def on_device(*arrays):
        parts = lax.axis_size("ctx")
        length, channels = arrays[0].shape[1:]
        square = parts * length == INNER * INNER
        run = fast_on_device if square and channels == parts * HALF else general_on_device
        return run(*arrays)

    return jax.shard_map(
        on_device, mesh=mesh, in_specs=placed, out_specs=P("segment", "ctx", None), check_vma=False
    )
```

```python
import functools
import math

import jax
import jax.numpy as jnp
import numpy as np
from jax import lax
from jax.experimental import pallas as pl
from jax.experimental.pallas import tpu as pltpu
from jax.sharding import PartitionSpec as P

HIGHEST = lax.Precision.HIGHEST
LANES = 128
HALF = 64
INNER = 64
STEP = 16
EXTRA = 16
DOUBLINGS = 4
SCALE = 215.0
SMALLEST = 1e-30
LIMIT = 30
PAD = 8
WIDE = 16
F32 = jnp.float32
BF16 = jnp.bfloat16


def from_behind(value, axis, steps):
    count = lax.axis_size(axis)
    pairs = [(source, (source + steps) % count) for source in range(count)]
    return lax.ppermute(value, axis, pairs)


def angles(modulus, left, right):
    phase = left[:, None] * right[None, :] % modulus
    theta = phase.astype(jnp.float32) * (2.0 * math.pi / modulus)
    return (jnp.cos(theta), jnp.sin(theta))


def frequency_order(width):
    rows = jnp.arange(2 * width, dtype=jnp.int32)
    halves = rows // 2
    return jnp.where(rows % 2 == 0, halves, jnp.where(halves == 0, width, 2 * width - halves))


def across(table, data):
    return jnp.einsum("rd,dsc->rsc", table, data, precision=HIGHEST)


def along(table, data):
    return jnp.einsum("kb,rbc->rkc", table, data, precision=HIGHEST)


def rotate(real_part, imag_part, cosine, sine):
    return (real_part * cosine + imag_part * sine, imag_part * cosine - real_part * sine)


def general_on_device(query_stream, key_stream, value_stream, filter_taps, skip_weight):
    parts = lax.axis_size("ctx")
    device = lax.axis_index("ctx")
    length = query_stream.shape[1]
    channels = query_stream.shape[2]
    share = length // parts
    total = 2 * parts * length
    product = key_stream[0].astype(jnp.float32) * value_stream[0].astype(jnp.float32)
    taps = filter_taps[0].astype(jnp.float32)
    block_prod, block_taps = (
        lax.all_to_all(
            product.reshape(1, length, channels), "ctx", split_axis=1, concat_axis=0, tiled=True
        ),
        lax.all_to_all(
            taps.reshape(1, length, channels), "ctx", split_axis=1, concat_axis=0, tiled=True
        ),
    )
    order = frequency_order(parts)
    cos_cross, sin_cross = angles(2 * parts, order, jnp.arange(parts, dtype=jnp.int32))
    positions = device * share + jnp.arange(share, dtype=jnp.int32)
    cos_twist, sin_twist = angles(total, order, positions)
    cos_twist = cos_twist[:, :, None]
    sin_twist = sin_twist[:, :, None]
    span = jnp.arange(length, dtype=jnp.int32)
    cos_along, sin_along = angles(length, span, span)
    local_rows = lax.dynamic_slice(order, (2 * device,), (2,))
    cos_back, sin_back = angles(total, local_rows, span)
    cos_back = cos_back[:, :, None]
    sin_back = sin_back[:, :, None]

    def forward_along(real_part, imag_part):
        return (
            along(cos_along, real_part) + along(sin_along, imag_part),
            along(cos_along, imag_part) - along(sin_along, real_part),
        )

    prod_real, prod_imag = rotate(
        across(cos_cross, block_prod), -across(sin_cross, block_prod), cos_twist, sin_twist
    )
    taps_real, taps_imag = rotate(
        across(cos_cross, block_taps), -across(sin_cross, block_taps), cos_twist, sin_twist
    )
    first_real, first_imag = forward_along(
        lax.all_to_all(prod_real, "ctx", split_axis=0, concat_axis=1, tiled=True),
        lax.all_to_all(prod_imag, "ctx", split_axis=0, concat_axis=1, tiled=True),
    )
    second_real, second_imag = forward_along(
        lax.all_to_all(taps_real, "ctx", split_axis=0, concat_axis=1, tiled=True),
        lax.all_to_all(taps_imag, "ctx", split_axis=0, concat_axis=1, tiled=True),
    )
    result_real = first_real * second_real - first_imag * second_imag
    result_imag = first_real * second_imag + first_imag * second_real
    back_real = along(cos_along, result_real) - along(sin_along, result_imag)
    back_imag = along(cos_along, result_imag) + along(sin_along, result_real)
    spec_real, spec_imag = rotate(back_real, back_imag, cos_back, -sin_back)
    rows_real, rows_imag = (
        lax.all_to_all(spec_real, "ctx", split_axis=1, concat_axis=0, tiled=True),
        lax.all_to_all(spec_imag, "ctx", split_axis=1, concat_axis=0, tiled=True),
    )
    cos_final, sin_final = angles(2 * parts, jnp.arange(parts, dtype=jnp.int32), order)
    by_block = jnp.einsum("dr,rsc->dsc", cos_final, rows_real, precision=HIGHEST) - jnp.einsum(
        "dr,rsc->dsc", sin_final, rows_imag, precision=HIGHEST
    )
    by_block = by_block * (1.0 / total)
    convolved = lax.all_to_all(by_block, "ctx", split_axis=0, concat_axis=1, tiled=True)[0]
    gated = query_stream[0].astype(jnp.float32) * (convolved + skip_weight[0][None, :] * product)
    gated = gated.astype(jnp.bfloat16)[None]
    return from_behind(gated, "segment", 1)


def split_two(value):
    high = value.astype(BF16)
    return high, (value - high.astype(F32)).astype(BF16)


def split_table(table):
    table = table.astype(np.float32)
    high = table.astype(jnp.bfloat16)
    low = (table - high.astype(np.float32)).astype(jnp.bfloat16)
    return np.concatenate([high, high, low], axis=1)


def stacked(value):
    high, low = split_two(value)
    return jnp.concatenate([high, low, high], axis=0)


def lower_half(shape):
    return lax.broadcasted_iota(jnp.int32, shape, len(shape) - 1) < HALF


def swap_halves(value):
    return pltpu.roll(value, HALF, value.ndim - 1)


def tables(outer):
    total = outer * INNER
    a = np.arange(outer)
    b = np.arange(INNER)
    c = np.arange(outer) + 0.25
    first = 2.0 * np.pi * np.outer(c, a) / outer
    second = 2.0 * np.pi * np.outer(b, b) / INNER
    forward_a = split_table(np.concatenate([np.cos(first), -np.sin(first)], axis=0))
    forward_b = split_table(
        np.block([[np.cos(second), np.sin(second)], [-np.sin(second), np.cos(second)]])
    )
    back_b = split_table(np.concatenate([np.cos(second), np.sin(second)], axis=0))
    back_a = split_table(np.concatenate([np.cos(first).T, -np.sin(first).T], axis=0) / total)

    def turns(steps):
        theta = 2.0 * np.pi * np.outer(steps, c) / total
        wide = np.stack([np.cos(theta), np.sin(theta)], axis=1).astype(np.float32)
        return np.ascontiguousarray(np.broadcast_to(wide[..., None], wide.shape + (LANES,)))

    return forward_a, forward_b, back_b, back_a, turns(b), turns(np.concatenate([b[:STEP], b[::STEP]]))


def fetched(sources, targets, sems):
    copies = [pltpu.make_async_copy(a, b, sems.at[i]) for i, (a, b) in enumerate(zip(sources, targets))]
    for copy in copies:
        copy.start()
    return copies


def pack_kernel(parts, index_ref, *refs):
    sources, outs, held, arrived, sems = refs[:3], refs[3 : 3 + parts], refs[-5], refs[-4:-1], refs[-1]
    k_ref, v_ref, h_ref = arrived
    rows = k_ref.shape[0] // 2
    low = lower_half((rows, LANES))
    for copy in fetched(sources, arrived, sems):
        copy.wait()

    def place(e, at, tile, low):
        half = tile.shape[0] // 2
        early, late = tile[:half], tile[half:]
        held[2 * e, at : at + half, :] = jnp.where(low, early, swap_halves(late)).astype(BF16)
        held[2 * e + 1, at : at + half, :] = jnp.where(low, swap_halves(early), late).astype(BF16)

    for e in range(parts // 2):
        lanes = slice(LANES * e, LANES * (e + 1))
        product = k_ref[:, lanes].astype(F32) * v_ref[:, lanes].astype(F32)
        largest = jnp.max(jnp.abs(product), axis=0, keepdims=True)
        largest = jnp.maximum(largest * 1.01, SMALLEST).astype(BF16).astype(F32)
        code = product * (SCALE / largest)
        power = code * code
        for _ in range(DOUBLINGS - 1):
            power = power * power
        place(e, 0, jnp.where(code < 0.0, -power, power), low)
        place(e, rows, h_ref[:, lanes].astype(F32), low)
        place(e, 2 * rows, jnp.broadcast_to(largest, (2 * EXTRA, LANES)), low[:EXTRA])
    for n, out in enumerate(outs):
        out[...] = held[lax.rem(index_ref[0] + n, parts)]


def pack_gate_kernel(parts, q_ref, out_ref):
    rows = q_ref.shape[0] // 2
    low = lower_half((rows, LANES))
    for e in range(parts // 2):
        tile = q_ref[:, LANES * e : LANES * (e + 1)].astype(F32)
        early, late = tile[:rows], tile[rows:]
        out_ref[2 * e] = jnp.where(low, early, swap_halves(late)).astype(BF16)
        out_ref[2 * e + 1] = jnp.where(low, swap_halves(early), late).astype(BF16)


def hold_kernel(*refs):
    half = len(refs) // 2
    for source, target in zip(refs[:half], refs[half:]):
        target[...] = source[...]


def longest_first(parts):
    return sorted(range(parts), key=lambda n: abs(n - parts // 2))


def unpack_kernel(parts, index_ref, *refs):
    blocks, out_ref, held = refs[:parts], refs[parts], refs[parts + 1]
    rows = held.shape[1]
    low = lower_half((rows, LANES))
    for n, block in zip(longest_first(parts), blocks):
        held[lax.rem(index_ref[0] + n, parts)] = block[...]
    for e in range(parts // 2):
        even, odd = held[2 * e].astype(F32), held[2 * e + 1].astype(F32)
        out_ref[:rows, LANES * e : LANES * (e + 1)] = jnp.where(low, even, swap_halves(odd)).astype(BF16)
        out_ref[rows:, LANES * e : LANES * (e + 1)] = jnp.where(low, swap_halves(even), odd).astype(BF16)


def forward_kernel(parts, outer, index_ref, *refs):
    blocks = refs[:parts]
    matrix_ref, turn_ref, z_s, p_s, x_s = refs[parts:]
    rows = p_s.shape[1]
    per = rows // INNER
    low = lower_half((INNER, LANES))

    def origin(n):
        return lax.rem(index_ref[0] + parts - n, parts)

    for n, block in zip(longest_first(parts), blocks):
        scale = block[2 * rows : 2 * rows + EXTRA, :].astype(F32)[:1] * (1.0 / SCALE)
        for m in range(per):
            at = m * INNER
            code = block[at : at + INNER, :].astype(F32)
            size = jnp.exp(jnp.log(jnp.abs(code)) * (0.5**DOUBLINGS)) * scale
            p = jnp.where(code == 0.0, 0.0, jnp.where(code < 0.0, -size, size))
            p_s[n, at : at + INNER, :] = p
            h = block[rows + at : rows + at + INNER, :].astype(F32)
            a = origin(n) * (2 * per) + m
            x_s[pl.ds(a, INNER, stride=outer + PAD), :] = jnp.where(low, p, swap_halves(h))
            x_s[pl.ds(a + per, INNER, stride=outer + PAD), :] = jnp.where(low, swap_halves(p), h)

    def turn(group, n):
        cos_1, sin_1 = turn_ref[STEP + group, 0], turn_ref[STEP + group, 1]
        if n == 0:
            return cos_1, sin_1
        cos_2, sin_2 = turn_ref[n, 0], turn_ref[n, 1]
        return cos_1 * cos_2 - sin_1 * sin_2, sin_1 * cos_2 + cos_1 * sin_2

    def forward_outer(group, carry):
        for n in range(0, STEP, WIDE):
            b = group * STEP + n
            data = jnp.concatenate(
                [
                    stacked(x_s[pl.ds(pl.multiple_of((b + j) * (outer + PAD), PAD), outer), :])
                    for j in range(WIDE)
                ],
                axis=1,
            )
            both = jnp.dot(matrix_ref[...], data, preferred_element_type=F32)
            for j in range(WIDE):
                re = both[:outer, LANES * j : LANES * (j + 1)]
                im = both[outer:, LANES * j : LANES * (j + 1)]
                cos, sin = turn(group, n + j)
                z_s[pl.ds(b + j, outer, stride=2 * INNER + PAD), :] = re * cos + im * sin
                z_s[pl.ds(b + j + INNER, outer, stride=2 * INNER + PAD), :] = im * cos - re * sin
        return carry

    lax.fori_loop(0, INNER // STEP, forward_outer, 0)


def middle_kernel(outer, z_s, forward_ref, back_ref, w_s):
    low = lower_half((INNER, LANES))

    def middle(group, carry):
        for n in range(0, STEP, WIDE):
            c = group * STEP + n
            data = jnp.concatenate(
                [
                    stacked(z_s[pl.ds(pl.multiple_of((c + j) * (2 * INNER + PAD), PAD), 2 * INNER), :])
                    for j in range(WIDE)
                ],
                axis=1,
            )
            both = jnp.dot(forward_ref[...], data, preferred_element_type=F32)
            mixed = []
            for j in range(WIDE):
                re = both[:INNER, LANES * j : LANES * (j + 1)]
                im = both[INNER:, LANES * j : LANES * (j + 1)]
                re_2, im_2 = swap_halves(re), swap_halves(im)
                mixed.append(
                    stacked(jnp.where(low, re * re_2 - im * im_2, re * im_2 + im * re_2))
                )
            both = jnp.dot(back_ref[...], jnp.concatenate(mixed, axis=1), preferred_element_type=F32)
            for j in range(WIDE):
                straight = both[:INNER, LANES * j : LANES * (j + 1)]
                crossed = swap_halves(both[INNER:, LANES * j : LANES * (j + 1)])
                w_s[pl.ds(c + j, INNER, stride=outer + PAD), :] = jnp.where(
                    low, straight - crossed, straight + crossed
                )
        return carry

    lax.fori_loop(0, outer // STEP, middle, 0)


def back_kernel(parts, outer, index_ref, skip_ref, w_s, p_s, *refs):
    matrix_ref, turn_ref, out_ref, y_s = refs
    rows = out_ref.shape[1]
    lowc = lower_half((outer, LANES))

    def origin(n):
        return lax.rem(index_ref[0] + parts - n, parts)

    def turn(group, n):
        return turn_ref[group * STEP + n, 0], turn_ref[group * STEP + n, 1]

    def back_outer(group, carry):
        for n in range(0, STEP, WIDE):
            b = group * STEP + n
            data = []
            for j in range(WIDE):
                value = w_s[pl.ds(pl.multiple_of((b + j) * (outer + PAD), PAD), outer), :]
                cos, sin = turn(group, n + j)
                other = swap_halves(value) * sin
                straight = value * cos
                data.append(stacked(jnp.where(lowc, straight - other, straight + other)))
            both = jnp.dot(matrix_ref[...], jnp.concatenate(data, axis=1), preferred_element_type=F32)
            for j in range(WIDE):
                re = both[:outer, LANES * j : LANES * (j + 1)]
                im = both[outer:, LANES * j : LANES * (j + 1)]
                y_s[pl.ds(b + j, outer, stride=INNER), :] = re + swap_halves(im)
        return carry

    lax.fori_loop(0, INNER // STEP, back_outer, 0)

    lowr = lower_half((rows, LANES))
    pair = pl.multiple_of(index_ref[0] // 2 * LANES, LANES)
    wide = skip_ref[:, pl.ds(pair, LANES)]
    mine = lower_half((1, LANES)) == (index_ref[0] % 2 == 0)
    skip = jnp.where(mine, wide, swap_halves(wide))
    for n in range(parts):
        at = pl.multiple_of(origin(n) * 2 * rows, 2 * rows)
        early = y_s[pl.ds(at, rows), :]
        late = y_s[pl.ds(at + rows, rows), :]
        out_ref[n] = jnp.where(lowr, early, swap_halves(late)) + skip * p_s[n]


def gate_kernel(parts, index_ref, y_ref, q_ref, *outs):
    for n, out in enumerate(outs):
        q = q_ref[lax.rem(index_ref[0] + parts - n, parts)]
        out[...] = (q.astype(F32) * y_ref[n]).astype(BF16)


def joint_shift(value, segment_step, ctx_step):
    segments, parts = lax.axis_size("segment"), lax.axis_size("ctx")
    pairs = [
        (s * parts + c, (s + segment_step) % segments * parts + (c + ctx_step) % parts)
        for s in range(segments)
        for c in range(parts)
    ]
    return lax.ppermute(value, ("segment", "ctx"), pairs)


def convolved(parts, length, index, slabs, skip_weight, consts):
    rows = length // 2
    outer = parts * length // INNER
    first_turns, forward_a, turns, forward_b, back_b, back_a = consts
    scalar = pl.BlockSpec(memory_space=pltpu.SMEM)
    whole = pl.BlockSpec(memory_space=pltpu.VMEM)

    def block(*shape):
        return jax.ShapeDtypeStruct(shape, F32)

    z, p = pl.pallas_call(
        functools.partial(forward_kernel, parts, outer),
        out_shape=(block(outer * (2 * INNER + PAD), LANES), block(parts, rows, LANES)),
        in_specs=[scalar] + [whole] * (parts + 2),
        scratch_shapes=[pltpu.VMEM((INNER * (outer + PAD), LANES), F32)],
        compiler_params=pltpu.CompilerParams(vmem_limit_bytes=LIMIT * 2**20),
    )(index, *[slabs[n] for n in longest_first(parts)], forward_a, first_turns)
    w = pl.pallas_call(
        functools.partial(middle_kernel, outer),
        out_shape=block(INNER * (outer + PAD), LANES),
        compiler_params=pltpu.CompilerParams(vmem_limit_bytes=LIMIT * 2**20),
    )(z, forward_b, back_b)
    return pl.pallas_call(
        functools.partial(back_kernel, parts, outer),
        out_shape=block(parts, rows, LANES),
        in_specs=[scalar] + [whole] * 5,
        scratch_shapes=[pltpu.VMEM((outer * INNER, LANES), F32)],
        compiler_params=pltpu.CompilerParams(vmem_limit_bytes=LIMIT * 2**20),
    )(index, skip_weight, w, p, back_a, turns)


def fast_on_device(query_stream, key_stream, value_stream, filter_taps, skip_weight):
    parts = lax.axis_size("ctx")
    device = lax.axis_index("ctx")
    length, channels = query_stream.shape[1:]
    rows = length // 2
    index = jnp.full((1,), device, jnp.int32)
    scalar = pl.BlockSpec(memory_space=pltpu.SMEM)
    whole = pl.BlockSpec(memory_space=pltpu.VMEM)
    far = pl.BlockSpec(memory_space=pltpu.HBM)
    small = pltpu.CompilerParams(vmem_limit_bytes=24 * 2**20)
    large = pltpu.CompilerParams(vmem_limit_bytes=60 * 2**20)

    def block(*shape, dtype=BF16):
        return jax.ShapeDtypeStruct(shape, dtype)

    size = 2 * rows + EXTRA
    sent = pl.pallas_call(
        functools.partial(pack_kernel, parts),
        out_shape=(block(size, LANES),) * parts,
        in_specs=[scalar] + [far] * 3,
        scratch_shapes=[pltpu.VMEM((parts, size, LANES), BF16)]
        + [pltpu.VMEM((length, channels), BF16)] * 3
        + [pltpu.SemaphoreType.DMA((3,))],
        compiler_params=large,
    )(index, key_stream[0], value_stream[0], filter_taps[0])
    slabs = {n: joint_shift(sent[n], 0, n) for n in longest_first(parts) if n}
    q = pl.pallas_call(
        functools.partial(pack_gate_kernel, parts),
        out_shape=block(parts, rows, LANES),
        compiler_params=large,
    )(query_stream[0])
    forward_a, forward_b, back_b, back_a, turns, two_turns = [
        jnp.asarray(t) for t in tables(parts * length // INNER)
    ]
    held = (sent[0], forward_a)
    held = pl.pallas_call(
        hold_kernel,
        out_shape=tuple(jax.ShapeDtypeStruct(x.shape, x.dtype) for x in held),
        compiler_params=small,
    )(*held)
    q, *_ = lax.optimization_barrier((q, *slabs.values(), *held))
    slabs[0] = held[0]
    consts = (two_turns, held[1], turns, forward_b, back_b, back_a)
    q = lax.all_to_all(q, "ctx", split_axis=0, concat_axis=0, tiled=True)
    y = convolved(parts, length, index, slabs, skip_weight, consts)
    gated = pl.pallas_call(
        functools.partial(gate_kernel, parts),
        out_shape=(block(rows, LANES),) * parts,
        in_specs=[scalar, whole, whole],
        compiler_params=small,
    )(index, y, q)
    gated = [joint_shift(gated[n], 1, -n) for n in longest_first(parts)]
    out = pl.pallas_call(
        functools.partial(unpack_kernel, parts),
        out_shape=block(length, channels),
        in_specs=[scalar] + [whole] * parts,
        scratch_shapes=[pltpu.VMEM((parts, rows, LANES), BF16)],
        compiler_params=small,
    )(index, *gated)
    return out[None]


def solution(mesh):
    placed = (
        P("segment", "ctx", None),
        P("segment", "ctx", None),
        P("segment", "ctx", None),
        P("segment", "ctx", None),
        P("segment", None),
    )

    def on_device(*arrays):
        parts = lax.axis_size("ctx")
        length, channels = arrays[0].shape[1:]
        square = parts * length == INNER * INNER
        run = fast_on_device if square and channels == parts * HALF else general_on_device
        return run(*arrays)

    return jax.shard_map(
        on_device, mesh=mesh, in_specs=placed, out_specs=P("segment", "ctx", None), check_vma=False
    )
```

```python
import functools
import math

import jax
import jax.numpy as jnp
import numpy as np
from jax import lax
from jax.experimental import pallas as pl
from jax.experimental.pallas import tpu as pltpu
from jax.sharding import PartitionSpec as P

HIGHEST = lax.Precision.HIGHEST
LANES = 128
HALF = 64
INNER = 64
STEP = 16
EXTRA = 16
DOUBLINGS = 4
SCALE = 215.0
SMALLEST = 1e-30
LIMIT = 30
PAD = 8
WIDE = 16
F32 = jnp.float32
BF16 = jnp.bfloat16


def from_behind(value, axis, steps):
    count = lax.axis_size(axis)
    pairs = [(source, (source + steps) % count) for source in range(count)]
    return lax.ppermute(value, axis, pairs)


def angles(modulus, left, right):
    phase = left[:, None] * right[None, :] % modulus
    theta = phase.astype(jnp.float32) * (2.0 * math.pi / modulus)
    return (jnp.cos(theta), jnp.sin(theta))


def frequency_order(width):
    rows = jnp.arange(2 * width, dtype=jnp.int32)
    halves = rows // 2
    return jnp.where(rows % 2 == 0, halves, jnp.where(halves == 0, width, 2 * width - halves))


def across(table, data):
    return jnp.einsum("rd,dsc->rsc", table, data, precision=HIGHEST)


def along(table, data):
    return jnp.einsum("kb,rbc->rkc", table, data, precision=HIGHEST)


def rotate(real_part, imag_part, cosine, sine):
    return (real_part * cosine + imag_part * sine, imag_part * cosine - real_part * sine)


def general_on_device(query_stream, key_stream, value_stream, filter_taps, skip_weight):
    parts = lax.axis_size("ctx")
    device = lax.axis_index("ctx")
    length = query_stream.shape[1]
    channels = query_stream.shape[2]
    share = length // parts
    total = 2 * parts * length
    product = key_stream[0].astype(jnp.float32) * value_stream[0].astype(jnp.float32)
    taps = filter_taps[0].astype(jnp.float32)
    block_prod, block_taps = (
        lax.all_to_all(
            product.reshape(1, length, channels), "ctx", split_axis=1, concat_axis=0, tiled=True
        ),
        lax.all_to_all(
            taps.reshape(1, length, channels), "ctx", split_axis=1, concat_axis=0, tiled=True
        ),
    )
    order = frequency_order(parts)
    cos_cross, sin_cross = angles(2 * parts, order, jnp.arange(parts, dtype=jnp.int32))
    positions = device * share + jnp.arange(share, dtype=jnp.int32)
    cos_twist, sin_twist = angles(total, order, positions)
    cos_twist = cos_twist[:, :, None]
    sin_twist = sin_twist[:, :, None]
    span = jnp.arange(length, dtype=jnp.int32)
    cos_along, sin_along = angles(length, span, span)
    local_rows = lax.dynamic_slice(order, (2 * device,), (2,))
    cos_back, sin_back = angles(total, local_rows, span)
    cos_back = cos_back[:, :, None]
    sin_back = sin_back[:, :, None]

    def forward_along(real_part, imag_part):
        return (
            along(cos_along, real_part) + along(sin_along, imag_part),
            along(cos_along, imag_part) - along(sin_along, real_part),
        )

    prod_real, prod_imag = rotate(
        across(cos_cross, block_prod), -across(sin_cross, block_prod), cos_twist, sin_twist
    )
    taps_real, taps_imag = rotate(
        across(cos_cross, block_taps), -across(sin_cross, block_taps), cos_twist, sin_twist
    )
    first_real, first_imag = forward_along(
        lax.all_to_all(prod_real, "ctx", split_axis=0, concat_axis=1, tiled=True),
        lax.all_to_all(prod_imag, "ctx", split_axis=0, concat_axis=1, tiled=True),
    )
    second_real, second_imag = forward_along(
        lax.all_to_all(taps_real, "ctx", split_axis=0, concat_axis=1, tiled=True),
        lax.all_to_all(taps_imag, "ctx", split_axis=0, concat_axis=1, tiled=True),
    )
    result_real = first_real * second_real - first_imag * second_imag
    result_imag = first_real * second_imag + first_imag * second_real
    back_real = along(cos_along, result_real) - along(sin_along, result_imag)
    back_imag = along(cos_along, result_imag) + along(sin_along, result_real)
    spec_real, spec_imag = rotate(back_real, back_imag, cos_back, -sin_back)
    rows_real, rows_imag = (
        lax.all_to_all(spec_real, "ctx", split_axis=1, concat_axis=0, tiled=True),
        lax.all_to_all(spec_imag, "ctx", split_axis=1, concat_axis=0, tiled=True),
    )
    cos_final, sin_final = angles(2 * parts, jnp.arange(parts, dtype=jnp.int32), order)
    by_block = jnp.einsum("dr,rsc->dsc", cos_final, rows_real, precision=HIGHEST) - jnp.einsum(
        "dr,rsc->dsc", sin_final, rows_imag, precision=HIGHEST
    )
    by_block = by_block * (1.0 / total)
    convolved = lax.all_to_all(by_block, "ctx", split_axis=0, concat_axis=1, tiled=True)[0]
    gated = query_stream[0].astype(jnp.float32) * (convolved + skip_weight[0][None, :] * product)
    gated = gated.astype(jnp.bfloat16)[None]
    return from_behind(gated, "segment", 1)


def split_two(value):
    high = value.astype(BF16)
    return high, (value - high.astype(F32)).astype(BF16)


def split_table(table):
    table = table.astype(np.float32)
    high = table.astype(jnp.bfloat16)
    low = (table - high.astype(np.float32)).astype(jnp.bfloat16)
    return np.concatenate([high, high, low], axis=1)


def stacked(value):
    high, low = split_two(value)
    return jnp.concatenate([high, low, high], axis=0)


def lower_half(shape):
    return lax.broadcasted_iota(jnp.int32, shape, len(shape) - 1) < HALF


def swap_halves(value):
    return pltpu.roll(value, HALF, value.ndim - 1)


def tables(outer):
    total = outer * INNER
    a = np.arange(outer)
    b = np.arange(INNER)
    c = np.arange(outer) + 0.25
    first = 2.0 * np.pi * np.outer(c, a) / outer
    second = 2.0 * np.pi * np.outer(b, b) / INNER
    forward_a = split_table(np.concatenate([np.cos(first), -np.sin(first)], axis=0))
    forward_b = split_table(
        np.block([[np.cos(second), np.sin(second)], [-np.sin(second), np.cos(second)]])
    )
    back_b = split_table(np.concatenate([np.cos(second), np.sin(second)], axis=0))
    back_a = split_table(np.concatenate([np.cos(first).T, -np.sin(first).T], axis=0) / total)

    def turns(steps):
        theta = 2.0 * np.pi * np.outer(steps, c) / total
        wide = np.stack([np.cos(theta), np.sin(theta)], axis=1).astype(np.float32)
        return np.ascontiguousarray(np.broadcast_to(wide[..., None], wide.shape + (LANES,)))

    return forward_a, forward_b, back_b, back_a, turns(b), turns(np.concatenate([b[:STEP], b[::STEP]]))


def fetched(sources, targets, sems):
    copies = [pltpu.make_async_copy(a, b, sems.at[i]) for i, (a, b) in enumerate(zip(sources, targets))]
    for copy in copies:
        copy.start()
    return copies


def pack_kernel(parts, index_ref, *refs):
    sources, outs, held, arrived, sems = refs[:3], refs[3 : 3 + parts], refs[-5], refs[-4:-1], refs[-1]
    k_ref, v_ref, h_ref = arrived
    rows = k_ref.shape[0] // 2
    low = lower_half((rows, LANES))
    tiles = [slice(LANES * e, LANES * (e + 1)) for e in range(parts // 2)]
    copies = fetched(
        [x.at[:, t] for t in tiles for x in sources], [x.at[:, t] for t in tiles for x in arrived], sems
    )

    def place(e, at, tile, low):
        half = tile.shape[0] // 2
        early, late = tile[:half], tile[half:]
        held[2 * e, at : at + half, :] = jnp.where(low, early, swap_halves(late)).astype(BF16)
        held[2 * e + 1, at : at + half, :] = jnp.where(low, swap_halves(early), late).astype(BF16)

    for e in range(parts // 2):
        lanes = tiles[e]
        for copy in copies[3 * e : 3 * e + 3]:
            copy.wait()
        product = k_ref[:, lanes].astype(F32) * v_ref[:, lanes].astype(F32)
        largest = jnp.max(jnp.abs(product), axis=0, keepdims=True)
        largest = jnp.maximum(largest * 1.01, SMALLEST).astype(BF16).astype(F32)
        code = product * (SCALE / largest)
        power = code * code
        for _ in range(DOUBLINGS - 1):
            power = power * power
        place(e, 0, jnp.where(code < 0.0, -power, power), low)
        place(e, rows, h_ref[:, lanes].astype(F32), low)
        place(e, 2 * rows, jnp.broadcast_to(largest, (2 * EXTRA, LANES)), low[:EXTRA])
    for n, out in enumerate(outs):
        out[...] = held[lax.rem(index_ref[0] + n, parts)]


def pack_gate_kernel(parts, q_ref, out_ref):
    rows = q_ref.shape[0] // 2
    low = lower_half((rows, LANES))
    for e in range(parts // 2):
        tile = q_ref[:, LANES * e : LANES * (e + 1)].astype(F32)
        early, late = tile[:rows], tile[rows:]
        out_ref[2 * e] = jnp.where(low, early, swap_halves(late)).astype(BF16)
        out_ref[2 * e + 1] = jnp.where(low, swap_halves(early), late).astype(BF16)


def hold_kernel(*refs):
    half = len(refs) // 2
    for source, target in zip(refs[:half], refs[half:]):
        target[...] = source[...]


def unpack_kernel(parts, index_ref, *refs):
    blocks, out_ref, held = refs[:parts], refs[parts], refs[parts + 1]
    rows = held.shape[1]
    low = lower_half((rows, LANES))
    for n, block in enumerate(blocks):
        held[lax.rem(index_ref[0] + n, parts)] = block[...]
    for e in range(parts // 2):
        even, odd = held[2 * e].astype(F32), held[2 * e + 1].astype(F32)
        out_ref[:rows, LANES * e : LANES * (e + 1)] = jnp.where(low, even, swap_halves(odd)).astype(BF16)
        out_ref[rows:, LANES * e : LANES * (e + 1)] = jnp.where(low, swap_halves(even), odd).astype(BF16)


def forward_kernel(parts, outer, index_ref, *refs):
    blocks = refs[:parts]
    matrix_ref, turn_ref, z_s, p_s, x_s = refs[parts:]
    rows = p_s.shape[1]
    per = rows // INNER
    low = lower_half((INNER, LANES))

    def origin(n):
        return lax.rem(index_ref[0] + parts - n, parts)

    for n, block in enumerate(blocks):
        scale = block[2 * rows : 2 * rows + EXTRA, :].astype(F32)[:1] * (1.0 / SCALE)
        for m in range(per):
            at = m * INNER
            code = block[at : at + INNER, :].astype(F32)
            size = jnp.exp(jnp.log(jnp.abs(code)) * (0.5**DOUBLINGS)) * scale
            p = jnp.where(code == 0.0, 0.0, jnp.where(code < 0.0, -size, size))
            p_s[n, at : at + INNER, :] = p
            h = block[rows + at : rows + at + INNER, :].astype(F32)
            a = origin(n) * (2 * per) + m
            x_s[pl.ds(a, INNER, stride=outer + PAD), :] = jnp.where(low, p, swap_halves(h))
            x_s[pl.ds(a + per, INNER, stride=outer + PAD), :] = jnp.where(low, swap_halves(p), h)

    def turn(group, n):
        cos_1, sin_1 = turn_ref[STEP + group, 0], turn_ref[STEP + group, 1]
        if n == 0:
            return cos_1, sin_1
        cos_2, sin_2 = turn_ref[n, 0], turn_ref[n, 1]
        return cos_1 * cos_2 - sin_1 * sin_2, sin_1 * cos_2 + cos_1 * sin_2

    def forward_outer(group, carry):
        for n in range(0, STEP, WIDE):
            b = group * STEP + n
            data = jnp.concatenate(
                [
                    stacked(x_s[pl.ds(pl.multiple_of((b + j) * (outer + PAD), PAD), outer), :])
                    for j in range(WIDE)
                ],
                axis=1,
            )
            both = jnp.dot(matrix_ref[...], data, preferred_element_type=F32)
            for j in range(WIDE):
                re = both[:outer, LANES * j : LANES * (j + 1)]
                im = both[outer:, LANES * j : LANES * (j + 1)]
                cos, sin = turn(group, n + j)
                z_s[pl.ds(b + j, outer, stride=2 * INNER + PAD), :] = re * cos + im * sin
                z_s[pl.ds(b + j + INNER, outer, stride=2 * INNER + PAD), :] = im * cos - re * sin
        return carry

    lax.fori_loop(0, INNER // STEP, forward_outer, 0)


def middle_kernel(outer, z_s, forward_ref, back_ref, w_s):
    low = lower_half((INNER, LANES))

    def middle(group, carry):
        for n in range(0, STEP, WIDE):
            c = group * STEP + n
            data = jnp.concatenate(
                [
                    stacked(z_s[pl.ds(pl.multiple_of((c + j) * (2 * INNER + PAD), PAD), 2 * INNER), :])
                    for j in range(WIDE)
                ],
                axis=1,
            )
            both = jnp.dot(forward_ref[...], data, preferred_element_type=F32)
            mixed = []
            for j in range(WIDE):
                re = both[:INNER, LANES * j : LANES * (j + 1)]
                im = both[INNER:, LANES * j : LANES * (j + 1)]
                re_2, im_2 = swap_halves(re), swap_halves(im)
                mixed.append(
                    stacked(jnp.where(low, re * re_2 - im * im_2, re * im_2 + im * re_2))
                )
            both = jnp.dot(back_ref[...], jnp.concatenate(mixed, axis=1), preferred_element_type=F32)
            for j in range(WIDE):
                straight = both[:INNER, LANES * j : LANES * (j + 1)]
                crossed = swap_halves(both[INNER:, LANES * j : LANES * (j + 1)])
                w_s[pl.ds(c + j, INNER, stride=outer + PAD), :] = jnp.where(
                    low, straight - crossed, straight + crossed
                )
        return carry

    lax.fori_loop(0, outer // STEP, middle, 0)


def back_kernel(parts, outer, index_ref, skip_ref, w_s, p_s, *refs):
    matrix_ref, turn_ref, out_ref, y_s = refs
    rows = out_ref.shape[1]
    lowc = lower_half((outer, LANES))

    def origin(n):
        return lax.rem(index_ref[0] + parts - n, parts)

    def turn(group, n):
        return turn_ref[group * STEP + n, 0], turn_ref[group * STEP + n, 1]

    def back_outer(group, carry):
        for n in range(0, STEP, WIDE):
            b = group * STEP + n
            data = []
            for j in range(WIDE):
                value = w_s[pl.ds(pl.multiple_of((b + j) * (outer + PAD), PAD), outer), :]
                cos, sin = turn(group, n + j)
                other = swap_halves(value) * sin
                straight = value * cos
                data.append(stacked(jnp.where(lowc, straight - other, straight + other)))
            both = jnp.dot(matrix_ref[...], jnp.concatenate(data, axis=1), preferred_element_type=F32)
            for j in range(WIDE):
                re = both[:outer, LANES * j : LANES * (j + 1)]
                im = both[outer:, LANES * j : LANES * (j + 1)]
                y_s[pl.ds(b + j, outer, stride=INNER + PAD), :] = re + swap_halves(im)
        return carry

    lax.fori_loop(0, INNER // STEP, back_outer, 0)

    lowr = lower_half((INNER, LANES))
    pair = pl.multiple_of(index_ref[0] // 2 * LANES, LANES)
    wide = skip_ref[:, pl.ds(pair, LANES)]
    mine = lower_half((1, LANES)) == (index_ref[0] % 2 == 0)
    skip = jnp.where(mine, wide, swap_halves(wide))
    per = rows // INNER
    for n in range(parts):
        for m in range(per):
            a = origin(n) * 2 * per + m
            early = y_s[pl.ds(pl.multiple_of(a * (INNER + PAD), PAD), INNER), :]
            late = y_s[pl.ds(pl.multiple_of((a + per) * (INNER + PAD), PAD), INNER), :]
            span = slice(m * INNER, (m + 1) * INNER)
            out_ref[n, span, :] = jnp.where(lowr, early, swap_halves(late)) + skip * p_s[n, span, :]


def gate_kernel(parts, index_ref, y_ref, q_ref, *outs):
    for n, out in enumerate(outs):
        q = q_ref[lax.rem(index_ref[0] + parts - n, parts)]
        out[...] = (q.astype(F32) * y_ref[n]).astype(BF16)


def joint_shift(value, segment_step, ctx_step):
    segments, parts = lax.axis_size("segment"), lax.axis_size("ctx")
    pairs = [
        (s * parts + c, (s + segment_step) % segments * parts + (c + ctx_step) % parts)
        for s in range(segments)
        for c in range(parts)
    ]
    return lax.ppermute(value, ("segment", "ctx"), pairs)


def convolved(parts, length, index, slabs, skip_weight, consts):
    rows = length // 2
    outer = parts * length // INNER
    first_turns, forward_a, turns, forward_b, back_b, back_a = consts
    scalar = pl.BlockSpec(memory_space=pltpu.SMEM)
    whole = pl.BlockSpec(memory_space=pltpu.VMEM)

    def block(*shape):
        return jax.ShapeDtypeStruct(shape, F32)

    z, p = pl.pallas_call(
        functools.partial(forward_kernel, parts, outer),
        out_shape=(block(outer * (2 * INNER + PAD), LANES), block(parts, rows, LANES)),
        in_specs=[scalar] + [whole] * (parts + 2),
        scratch_shapes=[pltpu.VMEM((INNER * (outer + PAD), LANES), F32)],
        compiler_params=pltpu.CompilerParams(vmem_limit_bytes=LIMIT * 2**20),
    )(index, *slabs, forward_a, first_turns)
    w = pl.pallas_call(
        functools.partial(middle_kernel, outer),
        out_shape=block(INNER * (outer + PAD), LANES),
        compiler_params=pltpu.CompilerParams(vmem_limit_bytes=LIMIT * 2**20),
    )(z, forward_b, back_b)
    return pl.pallas_call(
        functools.partial(back_kernel, parts, outer),
        out_shape=block(parts, rows, LANES),
        in_specs=[scalar] + [whole] * 5,
        scratch_shapes=[pltpu.VMEM((outer * (INNER + PAD), LANES), F32)],
        compiler_params=pltpu.CompilerParams(vmem_limit_bytes=LIMIT * 2**20),
    )(index, skip_weight, w, p, back_a, turns)


def fast_on_device(query_stream, key_stream, value_stream, filter_taps, skip_weight):
    parts = lax.axis_size("ctx")
    device = lax.axis_index("ctx")
    length, channels = query_stream.shape[1:]
    rows = length // 2
    index = jnp.full((1,), device, jnp.int32)
    scalar = pl.BlockSpec(memory_space=pltpu.SMEM)
    whole = pl.BlockSpec(memory_space=pltpu.VMEM)
    far = pl.BlockSpec(memory_space=pltpu.HBM)
    small = pltpu.CompilerParams(vmem_limit_bytes=24 * 2**20)
    large = pltpu.CompilerParams(vmem_limit_bytes=60 * 2**20)

    def block(*shape, dtype=BF16):
        return jax.ShapeDtypeStruct(shape, dtype)

    size = 2 * rows + EXTRA
    sent = pl.pallas_call(
        functools.partial(pack_kernel, parts),
        out_shape=(block(size, LANES),) * parts,
        in_specs=[scalar] + [far] * 3,
        scratch_shapes=[pltpu.VMEM((parts, size, LANES), BF16)]
        + [pltpu.VMEM((length, channels), BF16)] * 3
        + [pltpu.SemaphoreType.DMA((3 * parts // 2,))],
        compiler_params=large,
    )(index, key_stream[0], value_stream[0], filter_taps[0])
    slabs = [sent[0]] + [joint_shift(sent[n], 0, n) for n in range(1, parts)]
    q = pl.pallas_call(
        functools.partial(pack_gate_kernel, parts),
        out_shape=block(parts, rows, LANES),
        compiler_params=large,
    )(query_stream[0])
    forward_a, forward_b, back_b, back_a, turns, two_turns = [
        jnp.asarray(t) for t in tables(parts * length // INNER)
    ]
    held = (sent[0], forward_a)
    held = pl.pallas_call(
        hold_kernel,
        out_shape=tuple(jax.ShapeDtypeStruct(x.shape, x.dtype) for x in held),
        compiler_params=small,
    )(*held)
    q, *_ = lax.optimization_barrier((q, *slabs, *held))
    slabs = [held[0]] + slabs[1:]
    consts = (two_turns, held[1], turns, forward_b, back_b, back_a)
    q = lax.all_to_all(q, "ctx", split_axis=0, concat_axis=0, tiled=True)
    y = convolved(parts, length, index, slabs, skip_weight, consts)
    gated = pl.pallas_call(
        functools.partial(gate_kernel, parts),
        out_shape=(block(rows, LANES),) * parts,
        in_specs=[scalar, whole, whole],
        compiler_params=small,
    )(index, y, q)
    gated = [joint_shift(gated[n], 1, -n) for n in range(parts)]
    out = pl.pallas_call(
        functools.partial(unpack_kernel, parts),
        out_shape=block(length, channels),
        in_specs=[scalar] + [whole] * parts,
        scratch_shapes=[pltpu.VMEM((parts, rows, LANES), BF16)],
        compiler_params=small,
    )(index, *gated)
    return out[None]


def solution(mesh):
    placed = (
        P("segment", "ctx", None),
        P("segment", "ctx", None),
        P("segment", "ctx", None),
        P("segment", "ctx", None),
        P("segment", None),
    )

    def on_device(*arrays):
        parts = lax.axis_size("ctx")
        length, channels = arrays[0].shape[1:]
        square = parts * length == INNER * INNER
        run = fast_on_device if square and channels == parts * HALF else general_on_device
        return run(*arrays)

    return jax.shard_map(
        on_device, mesh=mesh, in_specs=placed, out_specs=P("segment", "ctx", None), check_vma=False
    )
```

```python
import functools
import math

import jax
import jax.numpy as jnp
import numpy as np
from jax import lax
from jax.experimental import pallas as pl
from jax.experimental.pallas import tpu as pltpu
from jax.sharding import PartitionSpec as P

HIGHEST = lax.Precision.HIGHEST
LANES = 128
HALF = 64
INNER = 64
STEP = 16
EXTRA = 16
DOUBLINGS = 4
SCALE = 215.0
SMALLEST = 1e-30
LIMIT = 30
PAD = 8
WIDE = 16
F32 = jnp.float32
BF16 = jnp.bfloat16


def from_behind(value, axis, steps):
    count = lax.axis_size(axis)
    pairs = [(source, (source + steps) % count) for source in range(count)]
    return lax.ppermute(value, axis, pairs)


def angles(modulus, left, right):
    phase = left[:, None] * right[None, :] % modulus
    theta = phase.astype(jnp.float32) * (2.0 * math.pi / modulus)
    return (jnp.cos(theta), jnp.sin(theta))


def frequency_order(width):
    rows = jnp.arange(2 * width, dtype=jnp.int32)
    halves = rows // 2
    return jnp.where(rows % 2 == 0, halves, jnp.where(halves == 0, width, 2 * width - halves))


def across(table, data):
    return jnp.einsum("rd,dsc->rsc", table, data, precision=HIGHEST)


def along(table, data):
    return jnp.einsum("kb,rbc->rkc", table, data, precision=HIGHEST)


def rotate(real_part, imag_part, cosine, sine):
    return (real_part * cosine + imag_part * sine, imag_part * cosine - real_part * sine)


def general_on_device(query_stream, key_stream, value_stream, filter_taps, skip_weight):
    parts = lax.axis_size("ctx")
    device = lax.axis_index("ctx")
    length = query_stream.shape[1]
    channels = query_stream.shape[2]
    share = length // parts
    total = 2 * parts * length
    product = key_stream[0].astype(jnp.float32) * value_stream[0].astype(jnp.float32)
    taps = filter_taps[0].astype(jnp.float32)
    block_prod, block_taps = (
        lax.all_to_all(
            product.reshape(1, length, channels), "ctx", split_axis=1, concat_axis=0, tiled=True
        ),
        lax.all_to_all(
            taps.reshape(1, length, channels), "ctx", split_axis=1, concat_axis=0, tiled=True
        ),
    )
    order = frequency_order(parts)
    cos_cross, sin_cross = angles(2 * parts, order, jnp.arange(parts, dtype=jnp.int32))
    positions = device * share + jnp.arange(share, dtype=jnp.int32)
    cos_twist, sin_twist = angles(total, order, positions)
    cos_twist = cos_twist[:, :, None]
    sin_twist = sin_twist[:, :, None]
    span = jnp.arange(length, dtype=jnp.int32)
    cos_along, sin_along = angles(length, span, span)
    local_rows = lax.dynamic_slice(order, (2 * device,), (2,))
    cos_back, sin_back = angles(total, local_rows, span)
    cos_back = cos_back[:, :, None]
    sin_back = sin_back[:, :, None]

    def forward_along(real_part, imag_part):
        return (
            along(cos_along, real_part) + along(sin_along, imag_part),
            along(cos_along, imag_part) - along(sin_along, real_part),
        )

    prod_real, prod_imag = rotate(
        across(cos_cross, block_prod), -across(sin_cross, block_prod), cos_twist, sin_twist
    )
    taps_real, taps_imag = rotate(
        across(cos_cross, block_taps), -across(sin_cross, block_taps), cos_twist, sin_twist
    )
    first_real, first_imag = forward_along(
        lax.all_to_all(prod_real, "ctx", split_axis=0, concat_axis=1, tiled=True),
        lax.all_to_all(prod_imag, "ctx", split_axis=0, concat_axis=1, tiled=True),
    )
    second_real, second_imag = forward_along(
        lax.all_to_all(taps_real, "ctx", split_axis=0, concat_axis=1, tiled=True),
        lax.all_to_all(taps_imag, "ctx", split_axis=0, concat_axis=1, tiled=True),
    )
    result_real = first_real * second_real - first_imag * second_imag
    result_imag = first_real * second_imag + first_imag * second_real
    back_real = along(cos_along, result_real) - along(sin_along, result_imag)
    back_imag = along(cos_along, result_imag) + along(sin_along, result_real)
    spec_real, spec_imag = rotate(back_real, back_imag, cos_back, -sin_back)
    rows_real, rows_imag = (
        lax.all_to_all(spec_real, "ctx", split_axis=1, concat_axis=0, tiled=True),
        lax.all_to_all(spec_imag, "ctx", split_axis=1, concat_axis=0, tiled=True),
    )
    cos_final, sin_final = angles(2 * parts, jnp.arange(parts, dtype=jnp.int32), order)
    by_block = jnp.einsum("dr,rsc->dsc", cos_final, rows_real, precision=HIGHEST) - jnp.einsum(
        "dr,rsc->dsc", sin_final, rows_imag, precision=HIGHEST
    )
    by_block = by_block * (1.0 / total)
    convolved = lax.all_to_all(by_block, "ctx", split_axis=0, concat_axis=1, tiled=True)[0]
    gated = query_stream[0].astype(jnp.float32) * (convolved + skip_weight[0][None, :] * product)
    gated = gated.astype(jnp.bfloat16)[None]
    return from_behind(gated, "segment", 1)


def split_two(value):
    high = value.astype(BF16)
    return high, (value - high.astype(F32)).astype(BF16)


def split_table(table):
    table = table.astype(np.float32)
    high = table.astype(jnp.bfloat16)
    low = (table - high.astype(np.float32)).astype(jnp.bfloat16)
    return np.concatenate([high, high, low], axis=1)


def stacked(value):
    high, low = split_two(value)
    return jnp.concatenate([high, low, high], axis=0)


def lower_half(shape):
    return lax.broadcasted_iota(jnp.int32, shape, len(shape) - 1) < HALF


def swap_halves(value):
    return pltpu.roll(value, HALF, value.ndim - 1)


def tables(outer):
    total = outer * INNER
    a = np.arange(outer)
    b = np.arange(INNER)
    c = np.arange(outer) + 0.25
    first = 2.0 * np.pi * np.outer(c, a) / outer
    second = 2.0 * np.pi * np.outer(b, b) / INNER
    forward_a = split_table(np.concatenate([np.cos(first), -np.sin(first)], axis=0))
    forward_b = split_table(
        np.block([[np.cos(second), np.sin(second)], [-np.sin(second), np.cos(second)]])
    )
    back_b = split_table(np.concatenate([np.cos(second), np.sin(second)], axis=0))
    back_a = split_table(np.concatenate([np.cos(first).T, -np.sin(first).T], axis=0) / total)

    def turns(steps):
        theta = 2.0 * np.pi * np.outer(steps, c) / total
        wide = np.stack([np.cos(theta), np.sin(theta)], axis=1).astype(np.float32)
        return np.ascontiguousarray(np.broadcast_to(wide[..., None], wide.shape + (LANES,)))

    return forward_a, forward_b, back_b, back_a, turns(b), turns(np.concatenate([b[:STEP], b[::STEP]]))


def fetched(sources, targets, sems):
    copies = [pltpu.make_async_copy(a, b, sems.at[i]) for i, (a, b) in enumerate(zip(sources, targets))]
    for copy in copies:
        copy.start()
    return copies


def pack_kernel(parts, index_ref, *refs):
    sources, outs, held, arrived, sems = refs[:3], refs[3 : 3 + parts], refs[-5], refs[-4:-1], refs[-1]
    k_ref, v_ref, h_ref = arrived
    rows = k_ref.shape[0] // 2
    low = lower_half((rows, LANES))
    tiles = [slice(LANES * e, LANES * (e + 1)) for e in range(parts // 2)]
    copies = fetched(
        [x.at[:, t] for t in tiles for x in sources], [x.at[:, t] for t in tiles for x in arrived], sems
    )

    def place(e, at, tile, low):
        half = tile.shape[0] // 2
        early, late = tile[:half], tile[half:]
        held[2 * e, at : at + half, :] = jnp.where(low, early, swap_halves(late)).astype(BF16)
        held[2 * e + 1, at : at + half, :] = jnp.where(low, swap_halves(early), late).astype(BF16)

    for e in range(parts // 2):
        lanes = tiles[e]
        for copy in copies[3 * e : 3 * e + 3]:
            copy.wait()
        product = k_ref[:, lanes].astype(F32) * v_ref[:, lanes].astype(F32)
        largest = jnp.max(jnp.abs(product), axis=0, keepdims=True)
        largest = jnp.maximum(largest * 1.01, SMALLEST).astype(BF16).astype(F32)
        code = product * (SCALE / largest)
        power = code * code
        for _ in range(DOUBLINGS - 1):
            power = power * power
        place(e, 0, jnp.where(code < 0.0, -power, power), low)
        place(e, rows, h_ref[:, lanes].astype(F32), low)
        place(e, 2 * rows, jnp.broadcast_to(largest, (2 * EXTRA, LANES)), low[:EXTRA])
    for n, out in enumerate(outs):
        out[...] = held[lax.rem(index_ref[0] + n, parts)]


def pack_gate_kernel(parts, q_ref, out_ref):
    rows = q_ref.shape[0] // 2
    low = lower_half((rows, LANES))
    for e in range(parts // 2):
        tile = q_ref[:, LANES * e : LANES * (e + 1)].astype(F32)
        early, late = tile[:rows], tile[rows:]
        out_ref[2 * e] = jnp.where(low, early, swap_halves(late)).astype(BF16)
        out_ref[2 * e + 1] = jnp.where(low, swap_halves(early), late).astype(BF16)


def hold_kernel(*refs):
    half = len(refs) // 2
    for source, target in zip(refs[:half], refs[half:]):
        target[...] = source[...]


def longest_first(parts):
    return sorted(range(parts), key=lambda n: abs(n - parts // 2))


def unpack_kernel(parts, index_ref, *refs):
    blocks, out_ref, held = refs[:parts], refs[parts], refs[parts + 1]
    rows = held.shape[1]
    low = lower_half((rows, LANES))
    for n, block in zip(longest_first(parts), blocks):
        held[lax.rem(index_ref[0] + n, parts)] = block[...]
    for e in range(parts // 2):
        even, odd = held[2 * e].astype(F32), held[2 * e + 1].astype(F32)
        out_ref[:rows, LANES * e : LANES * (e + 1)] = jnp.where(low, even, swap_halves(odd)).astype(BF16)
        out_ref[rows:, LANES * e : LANES * (e + 1)] = jnp.where(low, swap_halves(even), odd).astype(BF16)


def forward_kernel(parts, outer, index_ref, *refs):
    blocks = refs[:parts]
    matrix_ref, turn_ref, z_s, p_s, x_s = refs[parts:]
    rows = p_s.shape[1]
    per = rows // INNER
    low = lower_half((INNER, LANES))

    def origin(n):
        return lax.rem(index_ref[0] + parts - n, parts)

    for n, block in enumerate(blocks):
        scale = block[2 * rows : 2 * rows + EXTRA, :].astype(F32)[:1] * (1.0 / SCALE)
        for m in range(per):
            at = m * INNER
            code = block[at : at + INNER, :].astype(F32)
            size = jnp.exp(jnp.log(jnp.abs(code)) * (0.5**DOUBLINGS)) * scale
            p = jnp.where(code == 0.0, 0.0, jnp.where(code < 0.0, -size, size))
            p_s[n, at : at + INNER, :] = p
            h = block[rows + at : rows + at + INNER, :].astype(F32)
            a = origin(n) * (2 * per) + m
            x_s[pl.ds(a, INNER, stride=outer + PAD), :] = jnp.where(low, p, swap_halves(h))
            x_s[pl.ds(a + per, INNER, stride=outer + PAD), :] = jnp.where(low, swap_halves(p), h)

    def turn(group, n):
        cos_1, sin_1 = turn_ref[STEP + group, 0], turn_ref[STEP + group, 1]
        if n == 0:
            return cos_1, sin_1
        cos_2, sin_2 = turn_ref[n, 0], turn_ref[n, 1]
        return cos_1 * cos_2 - sin_1 * sin_2, sin_1 * cos_2 + cos_1 * sin_2

    def forward_outer(group, carry):
        for n in range(0, STEP, WIDE):
            b = group * STEP + n
            data = jnp.concatenate(
                [
                    stacked(x_s[pl.ds(pl.multiple_of((b + j) * (outer + PAD), PAD), outer), :])
                    for j in range(WIDE)
                ],
                axis=1,
            )
            both = jnp.dot(matrix_ref[...], data, preferred_element_type=F32)
            for j in range(WIDE):
                re = both[:outer, LANES * j : LANES * (j + 1)]
                im = both[outer:, LANES * j : LANES * (j + 1)]
                cos, sin = turn(group, n + j)
                z_s[pl.ds(b + j, outer, stride=2 * INNER + PAD), :] = re * cos + im * sin
                z_s[pl.ds(b + j + INNER, outer, stride=2 * INNER + PAD), :] = im * cos - re * sin
        return carry

    lax.fori_loop(0, INNER // STEP, forward_outer, 0)


def middle_kernel(outer, z_s, forward_ref, back_ref, w_s):
    low = lower_half((INNER, LANES))

    def middle(group, carry):
        for n in range(0, STEP, WIDE):
            c = group * STEP + n
            data = jnp.concatenate(
                [
                    stacked(z_s[pl.ds(pl.multiple_of((c + j) * (2 * INNER + PAD), PAD), 2 * INNER), :])
                    for j in range(WIDE)
                ],
                axis=1,
            )
            both = jnp.dot(forward_ref[...], data, preferred_element_type=F32)
            mixed = []
            for j in range(WIDE):
                re = both[:INNER, LANES * j : LANES * (j + 1)]
                im = both[INNER:, LANES * j : LANES * (j + 1)]
                re_2, im_2 = swap_halves(re), swap_halves(im)
                mixed.append(
                    stacked(jnp.where(low, re * re_2 - im * im_2, re * im_2 + im * re_2))
                )
            both = jnp.dot(back_ref[...], jnp.concatenate(mixed, axis=1), preferred_element_type=F32)
            for j in range(WIDE):
                straight = both[:INNER, LANES * j : LANES * (j + 1)]
                crossed = swap_halves(both[INNER:, LANES * j : LANES * (j + 1)])
                w_s[pl.ds(c + j, INNER, stride=outer + PAD), :] = jnp.where(
                    low, straight - crossed, straight + crossed
                )
        return carry

    lax.fori_loop(0, outer // STEP, middle, 0)


def back_kernel(parts, outer, index_ref, skip_ref, w_s, p_s, *refs):
    matrix_ref, turn_ref, out_ref, y_s = refs
    rows = out_ref.shape[1]
    lowc = lower_half((outer, LANES))

    def origin(n):
        return lax.rem(index_ref[0] + parts - n, parts)

    def turn(group, n):
        return turn_ref[group * STEP + n, 0], turn_ref[group * STEP + n, 1]

    def back_outer(group, carry):
        for n in range(0, STEP, WIDE):
            b = group * STEP + n
            data = []
            for j in range(WIDE):
                value = w_s[pl.ds(pl.multiple_of((b + j) * (outer + PAD), PAD), outer), :]
                cos, sin = turn(group, n + j)
                other = swap_halves(value) * sin
                straight = value * cos
                data.append(stacked(jnp.where(lowc, straight - other, straight + other)))
            both = jnp.dot(matrix_ref[...], jnp.concatenate(data, axis=1), preferred_element_type=F32)
            for j in range(WIDE):
                re = both[:outer, LANES * j : LANES * (j + 1)]
                im = both[outer:, LANES * j : LANES * (j + 1)]
                y_s[pl.ds(b + j, outer, stride=INNER + PAD), :] = re + swap_halves(im)
        return carry

    lax.fori_loop(0, INNER // STEP, back_outer, 0)

    lowr = lower_half((INNER, LANES))
    pair = pl.multiple_of(index_ref[0] // 2 * LANES, LANES)
    wide = skip_ref[:, pl.ds(pair, LANES)]
    mine = lower_half((1, LANES)) == (index_ref[0] % 2 == 0)
    skip = jnp.where(mine, wide, swap_halves(wide))
    per = rows // INNER
    for n in range(parts):
        for m in range(per):
            a = origin(n) * 2 * per + m
            early = y_s[pl.ds(pl.multiple_of(a * (INNER + PAD), PAD), INNER), :]
            late = y_s[pl.ds(pl.multiple_of((a + per) * (INNER + PAD), PAD), INNER), :]
            span = slice(m * INNER, (m + 1) * INNER)
            out_ref[n, span, :] = jnp.where(lowr, early, swap_halves(late)) + skip * p_s[n, span, :]


def gate_kernel(parts, index_ref, y_ref, q_ref, *outs):
    for n, out in enumerate(outs):
        q = q_ref[lax.rem(index_ref[0] + parts - n, parts)]
        out[...] = (q.astype(F32) * y_ref[n]).astype(BF16)


def joint_shift(value, segment_step, ctx_step):
    segments, parts = lax.axis_size("segment"), lax.axis_size("ctx")
    pairs = [
        (s * parts + c, (s + segment_step) % segments * parts + (c + ctx_step) % parts)
        for s in range(segments)
        for c in range(parts)
    ]
    return lax.ppermute(value, ("segment", "ctx"), pairs)


def convolved(parts, length, index, slabs, skip_weight, consts):
    rows = length // 2
    outer = parts * length // INNER
    first_turns, forward_a, turns, forward_b, back_b, back_a = consts
    scalar = pl.BlockSpec(memory_space=pltpu.SMEM)
    whole = pl.BlockSpec(memory_space=pltpu.VMEM)

    def block(*shape):
        return jax.ShapeDtypeStruct(shape, F32)

    z, p = pl.pallas_call(
        functools.partial(forward_kernel, parts, outer),
        out_shape=(block(outer * (2 * INNER + PAD), LANES), block(parts, rows, LANES)),
        in_specs=[scalar] + [whole] * (parts + 2),
        scratch_shapes=[pltpu.VMEM((INNER * (outer + PAD), LANES), F32)],
        compiler_params=pltpu.CompilerParams(vmem_limit_bytes=LIMIT * 2**20),
    )(index, *slabs, forward_a, first_turns)
    w = pl.pallas_call(
        functools.partial(middle_kernel, outer),
        out_shape=block(INNER * (outer + PAD), LANES),
        compiler_params=pltpu.CompilerParams(vmem_limit_bytes=LIMIT * 2**20),
    )(z, forward_b, back_b)
    return pl.pallas_call(
        functools.partial(back_kernel, parts, outer),
        out_shape=block(parts, rows, LANES),
        in_specs=[scalar] + [whole] * 5,
        scratch_shapes=[pltpu.VMEM((outer * (INNER + PAD), LANES), F32)],
        compiler_params=pltpu.CompilerParams(vmem_limit_bytes=LIMIT * 2**20),
    )(index, skip_weight, w, p, back_a, turns)


def fast_on_device(query_stream, key_stream, value_stream, filter_taps, skip_weight):
    parts = lax.axis_size("ctx")
    device = lax.axis_index("ctx")
    length, channels = query_stream.shape[1:]
    rows = length // 2
    index = jnp.full((1,), device, jnp.int32)
    scalar = pl.BlockSpec(memory_space=pltpu.SMEM)
    whole = pl.BlockSpec(memory_space=pltpu.VMEM)
    far = pl.BlockSpec(memory_space=pltpu.HBM)
    small = pltpu.CompilerParams(vmem_limit_bytes=24 * 2**20)
    large = pltpu.CompilerParams(vmem_limit_bytes=60 * 2**20)

    def block(*shape, dtype=BF16):
        return jax.ShapeDtypeStruct(shape, dtype)

    size = 2 * rows + EXTRA
    sent = pl.pallas_call(
        functools.partial(pack_kernel, parts),
        out_shape=(block(size, LANES),) * parts,
        in_specs=[scalar] + [far] * 3,
        scratch_shapes=[pltpu.VMEM((parts, size, LANES), BF16)]
        + [pltpu.VMEM((length, channels), BF16)] * 3
        + [pltpu.SemaphoreType.DMA((3 * parts // 2,))],
        compiler_params=large,
    )(index, key_stream[0], value_stream[0], filter_taps[0])
    slabs = [sent[0]] + [joint_shift(sent[n], 0, n) for n in range(1, parts)]
    q = pl.pallas_call(
        functools.partial(pack_gate_kernel, parts),
        out_shape=block(parts, rows, LANES),
        compiler_params=large,
    )(query_stream[0])
    forward_a, forward_b, back_b, back_a, turns, two_turns = [
        jnp.asarray(t) for t in tables(parts * length // INNER)
    ]
    held = (sent[0], forward_a)
    held = pl.pallas_call(
        hold_kernel,
        out_shape=tuple(jax.ShapeDtypeStruct(x.shape, x.dtype) for x in held),
        compiler_params=small,
    )(*held)
    q, *_ = lax.optimization_barrier((q, *slabs, *held))
    slabs = [held[0]] + slabs[1:]
    consts = (two_turns, held[1], turns, forward_b, back_b, back_a)
    q = lax.all_to_all(q, "ctx", split_axis=0, concat_axis=0, tiled=True)
    y = convolved(parts, length, index, slabs, skip_weight, consts)
    gated = pl.pallas_call(
        functools.partial(gate_kernel, parts),
        out_shape=(block(rows, LANES),) * parts,
        in_specs=[scalar, whole, whole],
        compiler_params=small,
    )(index, y, q)
    gated = [joint_shift(gated[n], 1, -n) for n in longest_first(parts)]
    out = pl.pallas_call(
        functools.partial(unpack_kernel, parts),
        out_shape=block(length, channels),
        in_specs=[scalar] + [whole] * parts,
        scratch_shapes=[pltpu.VMEM((parts, rows, LANES), BF16)],
        compiler_params=small,
    )(index, *gated)
    return out[None]


def solution(mesh):
    placed = (
        P("segment", "ctx", None),
        P("segment", "ctx", None),
        P("segment", "ctx", None),
        P("segment", "ctx", None),
        P("segment", None),
    )

    def on_device(*arrays):
        parts = lax.axis_size("ctx")
        length, channels = arrays[0].shape[1:]
        square = parts * length == INNER * INNER
        run = fast_on_device if square and channels == parts * HALF else general_on_device
        return run(*arrays)

    return jax.shard_map(
        on_device, mesh=mesh, in_specs=placed, out_specs=P("segment", "ctx", None), check_vma=False
    )
```
